256 devices in a mesh: lon: 16 (over z, y_lo), lat: 4 (over y_hi, core), ch: 4 (over x).
Axes of the slice: x: 4, y: 4 (y_hi: 2, y_lo: 2; y = y_hi * 2 + y_lo), z: 8, core: 2. Of those that a mesh axis runs over, the one named last changes fastest.
Arguments:
- features: bfloat16 [96, 384, 2048], P('lat', 'lon', 'ch'), may hold values from -8 to 8
- depth_kernel: float32 [3, 9, 2048], P(None, None, 'ch'), may hold values from -2 to 2
- branch_weight: bfloat16 [5, 2048, 256], P(None, 'ch'), may hold values from -0.1875 to 0.1875
- proj_weight: bfloat16 [5, 256, 256], P(None, 'ch'), may hold values from -0.25 to 0.25
- cotangent: bfloat16 [96, 384, 256], P('lat', 'lon', 'ch'), may hold values from -6 to 6
Outputs:
- mixed: bfloat16 [96, 384, 256], P('lat', 'lon', 'ch')
- grad_features: bfloat16 [96, 384, 2048], P('lat', 'lon', 'ch')
- grad_branch: float32 [5, 2048, 256], P(None, 'ch')
- grad_proj: float32 [5, 256, 256], P(None, 'ch')
- grad_depth: float32 [3, 9, 2048], P(None, None, 'ch')
The draws below stay inside these ranges and needn't reach their ends.
All inputs are finite; a program needn't handle non-finite values.
Results may differ from the reference program's by a relative error of at most 0.01.
Values may be sent and summed in bfloat16 or wider, within the bound.
No kernel may reach another device: no remote copies, remote signals or barrier semaphores. Data moves between devices by JAX's collectives and lax.ppermute only.
A program may use at most 128 MiB of HBM per device.

```python
import math
import jax
import jax.numpy as jnp
from jax import lax

C = 2048
F = 256
NLAT = 96
NLON = 384


def draw_features(key, part):
    key = jax.random.fold_in(key, 7)
    noise_key, mean_key, phase_key = jax.random.split(key, 3)
    grid_shape = (NLAT, NLON, C)
    noise_part = jax.random.truncated_normal(noise_key, -4.0, 4.0, grid_shape, jnp.float32)
    chan_means = jax.random.uniform(mean_key, (C,), jnp.float32, -1.5, 1.5)
    phases = jax.random.uniform(phase_key, (C,), jnp.float32, -math.pi, math.pi)
    lat_pos = jnp.arange(NLAT, dtype=jnp.float32)[:, None, None] / NLAT
    lon_pos = jnp.arange(NLON, dtype=jnp.float32)[None, :, None] / NLON
    envelope = 0.4 + 1.2 * lat_pos
    lon_wave = 1.0 + 0.5 * jnp.cos(2.0 * math.pi * lon_pos + phases)
    return (noise_part + chan_means * envelope * lon_wave).astype(jnp.bfloat16)


def strengthened(drawn, own_key, source, target, parts, factor):
    def block_of(dim):
        return (jnp.arange(drawn.shape[dim]) // (drawn.shape[dim] // parts)).reshape((-1,) + (1,) * (drawn.ndim - 1 - dim))

    first = jax.random.permutation(own_key, parts)[block_of(target)]
    far = (block_of(target) + parts // 2) % parts
    return jnp.where((block_of(source) == first) | (block_of(source) == far), factor * drawn, drawn)


def steps_of(key, extent, shards, low, high):
    factor_of, own = 1.0, jax.random.fold_in(key, 6)
    for axis_at, shards_of in shards:
        draws = jnp.exp(jax.random.uniform(jax.random.fold_in(own, axis_at), (shards_of,), jnp.float32, low / len(shards), high / len(shards)))
        factor_of = factor_of * jnp.repeat(draws, extent[axis_at] // shards_of).reshape([-1 if axis == axis_at else 1 for axis in range(len(extent))])
    return factor_of


def centred(stream_key, extent, scale, most, cuts=(), kind=jnp.bfloat16):
    entries = jax.random.normal(stream_key, extent, jnp.float32) * scale
    if len(cuts) > 0:
        entries = steps_of(stream_key, extent, cuts, -0.22, 0.18) * entries
    return jnp.clip(entries, min=-most, max=most).astype(kind)


def noise_with(key, dims, width, bound, cuts, heavy, kind=jnp.bfloat16):
    values = width * jax.random.normal(key, dims, jnp.float32)
    if cuts:
        values = values * steps_of(key, dims, cuts, -0.22, 0.18)
    return jnp.clip(strengthened(values, jax.random.fold_in(key, 3), *heavy), -bound, bound).astype(kind)


def setup_inputs(seed: int = 0) -> dict:
    key_list = jax.random.split(jax.random.key(seed), 6)
    return {
        "features": draw_features(jax.random.fold_in(key_list[5], 71), 0),
        "depth_kernel": centred(key_list[1], (3, 9, C), 0.35, 2.0, ((2, 4),), jnp.float32),
        "branch_weight": noise_with(key_list[2], (5, C, F), C ** -0.5, 0.1875, ((1, 4),), (1, 2, 4, 2.0)),
        "proj_weight": noise_with(key_list[3], (5, F, F), (5 * F) ** -0.5, 0.25, ((1, 4),), (1, 2, 4, 2.0)),
        "cotangent": centred(key_list[4], (NLAT, NLON, F), 1.0, 6.0, ((0, 4), (1, 16), (2, 4))),
    }


dilations = (6, 12, 18)
margin = 18
highest = lax.Precision.HIGHEST

def activate(value):
    return value * jax.nn.sigmoid(value)

def activate_slope(value):
    sig = jax.nn.sigmoid(value)
    return sig * (1.0 + value * (1.0 - sig))

def widen(block):
    padded = jnp.pad(block, ((margin, margin), (0, 0), (0, 0)))
    return jnp.concatenate([padded[:, -margin:], padded, padded[:, :margin]], axis=1)

def depthwise(extended, kernel_row, spacing, sign):
    summed = jnp.zeros((NLAT, NLON, extended.shape[2]), jnp.float32)
    for step_lat in (-1, 0, 1):
        for step_lon in (-1, 0, 1):
            tap_index = 3 * (step_lat + 1) + step_lon + 1
            top = margin + sign * step_lat * spacing
            left = margin + sign * step_lon * spacing
            summed = summed + kernel_row[tap_index] * extended[top:top + NLAT, left:left + NLON].astype(jnp.float32)
    return summed

def tap_sums(grad_piece, extended, spacing):
    results = []
    for step_lat in (-1, 0, 1):
        for step_lon in (-1, 0, 1):
            top = margin + step_lat * spacing
            left = margin + step_lon * spacing
            window = extended[top:top + NLAT, left:left + NLON].astype(jnp.float32)
            results.append(lax.optimization_barrier(jnp.sum(grad_piece.astype(jnp.float32) * window, axis=(0, 1))))
    return jnp.stack(results)

def reference(features, depth_kernel, branch_weight, proj_weight, cotangent):
    cell_count = NLAT * NLON
    block_width = min(256, C)
    block_count = C // block_width
    feat_blocks = features.reshape(NLAT, NLON, block_count, block_width).transpose(2, 0, 1, 3)
    kern_blocks = depth_kernel.reshape(3, 9, block_count, block_width).transpose(2, 0, 1, 3)
    weight_blocks = branch_weight[:4].reshape(4, block_count, block_width, F).transpose(1, 0, 2, 3)

    def branch_inputs(feat_block, kern_block):
        extended = widen(feat_block)
        inputs = [feat_block]
        for position, spacing in enumerate(dilations):
            inputs.append(depthwise(extended, kern_block[position], spacing, 1).astype(jnp.bfloat16))
        return (extended, inputs)

    def forward_step(carry, pieces):
        feat_block, kern_block, weight_block = pieces
        extended, inputs = branch_inputs(feat_block, kern_block)
        terms = jnp.stack([jnp.dot(inputs[member].reshape(cell_count, block_width), weight_block[member], preferred_element_type=jnp.float32) for member in range(4)])
        colsum = lax.optimization_barrier(jnp.sum(feat_block.astype(jnp.float32), axis=(0, 1)))
        return (carry + terms, colsum)
    pre, colsums = lax.scan(forward_step, jnp.zeros((4, cell_count, F), jnp.float32), (feat_blocks, kern_blocks, weight_blocks))
    pooled = colsums.reshape(C) / cell_count
    pool_pre = jnp.dot(pooled, branch_weight[4].astype(jnp.float32), precision=highest)
    branches = activate(pre).astype(jnp.bfloat16)
    pool_branch = activate(pool_pre).astype(jnp.bfloat16)
    proj_pre = jnp.dot(pool_branch, proj_weight[4], preferred_element_type=jnp.float32)[None, :]
    for member in range(4):
        proj_pre = proj_pre + jnp.dot(branches[member], proj_weight[member], preferred_element_type=jnp.float32)
    mixed = activate(proj_pre).astype(jnp.bfloat16).reshape(NLAT, NLON, F)
    back_proj = (cotangent.reshape(cell_count, F).astype(jnp.float32) * activate_slope(proj_pre)).astype(jnp.bfloat16)
    back_sum = lax.optimization_barrier(jnp.sum(back_proj.astype(jnp.float32), axis=0))
    grad_proj = jnp.stack([jnp.dot(branches[member].T, back_proj, preferred_element_type=jnp.float32) for member in range(4)] + [pool_branch.astype(jnp.float32)[:, None] * back_sum[None, :]])
    dpre = jnp.stack([jnp.dot(back_proj, proj_weight[member].T, preferred_element_type=jnp.float32) * activate_slope(pre[member]) for member in range(4)]).astype(jnp.bfloat16)
    pool_sum = jnp.dot(proj_weight[4].astype(jnp.float32), back_sum, precision=highest)
    dpool = pool_sum * activate_slope(pool_pre)
    dpooled = jnp.dot(branch_weight[4].astype(jnp.float32), dpool, precision=highest) / cell_count
    dpooled_blocks = dpooled.reshape(block_count, block_width)

    def backward_step(pieces):
        feat_block, kern_block, weight_block, pooled_block = pieces
        extended, inputs = branch_inputs(feat_block, kern_block)
        dinputs = [jnp.dot(dpre[member], weight_block[member].T, preferred_element_type=jnp.float32) for member in range(4)]
        branch_grads = jnp.stack([jnp.dot(inputs[member].reshape(cell_count, block_width).T, dpre[member], preferred_element_type=jnp.float32) for member in range(4)])
        grad_block = dinputs[0].reshape(NLAT, NLON, block_width) + pooled_block
        depth_grads = []
        for position, spacing in enumerate(dilations):
            grad_piece = dinputs[position + 1].astype(jnp.bfloat16).reshape(NLAT, NLON, block_width)
            grad_block = grad_block + depthwise(widen(grad_piece), kern_block[position], spacing, -1)
            depth_grads.append(tap_sums(grad_piece, extended, spacing))
        return (grad_block.astype(jnp.bfloat16), branch_grads, jnp.stack(depth_grads))
    grad_blocks, branch_blocks, depth_blocks = lax.map(backward_step, (feat_blocks, kern_blocks, weight_blocks, dpooled_blocks))
    grad_scale = 1.0 / math.sqrt(cell_count)
    grad_features = grad_blocks.transpose(1, 2, 0, 3).reshape(NLAT, NLON, C)
    grad_branch = jnp.concatenate([branch_blocks.transpose(1, 0, 2, 3).reshape(4, C, F), (pooled[:, None] * dpool[None, :])[None]], axis=0) * grad_scale
    grad_depth = depth_blocks.transpose(1, 2, 0, 3).reshape(3, 9, C) * grad_scale
    return (mixed, grad_features, grad_branch, grad_proj * grad_scale, grad_depth)
```

```python
import math

import jax
import jax.numpy as jnp
from jax import lax
from jax.experimental import pallas as pl
from jax.experimental.pallas import tpu as pltpu
from jax.sharding import PartitionSpec as P

dilations = (6, 12, 18)
margin = 18
lead = 24
f32, bf16 = jnp.float32, jnp.bfloat16
GRID = ("lon", "lat")


def params():
    return pltpu.CompilerParams(vmem_limit_bytes=48 * 1024 * 1024)


def window_of(spacing, step_lon):
    base = lead + step_lon * spacing
    return base // 8, base % 8


def fill_extended(ext, tile_ref, left_ref, right_ref, top_ref, bottom_ref):
    rows, cols, _ = tile_ref.shape
    wide = cols + 2 * margin
    off = lead - margin

    def tile_row(row, carry):
        ext[margin + row, lead : lead + cols, :] = tile_ref[row].astype(f32)
        ext[margin + row, off:lead, :] = left_ref[row].astype(f32)
        ext[margin + row, lead + cols : off + wide, :] = right_ref[row].astype(f32)
        return carry

    def strip_row(row, carry):
        ext[row, off : off + wide, :] = top_ref[row].astype(f32)
        ext[margin + rows + row, off : off + wide, :] = bottom_ref[row].astype(f32)
        return carry

    lax.fori_loop(0, rows, tile_row, 0)
    lax.fori_loop(0, margin, strip_row, 0)


def fill_taps(taps, kernel_ref):
    for member in range(3):
        for tap in range(9):
            taps[9 * member + tap] = jnp.broadcast_to(
                kernel_ref[member, tap : tap + 1, :], taps.shape[1:]
            )


def conv_body(
    me_ref, tile_ref, left_ref, right_ref, top_ref, bottom_ref, kernel_ref, weight_ref,
    inputs_ref, own_ref, one_ref, two_ref, three_ref, ext, cells, taps, total,
):
    step = pl.program_id(0)
    rows, cols, lanes = tile_ref.shape
    fan = weight_ref.shape[2]

    @pl.when(step == 0)
    def _():
        total[...] = jnp.zeros_like(total)
        ext[...] = jnp.zeros_like(ext)

    fill_extended(ext, tile_ref, left_ref, right_ref, top_ref, bottom_ref)
    fill_taps(taps, kernel_ref)

    def conv_row(row, carry):
        place = pl.ds(pl.multiple_of(row * cols, 8), cols)
        cells[0, place, :] = tile_ref[row].astype(f32)
        for member, spacing in enumerate(dilations):
            summed = None
            for step_lon in (-1, 0, 1):
                group, shift = window_of(spacing, step_lon)
                count = cols // 8 + (shift != 0)
                part = None
                for step_lat in (-1, 0, 1):
                    window = ext[
                        row + margin + step_lat * spacing, 8 * group : 8 * (group + count), :
                    ].reshape(count, 8, lanes)
                    term = window * taps[9 * member + 3 * (step_lat + 1) + step_lon + 1]
                    part = term if part is None else part + term
                part = part.reshape(8 * count, lanes)
                if shift:
                    part = pltpu.roll(part, 8 * count - shift, 0)[:cols]
                summed = part if summed is None else summed + part
            cells[member + 1, place, :] = summed
        return carry

    lax.fori_loop(0, rows, conv_row, 0)
    for member in range(4):
        block = cells[member].astype(bf16)
        inputs_ref[member] = block
        total[:, fan * member : fan * (member + 1)] += jnp.dot(
            block, weight_ref[member], preferred_element_type=f32
        )

    @pl.when(step == pl.num_programs(0) - 1)
    def _():
        size = own_ref.shape[0]
        me = me_ref[0]

        def chunk(ahead):
            return total[pl.ds(pl.multiple_of(lax.rem(me + ahead, 4) * size, 16), size), :]

        own_ref[...] = chunk(0)
        one_ref[...] = chunk(1).astype(bf16)
        two_ref[...] = chunk(2).astype(bf16)
        three_ref[...] = chunk(3).astype(bf16)


def conv_forward(me, tile, halos, kernel, weight):
    rows, cols, chan = tile.shape
    fan = weight.shape[2]
    wide = cols + 2 * margin
    lanes = 128
    size = rows * cols // 4
    cells = rows * cols
    whole = lambda *shape: pl.BlockSpec(shape, lambda i: (0,) * len(shape))
    last = lambda *shape: pl.BlockSpec(
        shape + (lanes,), lambda i: (0,) * len(shape) + (i,)
    )
    return pl.pallas_call(
        conv_body,
        grid=(chan // lanes,),
        in_specs=[
            pl.BlockSpec(memory_space=pltpu.SMEM),
            last(rows, cols),
            last(rows, margin),
            last(rows, margin),
            last(margin, wide),
            last(margin, wide),
            last(3, 9),
            pl.BlockSpec((4, lanes, fan), lambda i: (0, i, 0)),
        ],
        out_specs=[last(4, cells)] + [whole(size, 4 * fan)] * 4,
        out_shape=[
            jax.ShapeDtypeStruct((4, cells, chan), bf16),
            jax.ShapeDtypeStruct((size, 4 * fan), f32),
        ]
        + [jax.ShapeDtypeStruct((size, 4 * fan), bf16)] * 3,
        scratch_shapes=[
            pltpu.VMEM((rows + 2 * margin, cols + 2 * lead, lanes), f32),
            pltpu.VMEM((4, cells, lanes), f32),
            pltpu.VMEM((27, 8, lanes), f32),
            pltpu.VMEM((cells, 4 * fan), f32),
        ],
        compiler_params=params(),
        cost_estimate=pl.CostEstimate(
            flops=2 * cells * chan * (4 * fan + 27), bytes_accessed=20_000_000, transcendentals=0
        ),
        name="conv_forward",
    )(me, tile, *halos, kernel, weight)


def slope(value, sig):
    return sig * (1.0 + value * (1.0 - sig))


def proj_body(
    me_ref, own_ref, one_ref, two_ref, three_ref, cot_ref, weight_ref, pool_ref,
    mixed_ref, dpre_ref, grad_own_ref, grad_one_ref, grad_two_ref, grad_three_ref, sum_ref,
    pre, grads,
):
    fan = weight_ref.shape[1]
    size = own_ref.shape[0]
    me = me_ref[0]
    pre[...] = (
        own_ref[...] + one_ref[...].astype(f32) + two_ref[...].astype(f32) + three_ref[...].astype(f32)
    )
    pool = jnp.broadcast_to(pool_ref[...], (8, fan))
    pool_branch = (pool * jax.nn.sigmoid(pool)).astype(bf16)
    proj = jnp.dot(pool_branch, weight_ref[4], preferred_element_type=f32)[0:1, :]
    for member in range(4):
        value = pre[:, fan * member : fan * (member + 1)]
        branch = (value * jax.nn.sigmoid(value)).astype(bf16)
        proj = proj + jnp.dot(branch, weight_ref[member], preferred_element_type=f32)
    sig = jax.nn.sigmoid(proj)
    mixed = (proj * sig).astype(bf16)
    part = fan // 4
    for target in range(4):
        mixed_ref[target] = mixed[:, part * target : part * (target + 1)]
    back = (cot_ref[...].astype(f32) * slope(proj, sig)).astype(bf16)
    sum_ref[...] = jnp.sum(back.astype(f32), axis=0, keepdims=True)
    for member in range(4):
        value = pre[:, fan * member : fan * (member + 1)]
        sig = jax.nn.sigmoid(value)
        branch = (value * sig).astype(bf16)
        grads[member] = lax.dot_general(
            branch, back, (((0,), (0,)), ((), ())), preferred_element_type=f32
        )
        dbranch = lax.dot_general(
            back, weight_ref[member], (((1,), (1,)), ((), ())), preferred_element_type=f32
        )
        dpre_ref[:, fan * member : fan * (member + 1)] = (dbranch * slope(value, sig)).astype(bf16)
        for ahead, ref in enumerate((grad_own_ref, grad_one_ref, grad_two_ref, grad_three_ref)):
            first = pl.multiple_of(lax.rem(me + ahead, 4) * part, 16)
            ref[member] = grads[member, pl.ds(first, part), :].astype(ref.dtype)


def project(me, own, others, cot, weight, pool_pre):
    size, wide = own.shape
    fan = wide // 4
    part = fan // 4
    vmem = pl.BlockSpec(memory_space=pltpu.VMEM)
    return pl.pallas_call(
        proj_body,
        in_specs=[pl.BlockSpec(memory_space=pltpu.SMEM)] + [vmem] * 7,
        out_specs=[vmem] * 7,
        out_shape=[
            jax.ShapeDtypeStruct((4, size, part), bf16),
            jax.ShapeDtypeStruct((size, wide), bf16),
            jax.ShapeDtypeStruct((4, part, fan), f32),
        ]
        + [jax.ShapeDtypeStruct((4, part, fan), bf16)] * 3
        + [jax.ShapeDtypeStruct((1, fan), f32)],
        scratch_shapes=[pltpu.VMEM((size, wide), f32), pltpu.VMEM((4, fan, fan), f32)],
        compiler_params=params(),
        cost_estimate=pl.CostEstimate(
            flops=6 * size * wide * fan, bytes_accessed=4_000_000, transcendentals=2 * size * wide
        ),
        name="project",
    )(me, own, *others, cot, weight, pool_pre)


def weight_body(me_ref, own_ref, one_ref, two_ref, three_ref, inputs_ref, grad_ref, full_ref):
    fan = grad_ref.shape[2]
    size = own_ref.shape[0]
    me = me_ref[0]

    @pl.when(pl.program_id(0) == 0)
    def _():
        for behind, ref in enumerate((own_ref, one_ref, two_ref, three_ref)):
            first = pl.multiple_of(lax.rem(me + 4 - behind, 4) * size, 16)
            full_ref[pl.ds(first, size), :] = ref[...]

    for member in range(4):
        grad_ref[member] = lax.dot_general(
            inputs_ref[member],
            full_ref[:, fan * member : fan * (member + 1)],
            (((0,), (0,)), ((), ())),
            preferred_element_type=f32,
        )


def weight_grads(me, own, others, inputs):
    size, wide = own.shape
    fan = wide // 4
    _, cells, chan = inputs.shape
    lanes = 128
    piece = pl.BlockSpec((size, wide), lambda i: (0, 0))
    return pl.pallas_call(
        weight_body,
        grid=(chan // lanes,),
        in_specs=[pl.BlockSpec(memory_space=pltpu.SMEM)]
        + [piece] * 4
        + [pl.BlockSpec((4, cells, lanes), lambda i: (0, 0, i))],
        out_specs=[
            pl.BlockSpec((4, lanes, fan), lambda i: (0, i, 0)),
            pl.BlockSpec((cells, wide), lambda i: (0, 0)),
        ],
        out_shape=[
            jax.ShapeDtypeStruct((4, chan, fan), f32),
            jax.ShapeDtypeStruct((cells, wide), bf16),
        ],
        compiler_params=params(),
        cost_estimate=pl.CostEstimate(
            flops=2 * cells * chan * wide, bytes_accessed=6_000_000, transcendentals=0
        ),
        name="weight_grads",
    )(me, own, *others, inputs)


placed = {}
for _member in range(3):
    for _step in (-1, 0, 1):
        _key = (_member, window_of(dilations[_member], _step)[1])
        placed.setdefault(_key, len(placed))


def scatter_body(
    dpre_ref, weight_ref, tile_ref, left_ref, right_ref, top_ref, bottom_ref, kernel_ref,
    mid_ref, up_ref, down_ref, tap_ref, ext, taps, first, grads, shifted,
):
    rows, cols, lanes = tile_ref.shape
    fan = weight_ref.shape[2]
    wide = cols + 2 * margin
    groups = (cols + 2 * lead) // 8

    @pl.when(pl.program_id(0) == 0)
    def _():
        ext[...] = jnp.zeros_like(ext)

    fill_extended(ext, tile_ref, left_ref, right_ref, top_ref, bottom_ref)
    fill_taps(taps, kernel_ref)
    for member in range(4):
        piece = lax.dot_general(
            dpre_ref[:, fan * member : fan * (member + 1)],
            weight_ref[member],
            (((1,), (1,)), ((), ())),
            preferred_element_type=f32,
        )
        if member == 0:
            first[...] = piece
        else:
            grads[member - 1] = piece.astype(bf16).astype(f32)

    def shift_row(row, carry):
        place = pl.ds(pl.multiple_of(row * cols, 8), cols)
        for (member, shift), number in placed.items():
            value = grads[member, place, :]
            if shift:
                value = jnp.concatenate([value, jnp.zeros((8, lanes), f32)], axis=0)
                shifted[number, row] = pltpu.roll(value, shift, 0)
            else:
                shifted[number, row, :cols, :] = value
        return carry

    lax.fori_loop(0, rows, shift_row, 0)

    def tap_row(row, carry):
        sums = list(carry)
        for member, spacing in enumerate(dilations):
            for step_lon in (-1, 0, 1):
                group, shift = window_of(spacing, step_lon)
                count = cols // 8 + (shift != 0)
                grad = shifted[placed[member, shift], row, : 8 * count, :].reshape(count, 8, lanes)
                for step_lat in (-1, 0, 1):
                    window = ext[
                        row + margin + step_lat * spacing, 8 * group : 8 * (group + count), :
                    ].reshape(count, 8, lanes)
                    tap = 9 * member + 3 * (step_lat + 1) + step_lon + 1
                    sums[tap] = sums[tap] + jnp.sum(grad * window, axis=0)
        return tuple(sums)

    sums = lax.fori_loop(0, rows, tap_row, (jnp.zeros((8, lanes), f32),) * 27)
    for member in range(3):
        for tap in range(9):
            tap_ref[member, tap : tap + 1, :] = jnp.sum(
                sums[9 * member + tap], axis=0, keepdims=True
            )

    for begin in range(0, rows + 2 * margin, 6):
        active = [
            (member, step_lat)
            for member, spacing in enumerate(dilations)
            for step_lat in (-1, 0, 1)
            if margin + step_lat * spacing <= begin < margin + rows + step_lat * spacing
        ]

        def ext_row(step, carry, begin=begin, active=active):
            at = begin + step
            sums = [jnp.zeros((8, lanes), f32)] * groups
            inside = margin <= begin < margin + rows
            if inside:
                value = first[pl.ds(pl.multiple_of((at - margin) * cols, 8), cols), :]
                for number in range(cols // 8):
                    sums[lead // 8 + number] = value[8 * number : 8 * (number + 1)]
            for member, step_lat in active:
                spacing = dilations[member]
                for step_lon in (-1, 0, 1):
                    group, shift = window_of(spacing, step_lon)
                    count = cols // 8 + (shift != 0)
                    grad = shifted[
                        placed[member, shift], at - margin - step_lat * spacing, : 8 * count, :
                    ]
                    weight = taps[9 * member + 3 * (step_lat + 1) + step_lon + 1]
                    for number in range(count):
                        sums[group + number] = (
                            sums[group + number] + grad[8 * number : 8 * (number + 1)] * weight
                        )
            line = jnp.concatenate(sums, axis=0)
            line = pltpu.roll(line, 8 * groups - (lead - margin), 0)[:wide]
            if inside:
                mid_ref[at - margin] = line
            elif begin < margin:
                up_ref[at] = line.astype(bf16)
            else:
                down_ref[at - margin - rows] = line.astype(bf16)
            return carry

        lax.fori_loop(0, 6, ext_row, 0)


def scatter_grads(dpre, weight, tile, halos, kernel):
    rows, cols, chan = tile.shape
    cells, wide_fan = dpre.shape
    fan = wide_fan // 4
    wide = cols + 2 * margin
    lanes = 128
    last = lambda *shape: pl.BlockSpec(shape + (lanes,), lambda i: (0,) * len(shape) + (i,))
    return pl.pallas_call(
        scatter_body,
        grid=(chan // lanes,),
        in_specs=[
            pl.BlockSpec((cells, wide_fan), lambda i: (0, 0)),
            pl.BlockSpec((4, lanes, fan), lambda i: (0, i, 0)),
            last(rows, cols),
            last(rows, margin),
            last(rows, margin),
            last(margin, wide),
            last(margin, wide),
            last(3, 9),
        ],
        out_specs=[last(rows, wide), last(margin, wide), last(margin, wide), last(3, 9)],
        out_shape=[
            jax.ShapeDtypeStruct((rows, wide, chan), f32),
            jax.ShapeDtypeStruct((margin, wide, chan), bf16),
            jax.ShapeDtypeStruct((margin, wide, chan), bf16),
            jax.ShapeDtypeStruct((3, 9, chan), f32),
        ],
        scratch_shapes=[
            pltpu.VMEM((rows + 2 * margin, cols + 2 * lead, lanes), f32),
            pltpu.VMEM((27, 8, lanes), f32),
            pltpu.VMEM((cells, lanes), f32),
            pltpu.VMEM((3, cells, lanes), f32),
            pltpu.VMEM((len(placed), rows, cols + 8, lanes), f32),
        ],
        compiler_params=params(),
        cost_estimate=pl.CostEstimate(
            flops=2 * cells * chan * (wide_fan + 54), bytes_accessed=20_000_000, transcendentals=0
        ),
        name="scatter_grads",
    )(dpre, weight, tile, *halos, kernel)


def shift(value, axis, ahead, closed=True):
    count = lax.axis_size(axis)
    pairs = [
        (i, (i + ahead) % count) for i in range(count) if closed or 0 <= i + ahead < count
    ]
    return lax.ppermute(value, axis, pairs)


def place_in_grid():
    return lax.axis_index("lon") * lax.axis_size("lat") + lax.axis_index("lat")


def swap(value, mask):
    count = lax.axis_size("lon") * lax.axis_size("lat")
    return lax.ppermute(value, GRID, [(i, i ^ mask) for i in range(count)])


def has(mask):
    return (place_in_grid() & mask) != 0


def number_in(bits):
    return sum(has(bit).astype(jnp.int32) << at for at, bit in enumerate(bits))


def mask_of(bits, code):
    return sum(bit for at, bit in enumerate(bits) if (code >> at) & 1)


def grid_sum(value):
    mask = 1
    while mask < lax.axis_size("lon") * lax.axis_size("lat"):
        value = value + swap(value, mask)
        mask *= 2
    return value


def by_channel(pieces):
    me = lax.axis_index("ch")
    stacked = jnp.stack(pieces)
    return [lax.dynamic_index_in_dim(stacked, (me - p) % 4, 0, False) for p in range(4)]


core_bit, y_bits = 1, (4, 2)


def z_bits():
    bits, mask = [], 8
    while mask < lax.axis_size("lon") * lax.axis_size("lat"):
        bits.append(mask)
        mask *= 2
    return bits


def reduce_all(big, extra_of):
    half = big.shape[0] // 2
    upper = has(core_bit)
    give = jnp.where(upper, big[:half], big[half:]).astype(bf16)
    big = jnp.where(upper, big[half:], big[:half]) + swap(give, core_bit).astype(f32)

    size = half // 4
    here = number_in(y_bits)
    taken = [
        swap(
            lax.dynamic_slice_in_dim(big, (here ^ code) * size, size).astype(bf16),
            mask_of(y_bits, code),
        )
        for code in (1, 2, 3)
    ]
    big = lax.dynamic_slice_in_dim(big, here * size, size) + sum(t.astype(f32) for t in taken)

    extra = extra_of
    for mask in z_bits():
        half = big.shape[0] // 2
        upper = has(mask)
        give = jnp.where(upper, big[:half], big[half:])
        got = swap(jnp.concatenate([give, extra]).astype(bf16), mask).astype(f32)
        big = jnp.where(upper, big[half:], big[:half]) + got[:half]
        extra = extra + got[half:]

    big = big.astype(bf16)
    for mask in z_bits()[::-1]:
        got = swap(big, mask)
        big = jnp.where(has(mask), jnp.concatenate([got, big]), jnp.concatenate([big, got]))

    size = big.shape[0]
    sent = jnp.concatenate([big, extra.astype(bf16)])
    taken = [swap(sent, mask_of(y_bits, code)) for code in (1, 2, 3)]
    extra = extra + sum(t[size:].astype(f32) for t in taken)
    stacked = jnp.stack([big] + [t[:size] for t in taken])
    big = jnp.concatenate(
        [lax.dynamic_index_in_dim(stacked, here ^ code, 0, False) for code in range(4)]
    )

    size = big.shape[0]
    got = swap(jnp.concatenate([big, extra.astype(bf16)]), core_bit)
    extra = extra + got[size:].astype(f32)
    upper = has(core_bit)
    big = jnp.concatenate(
        [jnp.where(upper, got[:size], big), jnp.where(upper, big, got[:size])]
    )
    return big.astype(f32), extra


def activate_slope(value):
    return slope(value, jax.nn.sigmoid(value))


def per_device(features, depth_kernel, branch_weight, proj_weight, cotangent):
    rows, cols, chan = features.shape
    fan = branch_weight.shape[2]
    part = proj_weight.shape[1]
    cell_count = rows * cols * lax.axis_size("lat") * lax.axis_size("lon")
    grad_scale = 1.0 / math.sqrt(cell_count)
    me = lax.axis_index("ch")
    me_arg = me.astype(jnp.int32).reshape(1)
    band = rows // 4

    left = shift(features[:, cols - margin :], "lon", 1)
    right = shift(features[:, :margin], "lon", -1)
    strip = jnp.concatenate([left, features, right], axis=1)
    top = shift(strip[rows - margin :], "lat", 1, False)
    bottom = shift(strip[:margin], "lat", -1, False)
    halos = (left, right, top, bottom)

    pool_weight = branch_weight[4].astype(f32)
    colsum = jnp.sum(features, axis=(0, 1), dtype=f32)
    pooled = grid_sum(colsum.reshape(4, chan // 4)).reshape(chan) / cell_count
    pool_pre = jnp.sum(pool_weight * pooled[:, None], axis=0).reshape(2, fan // 2)
    for mask in (1, 2):
        pool_pre = pool_pre + lax.ppermute(pool_pre, "ch", [(i, i ^ mask) for i in range(4)])
    pool_pre = pool_pre.reshape(1, fan)

    proj_full = jnp.concatenate(
        by_channel([proj_weight] + [shift(proj_weight, "ch", d) for d in (1, 2, 3)]), axis=1
    )
    bands = cotangent.reshape(4, band * cols, part)
    cot = jnp.concatenate(
        by_channel(
            [
                shift(lax.dynamic_index_in_dim(bands, (me + d) % 4, 0, False), "ch", d)
                if d
                else lax.dynamic_index_in_dim(bands, me, 0, False)
                for d in range(4)
            ]
        ),
        axis=1,
    )

    inputs, own, *ahead = conv_forward(
        me_arg, features, halos, depth_kernel, branch_weight
    )
    others = [shift(value, "ch", d + 1) for d, value in enumerate(ahead)]
    mixed_parts, dpre, gp_own, *gp_ahead, back_part = project(
        me_arg, own, others, cot, proj_full, pool_pre
    )
    dpre_others = [shift(dpre, "ch", d) for d in (1, 2, 3)]
    gp = gp_own + sum(shift(v, "ch", d + 1).astype(f32) for d, v in enumerate(gp_ahead))

    branch_part, dpre_full = weight_grads(me_arg, dpre, dpre_others, inputs)
    mid, up, down, tap_part = scatter_grads(
        dpre_full, branch_weight, features, halos, depth_kernel
    )

    from_above = shift(down, "lat", 1, False).astype(f32)
    from_below = shift(up, "lat", -1, False).astype(f32)
    mid = (
        mid
        + jnp.pad(from_above, ((0, rows - margin), (0, 0), (0, 0)))
        + jnp.pad(from_below, ((rows - margin, 0), (0, 0), (0, 0)))
    )
    from_left = shift(mid[:, margin + cols :].astype(bf16), "lon", 1).astype(f32)
    from_right = shift(mid[:, :margin].astype(bf16), "lon", -1).astype(f32)

    for mask in (1, 2):
        back_part = back_part + lax.ppermute(back_part, "ch", [(i, i ^ mask) for i in range(4)])

    tap_rows = tap_part.reshape(27 * chan // fan, fan)
    extra = jnp.concatenate([tap_rows, back_part])
    extra = jnp.pad(extra, ((0, -extra.shape[0] % 16), (0, 0)))
    big = jnp.concatenate([branch_part.reshape(4 * chan, fan), gp.reshape(4 * part, fan)])
    big, extra = reduce_all(big, extra)
    count = tap_rows.shape[0]
    back_sum = extra[count]
    grad_depth = extra[:count].reshape(3, 9, chan) * grad_scale

    dpool = jnp.sum(proj_full[4].astype(f32) * back_sum[None, :], axis=1)
    dpool = dpool * activate_slope(pool_pre[0])
    dpooled = jnp.sum(pool_weight * dpool[None, :], axis=1) / cell_count
    grad_features = (
        mid[:, margin : margin + cols]
        + jnp.pad(from_left, ((0, 0), (0, cols - margin), (0, 0)))
        + jnp.pad(from_right, ((0, 0), (cols - margin, 0), (0, 0)))
        + dpooled[None, None, :]
    ).astype(bf16)

    mixed = jnp.concatenate(
        by_channel(
            [
                shift(lax.dynamic_index_in_dim(mixed_parts, (me + d) % 4, 0, False), "ch", d)
                if d
                else lax.dynamic_index_in_dim(mixed_parts, me, 0, False)
                for d in range(4)
            ]
        ),
        axis=0,
    ).reshape(rows, cols, part)

    grad_branch = jnp.concatenate(
        [
            big[: 4 * chan].reshape(4, chan, fan),
            (pooled[:, None] * dpool[None, :])[None],
        ]
    ) * grad_scale
    pool_branch = pool_pre[0] * jax.nn.sigmoid(pool_pre[0])
    pool_own = lax.dynamic_slice_in_dim(pool_branch.astype(bf16).astype(f32), me * part, part)
    grad_proj = jnp.concatenate(
        [big[4 * chan :].reshape(4, part, fan), (pool_own[:, None] * back_sum[None, :])[None]]
    ) * grad_scale
    return (mixed, grad_features, grad_branch, grad_proj, grad_depth)


def solution(mesh):
    return jax.shard_map(
        per_device,
        mesh=mesh,
        in_specs=(
            P("lat", "lon", "ch"),
            P(None, None, "ch"),
            P(None, "ch", None),
            P(None, "ch", None),
            P("lat", "lon", "ch"),
        ),
        out_specs=(
            P("lat", "lon", "ch"),
            P("lat", "lon", "ch"),
            P(None, "ch", None),
            P(None, "ch", None),
            P(None, None, "ch"),
        ),
        check_vma=False,
    )
```

```python
import math

import jax
import jax.numpy as jnp
from jax import lax
from jax.experimental import pallas as pl
from jax.experimental.pallas import tpu as pltpu
from jax.sharding import PartitionSpec as P

dilations = (6, 12, 18)
margin = 18
lead = 24
f32, bf16 = jnp.float32, jnp.bfloat16
GRID = ("lon", "lat")


MIB = 1024 * 1024


def params(size):
    return pltpu.CompilerParams(vmem_limit_bytes=size * MIB)


def smem():
    return pl.BlockSpec(memory_space=pltpu.SMEM)


def vmem():
    return pl.BlockSpec(memory_space=pltpu.VMEM)


def anywhere():
    return pl.BlockSpec(memory_space=pl.ANY)


def stay(value):
    return pltpu.with_memory_space_constraint(value, pltpu.HBM)


def remote():
    return pl.BlockSpec(memory_space=pltpu.HBM)


def by_lanes(*shape, lanes=128):
    return pl.BlockSpec(shape + (lanes,), lambda i: (0,) * len(shape) + (i,))


def whole(*shape):
    return pl.BlockSpec(shape, lambda i: (0,) * len(shape))


def shaped(dtype, *shape):
    return jax.ShapeDtypeStruct(shape, dtype)


def far(dtype, *shape):
    return pltpu.HBM(shape, dtype)


def cost(flops, moved, hard=0):
    return pl.CostEstimate(flops=flops, bytes_accessed=moved, transcendentals=hard)


def window_of(spacing, step_lon):
    base = lead + step_lon * spacing
    return base // 8, base % 8


def roll_rows(value, shift, count):
    if shift:
        value = pltpu.roll(value, value.shape[0] - shift, 0)
    return value[:count]


def pick(value, scalar):
    return pl.multiple_of(value, scalar)


def split_lanes(line):
    return [line[:, 128 * n : 128 * (n + 1)] for n in range(line.shape[1] // 128)]


def edges_body(tile_ref, right_ref, left_ref, sum_ref, packed):
    rows, cols, chan = tile_ref.shape

    def row_step(row, carry):
        line = tile_ref[row].astype(f32)
        for number, block in enumerate(split_lanes(line)):
            place = slice(margin * number, margin * (number + 1))
            packed[0, row, place, :] = block[:margin]
            packed[1, row, place, :] = roll_rows(block, cols - margin, margin)
        return carry + line

    total = lax.fori_loop(0, rows, row_step, jnp.zeros((cols, chan), f32))
    left_ref[...] = packed[0].astype(bf16)
    right_ref[...] = packed[1].astype(bf16)

    @pl.when(pl.program_id(0) == 0)
    def _():
        sum_ref[...] = jnp.zeros_like(sum_ref)

    sum_ref[...] += jnp.sum(total, axis=0, keepdims=True)


def edges(tile):
    rows, cols, chan = tile.shape
    wide = margin * chan // 128
    block = rows // 3
    by_rows = lambda *shape: pl.BlockSpec((block,) + shape, lambda i: (i, 0, 0))
    return pl.pallas_call(
        edges_body,
        grid=(3,),
        in_specs=[by_rows(cols, chan)],
        out_specs=[by_rows(wide, 128), by_rows(wide, 128), whole(1, chan)],
        out_shape=[
            shaped(bf16, rows, wide, 128),
            shaped(bf16, rows, wide, 128),
            shaped(f32, 1, chan),
        ],
        scratch_shapes=[pltpu.VMEM((2, block, wide, 128), f32)],
        compiler_params=params(8),
        cost_estimate=cost(rows * cols * chan, 2_000_000),
        name="edges",
    )(stay(tile))


def corners_body(left_ref, right_ref, sum_ref, *refs):
    up_ref, down_ref, out_ref = refs[-3:]
    rows = left_ref.shape[0]
    for number, ref in enumerate((left_ref, right_ref)):
        place = slice(margin * number, margin * (number + 1))
        up_ref[place] = ref[rows - margin :]
        down_ref[place] = ref[:margin]
    out_ref[...] = sum_ref[...]


def corners(left, right, running, before):
    _, wide, lanes = left.shape
    return pl.pallas_call(
        corners_body,
        in_specs=[vmem()] * 3 + [anywhere()] * len(before),
        out_specs=[vmem()] * 3,
        out_shape=[shaped(bf16, 2 * margin, wide, lanes)] * 2 + [shaped(f32, *running.shape)],
        compiler_params=params(8),
        cost_estimate=cost(1000, 3_000_000),
        name="corners",
    )(left, right, running, *before)


def fill_extended(ext, halos, blocks):
    tile, left, right, top, bottom, up, down = halos
    rows, cols, _ = tile.shape
    off, after = lead - margin, lead + cols

    def put(at, row, middle, before, behind, skip=0):
        before, behind = before[row].astype(f32), behind[row + skip].astype(f32)
        for number, block in blocks:
            place = slice(margin * number, margin * (number + 1))
            line = ext(block, at)
            line[lead:after, :] = middle[row, :, 128 * block : 128 * (block + 1)].astype(f32)
            line[off:lead, :] = before[place]
            line[after : after + margin, :] = behind[place]

    def tile_row(row, carry):
        put(margin + row, row, tile, left, right)
        return carry

    def strip_row(row, carry):
        put(row, row, top, up, up, margin)
        put(margin + rows + row, row, bottom, down, down, margin)
        return carry

    lax.fori_loop(0, rows, tile_row, 0)
    lax.fori_loop(0, margin, strip_row, 0)


def halo_specs(halos, lanes):
    return [
        by_lanes(*halo.shape[:2], lanes=lanes) if number in (0, 3, 4) else whole(*halo.shape)
        for number, halo in enumerate(halos)
    ]


def fill_taps(taps, kernel_ref):
    for member in range(3):
        for tap in range(9):
            taps[9 * member + tap] = jnp.broadcast_to(
                kernel_ref[member, tap : tap + 1, :], taps.shape[1:]
            )


def pack(row_ref, value, vector):
    size, part = value.shape
    row_ref[...] = jnp.zeros_like(row_ref)
    for number in range(size // 16):
        row_ref[:, part * number : part * (number + 1)] = value[16 * number : 16 * (number + 1)]
    row_ref[0:1, 640 : 640 + vector.shape[1]] = vector
    return row_ref[...].astype(bf16)


def unpack(message, put, part, size, fan):
    for number in range(size // 16):
        put(number, message[:, part * number : part * (number + 1)])
    return message[0:1, 640 : 640 + fan]


def conv_body(
    id_ref, tile_ref, left_ref, right_ref, top_ref, bottom_ref, up_ref, down_ref, kernel_ref,
    weight_ref, pooled_ref, cot_ref,
    inputs_ref, own_ref, one_ref, two_ref, three_ref, own_cot_ref, own_pool_ref,
    ext, cells, taps, total, pool, rows_ref,
):
    step = pl.program_id(0)
    halos = (tile_ref, left_ref, right_ref, top_ref, bottom_ref, up_ref, down_ref)
    rows, cols, _ = tile_ref.shape
    blocks, lanes = 2, 128
    fan = weight_ref.shape[2]

    @pl.when(step == 0)
    def _():
        total[...] = jnp.zeros_like(total)
        pool[...] = jnp.zeros_like(pool)

    fill_taps(taps, kernel_ref)

    for number in range(2):

        @pl.when(step == number)
        def _(number=number):
            fill_extended(
                lambda block, row: ext.at[block, row],
                halos,
                [(blocks * number + block, block) for block in range(blocks)],
            )

    for block in range(blocks):
        across = slice(lanes * block, lanes * (block + 1))

        def conv_rows(pair, carry, block=block, across=across):
            at = (2 * pair, 2 * pair + 1)
            places = [pl.ds(pl.multiple_of(row * cols, 8), cols) for row in at]
            for row, place in zip(at, places):
                cells[0, place, across] = ext[block, margin + row, lead : lead + cols, :]
            for member, spacing in enumerate(dilations):
                summed = [None, None]
                for step_lon in (-1, 0, 1):
                    group, shift = window_of(spacing, step_lon)
                    count = cols // 8 + (shift != 0)
                    part = [None, None]
                    for step_lat in (-1, 0, 1):
                        tap = taps[9 * member + 3 * (step_lat + 1) + step_lon + 1, :, across]
                        for n in (0, 1):
                            window = ext[
                                block,
                                at[n] + margin + step_lat * spacing,
                                8 * group : 8 * (group + count),
                                :,
                            ].reshape(count, 8, lanes)
                            term = window * tap
                            part[n] = term if part[n] is None else part[n] + term
                    for n in (0, 1):
                        piece = roll_rows(part[n].reshape(8 * count, lanes), shift, cols)
                        summed[n] = piece if summed[n] is None else summed[n] + piece
                for n in (0, 1):
                    cells[member + 1, places[n], across] = summed[n]
            return carry

        lax.fori_loop(0, rows // 2, conv_rows, 0)
    for member in range(4):
        block = cells[member].astype(bf16)
        inputs_ref[member] = block
        total[:, fan * member : fan * (member + 1)] += jnp.dot(
            block, weight_ref[member], preferred_element_type=f32
        )
    pool[...] += jnp.dot(
        jnp.broadcast_to(pooled_ref[...], (8, blocks * lanes)),
        weight_ref[4].astype(f32),
        precision=lax.Precision.HIGHEST,
        preferred_element_type=f32,
    )

    @pl.when(step == pl.num_programs(0) - 1)
    def _():
        size = own_ref.shape[0]
        me = id_ref[0]
        band = rows // 4
        part = cot_ref.shape[2]

        def chunk(ahead):
            return total[pl.ds(pl.multiple_of(lax.rem(me + ahead, 4) * size, 16), size), :]

        def cot_chunk(ahead):
            picked = cot_ref[pl.ds(lax.rem(me + ahead, 4) * band, band)]
            return picked.astype(f32).reshape(size, part)

        own_ref[...] = chunk(0)
        own_cot_ref[...] = cot_chunk(0)
        own_pool_ref[...] = pool[0:1, :]
        for ahead, ref in enumerate((one_ref, two_ref, three_ref), 1):
            ref[:size, :] = chunk(ahead).astype(bf16)
            ref[size:, :] = pack(rows_ref, cot_chunk(ahead), pool[0:1, :])


def conv_forward(ids, halos, kernel, weight, pooled, cotangent):
    rows, cols, chan = halos[0].shape
    tall, wide = rows + 2 * margin, cols + 2 * lead
    fan = weight.shape[2]
    lanes = 256
    size = rows * cols // 4
    cells = rows * cols
    part = cotangent.shape[2]
    return pl.pallas_call(
        conv_body,
        grid=(chan // lanes,),
        in_specs=[smem()]
        + halo_specs(halos, lanes)
        + [
            by_lanes(3, 9, lanes=lanes),
            pl.BlockSpec((5, lanes, fan), lambda i: (0, i, 0)),
            by_lanes(1, lanes=lanes),
            whole(*cotangent.shape),
        ],
        out_specs=[by_lanes(4, cells, lanes=lanes), whole(size, 4 * fan)]
        + [whole(size + 16, 4 * fan)] * 3
        + [whole(size, part), whole(1, fan)],
        out_shape=[
            far(bf16, 4, cells, chan),
            far(f32, size, 4 * fan),
        ]
        + [shaped(bf16, size + 16, 4 * fan)] * 3
        + [shaped(f32, size, part), shaped(f32, 1, fan)],
        scratch_shapes=[
            pltpu.VMEM((lanes // 128, tall, wide, 128), f32),
            pltpu.VMEM((4, cells, lanes), f32),
            pltpu.VMEM((27, 8, lanes), f32),
            pltpu.VMEM((cells, 4 * fan), f32),
            pltpu.VMEM((8, fan), f32),
            pltpu.VMEM((16, 4 * fan), f32),
        ],
        compiler_params=params(58),
        cost_estimate=cost(2 * cells * chan * (4 * fan + 27), 20_000_000),
        name="conv_forward",
    )(ids, stay(halos[0]), *halos[1:], kernel, weight, pooled, cotangent)


def slope(value, sig):
    return sig * (1.0 + value * (1.0 - sig))


def proj_body(
    id_ref, own_ref, one_ref, two_ref, three_ref, own_cot_ref, own_pool_ref,
    weight_own, weight_one, weight_two, weight_three, last_ref, dpre_ref, send_one_ref, send_two_ref, send_three_ref,
    grad_own_ref, own_mixed_ref, own_sum_ref, pool_ref,
    pre, grads, weights, pieces, cot, rows_ref,
):
    size, part = own_cot_ref.shape
    fan = 4 * part
    me = id_ref[0]
    pre[...] = own_ref[...]
    pool = own_pool_ref[...]
    pieces[me] = own_cot_ref[...]
    for behind, ref in enumerate((one_ref, two_ref, three_ref), 1):
        pre[...] += ref[:size, :].astype(f32)
        origin = lax.rem(me + 4 - behind, 4)

        def put(number, value, origin=origin):
            pieces[origin, 16 * number : 16 * (number + 1), :] = value

        pool = pool + unpack(ref[size:, :].astype(f32), put, part, size, fan)
    for origin in range(4):
        cot[:, part * origin : part * (origin + 1)] = pieces[origin]
    for behind, ref in enumerate((weight_own, weight_one, weight_two, weight_three)):
        first = pl.multiple_of(lax.rem(me + 4 - behind, 4) * part, 16)
        weights[:, pl.ds(first, part), :] = ref[...]
    last_ref[...] = weights[4]

    pool_ref[...] = pool
    pool = jnp.broadcast_to(pool, (8, fan))
    pool_branch = (pool * jax.nn.sigmoid(pool)).astype(bf16)
    proj = jnp.dot(pool_branch, weights[4], preferred_element_type=f32)[0:1, :]
    for member in range(4):
        value = pre[:, fan * member : fan * (member + 1)]
        branch = (value * jax.nn.sigmoid(value)).astype(bf16)
        proj = proj + jnp.dot(branch, weights[member], preferred_element_type=f32)
    sig = jax.nn.sigmoid(proj)
    mixed = (proj * sig).astype(bf16).astype(f32)
    back = (cot[...] * slope(proj, sig)).astype(bf16)
    back_sum = jnp.sum(back.astype(f32), axis=0, keepdims=True)
    own_sum_ref[...] = back_sum
    for target in range(4):
        pieces[target] = mixed[:, part * target : part * (target + 1)]
    own_mixed_ref[...] = pieces[me]
    for member in range(4):
        lanes = slice(fan * member, fan * (member + 1))
        value = pre[:, lanes]
        sig = jax.nn.sigmoid(value)
        branch = (value * sig).astype(bf16)
        grads[member] = lax.dot_general(
            branch, back, (((0,), (0,)), ((), ())), preferred_element_type=f32
        )
        dbranch = lax.dot_general(
            back, weights[member], (((1,), (1,)), ((), ())), preferred_element_type=f32
        )
        dpre = (dbranch * slope(value, sig)).astype(bf16)
        for ref in (dpre_ref, send_one_ref, send_two_ref, send_three_ref):
            ref[:size, lanes] = dpre
        grad_own_ref[member] = grads[member, pl.ds(pl.multiple_of(me * part, 16), part), :]
        for ahead, ref in enumerate((send_one_ref, send_two_ref, send_three_ref), 1):
            first = pl.multiple_of(lax.rem(me + ahead, 4) * part, 16)
            ref[size + 16 :, lanes] = grads[member, pl.ds(first, part), :].astype(bf16)
    for ahead, ref in enumerate((send_one_ref, send_two_ref, send_three_ref), 1):
        ref[size : size + 16, :] = pack(rows_ref, pieces[lax.rem(me + ahead, 4)], back_sum)


def project(ids, own, others, own_cot, own_pool, weights):
    size, wide = own.shape
    fan = wide // 4
    part = fan // 4
    return pl.pallas_call(
        proj_body,
        in_specs=[smem()] + [vmem()] * 10,
        out_specs=[vmem()] * 9,
        out_shape=[shaped(bf16, fan, fan), shaped(bf16, size, wide)]
        + [shaped(bf16, size + 16 + part, wide)] * 3
        + [shaped(f32, 4, part, fan)]
        + [shaped(f32, size, part), shaped(f32, 1, fan), shaped(f32, 1, fan)],
        scratch_shapes=[
            pltpu.VMEM((size, wide), f32),
            pltpu.VMEM((4, fan, fan), f32),
            pltpu.VMEM((5, fan, fan), bf16),
            pltpu.VMEM((4, size, part), f32),
            pltpu.VMEM((size, fan), f32),
            pltpu.VMEM((16, wide), f32),
        ],
        compiler_params=params(16),
        cost_estimate=cost(6 * size * wide * fan, 4_000_000, 2 * size * wide),
        name="project",
    )(ids, stay(own), *others, own_cot, own_pool, *weights)


def weight_body(
    id_ref, own_ref, gp_ref, one_ref, two_ref, three_ref, inputs_ref,
    keep_ref, give_ref, full_ref, total_ref,
):
    size = own_ref.shape[0]
    fan = keep_ref.shape[2]
    me, upper = id_ref[0], id_ref[1]
    others = (one_ref, two_ref, three_ref)
    full_ref[pl.ds(pl.multiple_of(me * size, 16), size), :] = own_ref[...]
    for behind, ref in enumerate(others, 1):
        first = pl.multiple_of(lax.rem(me + 4 - behind, 4) * size, 16)
        full_ref[pl.ds(first, size), :] = ref[:size, :]

    def grad(member):
        lanes = pl.ds(pl.multiple_of(member * fan, 256), fan)
        return lax.dot_general(
            inputs_ref[member],
            full_ref[:, lanes],
            (((0,), (0,)), ((), ())),
            preferred_element_type=f32,
        )

    for number in range(2):
        give_ref[number] = grad(2 * (1 - upper) + number).astype(bf16)
        keep_ref[number] = grad(2 * upper + number)
    for member in range(4):
        value = gp_ref[member]
        for ref in others:
            value = value + ref[size + 16 :, fan * member : fan * (member + 1)].astype(f32)
        total_ref[member] = value


def weight_grads(ids, own, gp_own, others, inputs):
    size, wide = own.shape
    fan = wide // 4
    part = fan // 4
    _, cells, chan = inputs.shape
    return pl.pallas_call(
        weight_body,
        in_specs=[smem()] + [vmem()] * 6,
        out_specs=[vmem()] * 4,
        out_shape=[
            shaped(f32, 2, chan, fan),
            shaped(bf16, 2, chan, fan),
            shaped(bf16, cells, wide),
            shaped(f32, 4, part, fan),
        ],
        compiler_params=params(20),
        cost_estimate=cost(2 * cells * chan * wide, 6_000_000),
        name="weight_grads",
    )(ids, own, gp_own, *others, stay(inputs))


def unpack_body(
    id_ref, own_mixed_ref, own_sum_ref, one_ref, two_ref, three_ref, mixed_ref, sum_ref, pieces
):
    size, part = own_mixed_ref.shape
    me = id_ref[0]
    pieces[me] = own_mixed_ref[...]
    total = own_sum_ref[...]
    for behind, ref in enumerate((one_ref, two_ref, three_ref), 1):
        origin = lax.rem(me + 4 - behind, 4)

        def put(number, value, origin=origin):
            pieces[origin, 16 * number : 16 * (number + 1), :] = value

        total = total + unpack(ref[...].astype(f32), put, part, size, 4 * part)
    mixed_ref[...] = pieces[...].astype(bf16)
    sum_ref[...] = total


def unpack_mixed(ids, own_mixed, own_sum, others):
    size, part = own_mixed.shape
    rows = pl.BlockSpec((16, others[0].shape[1]), lambda i: (size // 16, 0))
    return pl.pallas_call(
        unpack_body,
        grid=(1,),
        in_specs=[smem(), whole(size, part), whole(*own_sum.shape)] + [rows] * 3,
        out_specs=[whole(4, size, part), whole(*own_sum.shape)],
        out_shape=[shaped(bf16, 4, size, part), shaped(f32, *own_sum.shape)],
        scratch_shapes=[pltpu.VMEM((4, size, part), f32)],
        compiler_params=params(8),
        cost_estimate=cost(100_000, 500_000),
        name="unpack_mixed",
    )(ids, own_mixed, own_sum, *[stay(value) for value in others])


placed = {}
for _member in range(3):
    for _step in (-1, 0, 1):
        _key = (_member, window_of(dilations[_member], _step)[1])
        placed.setdefault(_key, len(placed))


def shift_rows(shifted, source, rows, cols, lanes):
    def row_step(row, carry):
        place = pl.ds(pl.multiple_of(row * cols, 8), cols)
        for member in range(3):
            value = source(member, place)
            wide = jnp.concatenate([value, jnp.zeros((8, lanes), f32)], axis=0)
            for (owner, shift), number in placed.items():
                if owner != member:
                    continue
                shifted[number, row] = pltpu.roll(wide, shift, 0) if shift else wide
        return carry

    lax.fori_loop(0, rows, row_step, 0)


def scatter_body(
    dpre_ref, weight_ref, kernel_ref, _,
    grad_ref, center_ref, left_ref, right_ref, up_ref, up_two, down_ref, down_two, token_ref,
    taps, first, grads, shifted,
):
    rows, cols, lanes = center_ref.shape
    fan = weight_ref.shape[2]
    wide = cols + 2 * margin
    groups = (cols + 2 * lead) // 8
    off = lead - margin
    fill_taps(taps, kernel_ref)
    token_ref[...] = jnp.zeros_like(token_ref)
    for member in range(4):
        piece = lax.dot_general(
            dpre_ref[:, fan * member : fan * (member + 1)],
            weight_ref[member],
            (((1,), (1,)), ((), ())),
            preferred_element_type=f32,
        )
        if member == 0:
            first[...] = piece
        else:
            piece = piece.astype(bf16)
            grad_ref[member - 1] = piece
            grads[member - 1] = piece.astype(f32)
    shift_rows(shifted, lambda member, place: grads[member, place, :], rows, cols, lanes)

    for begin in range(0, rows + 2 * margin, 6):
        active = [
            (member, step_lat)
            for member, spacing in enumerate(dilations)
            for step_lat in (-1, 0, 1)
            if margin + step_lat * spacing <= begin < margin + rows + step_lat * spacing
        ]

        def ext_rows(step, carry, begin=begin, active=active):
            at = (begin + 2 * step, begin + 2 * step + 1)
            inside = margin <= begin < margin + rows
            sums = [[None] * groups, [None] * groups]
            for n in (0, 1):
                if inside:
                    value = first[pl.ds(pl.multiple_of((at[n] - margin) * cols, 8), cols), :]
                    for number in range(cols // 8):
                        sums[n][lead // 8 + number] = value[8 * number : 8 * (number + 1)]
            for member, step_lat in active:
                spacing = dilations[member]
                for step_lon in (-1, 0, 1):
                    group, shift = window_of(spacing, step_lon)
                    count = cols // 8 + (shift != 0)
                    weight = taps[9 * member + 3 * (step_lat + 1) + step_lon + 1]
                    for n in (0, 1):
                        grad = shifted[
                            placed[member, shift], at[n] - margin - step_lat * spacing, : 8 * count, :
                        ]
                        for number in range(count):
                            term = grad[8 * number : 8 * (number + 1)] * weight
                            old = sums[n][group + number]
                            sums[n][group + number] = term if old is None else old + term
            for n in (0, 1):
                parts = [jnp.zeros((8, lanes), f32) if s is None else s for s in sums[n]]
                if inside:
                    row = at[n] - margin
                    center = jnp.concatenate(parts[lead // 8 : (lead + cols) // 8], axis=0)
                    center_ref[row] = center.astype(bf16)
                    left = roll_rows(jnp.concatenate(parts[: lead // 8], axis=0), off, margin)
                    left_ref[row] = left.astype(bf16)
                    right = jnp.concatenate(parts[(lead + cols) // 8 :], axis=0)[:margin]
                    right_ref[row] = right.astype(bf16)
                else:
                    line = roll_rows(jnp.concatenate(parts, axis=0), off, wide).astype(bf16)
                    pair, number = (
                        ((up_ref, up_two), at[n])
                        if begin < margin
                        else ((down_ref, down_two), at[n] - margin - rows)
                    )
                    half = pair[0].shape[0]

                    @pl.when(number < half)
                    def _(ref=pair[0], number=number, line=line):
                        ref[number] = line

                    @pl.when(number >= half)
                    def _(ref=pair[1], number=number, line=line):
                        ref[number - half] = line
            return carry

        lax.fori_loop(0, 3, ext_rows, 0)


def scatter_grads(dpre, weight, kernel, rows, cols, before):
    cells, wide_fan = dpre.shape
    fan = wide_fan // 4
    chan = weight.shape[1]
    wide = cols + 2 * margin
    lanes = 128
    return pl.pallas_call(
        scatter_body,
        grid=(chan // lanes,),
        in_specs=[
            whole(cells, wide_fan),
            pl.BlockSpec((4, lanes, fan), lambda i: (0, i, 0)),
            by_lanes(3, 9),
            anywhere(),
        ],
        out_specs=[
            by_lanes(3, cells),
            by_lanes(rows, cols),
            by_lanes(rows, margin),
            by_lanes(rows, margin),
        ]
        + [by_lanes(margin // 2, wide)] * 4
        + [whole(8, 128)],
        out_shape=[
            far(bf16, 3, cells, chan),
            far(bf16, rows, cols, chan),
            far(bf16, rows, margin, chan),
            far(bf16, rows, margin, chan),
        ]
        + [shaped(bf16, margin // 2, wide, chan)] * 4
        + [shaped(f32, 8, 128)],
        scratch_shapes=[
            pltpu.VMEM((27, 8, lanes), f32),
            pltpu.VMEM((cells, lanes), f32),
            pltpu.VMEM((3, cells, lanes), f32),
            pltpu.VMEM((len(placed), rows, cols + 8, lanes), f32),
        ],
        compiler_params=params(16),
        cost_estimate=cost(2 * cells * chan * (wide_fan + 27), 15_000_000),
        name="scatter_grads",
    )(dpre, weight, kernel, before)


def taps_body(
    grad_ref, tile_ref, left_ref, right_ref, top_ref, bottom_ref, up_ref, down_ref, sum_ref,
    tap_ref, ext, grads, shifted,
):
    step = pl.program_id(0)
    rows, cols, lanes = tile_ref.shape
    halos = (tile_ref, left_ref, right_ref, top_ref, bottom_ref, up_ref, down_ref)
    per = sum_ref.shape[1] // lanes
    first = 32 * (step // per)
    place = pl.ds(pl.multiple_of(lanes * lax.rem(step, per), 128), lanes)

    @pl.when(step == 0)
    def _():
        ext[...] = jnp.zeros_like(ext)

    for number in range(4):

        @pl.when(step == number)
        def _(number=number):
            fill_extended(lambda _, row: ext.at[row], halos, [(number, 0)])

    grads[...] = grad_ref[...].astype(f32)
    shift_rows(shifted, lambda member, place: grads[member, place, :], rows, cols, lanes)

    def tap_row(row, carry):
        sums = list(carry)
        for member, spacing in enumerate(dilations):
            for step_lon in (-1, 0, 1):
                group, shift = window_of(spacing, step_lon)
                count = cols // 8 + (shift != 0)
                grad = shifted[placed[member, shift], row, : 8 * count, :].reshape(count, 8, lanes)
                for step_lat in (-1, 0, 1):
                    window = ext[
                        row + margin + step_lat * spacing, 8 * group : 8 * (group + count), :
                    ].reshape(count, 8, lanes)
                    tap = 9 * member + 3 * (step_lat + 1) + step_lon + 1
                    sums[tap] = sums[tap] + jnp.sum(grad * window, axis=0)
        return tuple(sums)

    sums = lax.fori_loop(0, rows, tap_row, (jnp.zeros((8, lanes), f32),) * 27)
    rows_of = [jnp.sum(value, axis=0, keepdims=True) for value in sums]
    rows_of.append(sum_ref[:, place])
    rows_of += [jnp.zeros((1, lanes), f32)] * 4
    tap_ref[pl.ds(pl.multiple_of(first, 32), 32), place] = jnp.concatenate(rows_of, axis=0)


def tap_sums(grads, halos, back_sum):
    rows, cols, chan = halos[0].shape
    _, cells, _ = grads.shape
    lanes = 128
    shape = (32 * chan // back_sum.shape[1], back_sum.shape[1])
    return pl.pallas_call(
        taps_body,
        grid=(chan // lanes,),
        in_specs=[by_lanes(3, cells)] + halo_specs(halos, lanes) + [whole(*back_sum.shape)],
        out_specs=whole(*shape),
        out_shape=shaped(f32, *shape),
        scratch_shapes=[
            pltpu.VMEM((rows + 2 * margin, cols + 2 * lead, lanes), f32),
            pltpu.VMEM((3, cells, lanes), f32),
            pltpu.VMEM((len(placed), rows, cols + 8, lanes), f32),
        ],
        compiler_params=params(20),
        cost_estimate=cost(2 * cells * chan * 27, 15_000_000),
        name="tap_sums",
    )(stay(grads), *[stay(halo) for halo in halos], back_sum)


def home_body(
    center_ref, left_ref, right_ref, above_ref, above_two, below_ref, below_two,
    center_out, left_out, right_out, packed,
):
    rows, cols, chan = center_ref.shape
    shifted = rows - margin

    def one_row(row, refs):
        line = None
        for ref, first in refs:
            piece = ref[row - first].astype(f32)
            line = piece if line is None else line + piece
        left = left_ref[row].astype(f32) + line[:margin]
        center_out[row] = center_ref[row].astype(f32) + roll_rows(line, margin, cols)
        right = right_ref[row].astype(f32) + roll_rows(line, margin + cols, margin)
        for number, (one, two) in enumerate(zip(split_lanes(left), split_lanes(right))):
            place = slice(margin * number, margin * (number + 1))
            packed[0, row, place, :] = one
            packed[1, row, place, :] = two

    half = margin // 2
    pieces = [(above_ref, 0), (above_two, half), (below_ref, shifted), (below_two, shifted + half)]
    cuts = sorted({0, rows} | {at for _, first in pieces for at in (first, first + half)})
    for first, last in zip(cuts, cuts[1:]):
        refs = [piece for piece in pieces if piece[1] <= first < piece[1] + half]

        def step(number, carry, first=first, refs=refs):
            one_row(first + number, refs)
            return carry

        lax.fori_loop(0, last - first, step, 0)
    left_out[...] = packed[0].astype(bf16)
    right_out[...] = packed[1].astype(bf16)


def home(center, left, right, above, below):
    rows, cols, chan = center.shape
    wide = margin * chan // 128
    return pl.pallas_call(
        home_body,
        in_specs=[vmem()] * 7,
        out_specs=[vmem()] * 3,
        out_shape=[far(f32, rows, cols, chan)] + [shaped(bf16, rows, wide, 128)] * 2,
        scratch_shapes=[pltpu.VMEM((2, rows, wide, 128), f32)],
        compiler_params=params(16),
        cost_estimate=cost(rows * cols * chan, 8_000_000),
        name="home",
    )(stay(center), stay(left), stay(right), *above, *below)


def finish_body(center_ref, left_ref, right_ref, pooled_ref, out_ref, pads):
    rows, cols, chan = center_ref.shape
    base = pooled_ref[...]

    @pl.when(pl.program_id(0) == 0)
    def _():
        pads[...] = jnp.zeros_like(pads)

    def row_step(row, carry):
        left, right = left_ref[row].astype(f32), right_ref[row].astype(f32)
        for number in range(chan // 128):
            place = slice(margin * number, margin * (number + 1))
            across = slice(128 * number, 128 * (number + 1))
            pads[0, row, :margin, across] = left[place]
            pads[1, row, cols - margin :, across] = right[place]
        return carry

    lax.fori_loop(0, rows, row_step, 0)

    def add_row(row, carry):
        out_ref[row] = (center_ref[row] + pads[0, row] + pads[1, row] + base).astype(bf16)
        return carry

    lax.fori_loop(0, rows, add_row, 0)


def finish(center, left, right, pooled):
    rows, cols, chan = center.shape
    wide = margin * chan // 128
    block = rows // 3
    by_rows = lambda *shape: pl.BlockSpec((block,) + shape, lambda i: (i, 0, 0))
    return pl.pallas_call(
        finish_body,
        grid=(3,),
        in_specs=[by_rows(cols, chan), by_rows(wide, 128), by_rows(wide, 128), whole(1, chan)],
        out_specs=by_rows(cols, chan),
        out_shape=shaped(bf16, rows, cols, chan),
        scratch_shapes=[pltpu.VMEM((2, block, cols, chan), f32)],
        compiler_params=params(10),
        cost_estimate=cost(rows * cols * chan, 4_000_000),
        name="finish",
    )(center, left, right, pooled)


def core_body(id_ref, keep_ref, got_ref, gp_ref, own_ref, one_ref, two_ref, three_ref, token_ref):
    token_ref[...] = jnp.zeros_like(token_ref)
    fan = keep_ref.shape[1]
    rows = own_ref.shape[0] - gp_ref.shape[1]
    here = id_ref[2]
    for code, ref in enumerate((own_ref, one_ref, two_ref, three_ref)):
        target = here ^ code
        place = pl.ds(pl.multiple_of(target * rows, 16), rows)
        ref[:rows, :] = (keep_ref[place, :] + got_ref[place, :].astype(f32)).astype(ref.dtype)
        ref[rows:, :] = gp_ref[target].astype(ref.dtype)


def core_stage(ids, keep, got, gp):
    rows, fan = keep.shape
    part = gp.shape[1]
    size = rows // 4 + part
    return pl.pallas_call(
        core_body,
        in_specs=[smem()] + [vmem()] * 3,
        out_specs=[vmem()] * 5,
        out_shape=[shaped(f32, size, fan)] + [shaped(bf16, size, fan)] * 3 + [shaped(f32, 8, 128)],
        compiler_params=params(12),
        cost_estimate=cost(rows * fan, 3_000_000),
        name="core_stage",
    )(ids, keep, got, gp)


def y_body(id_ref, own_ref, one_ref, two_ref, three_ref, _, keep_ref, give_ref, total):
    half, _ = keep_ref.shape
    upper = id_ref[3]
    total[...] = (
        own_ref[...] + one_ref[...].astype(f32) + two_ref[...].astype(f32) + three_ref[...].astype(f32)
    )
    keep_ref[...] = total[pl.ds(pl.multiple_of(upper * half, 16), half), :]
    give_ref[...] = total[pl.ds(pl.multiple_of((1 - upper) * half, 16), half), :].astype(bf16)


def y_stage(ids, own, others, before):
    size, fan = own.shape
    return pl.pallas_call(
        y_body,
        in_specs=[smem()] + [vmem()] * 4 + [anywhere()],
        out_specs=[vmem()] * 2,
        out_shape=[shaped(f32, size // 2, fan), shaped(bf16, size // 2, fan)],
        scratch_shapes=[pltpu.VMEM((size, fan), f32)],
        compiler_params=params(8),
        cost_estimate=cost(size * fan, 1_000_000),
        name="y_stage",
    )(ids, own, *others, before)


def gather_body(id_ref, own_ref, extra_ref, one_ref, two_ref, three_ref, out_ref, sum_ref):
    size = own_ref.shape[0]
    here = id_ref[2]
    total = extra_ref[...]
    out_ref[pl.ds(pl.multiple_of(here * size, 16), size), :] = own_ref[...]
    for code, ref in enumerate((one_ref, two_ref, three_ref), 1):
        place = pl.ds(pl.multiple_of((here ^ code) * size, 16), size)
        out_ref[place, :] = ref[:size, :]
        total = total + ref[size:, :].astype(f32)
    out_ref[4 * size :, :] = total.astype(bf16)
    sum_ref[...] = total


def y_gather(ids, own, extra, others):
    size, fan = own.shape
    count = extra.shape[0]
    return pl.pallas_call(
        gather_body,
        in_specs=[smem()] + [vmem()] * 5,
        out_specs=[vmem()] * 2,
        out_shape=[shaped(bf16, 4 * size + count, fan), shaped(f32, count, fan)],
        compiler_params=params(8),
        cost_estimate=cost(size * fan, 2_000_000),
        name="y_gather",
    )(ids, own, extra, *others)


def last_body(
    id_ref, own_ref, got_ref, own_extra_ref, got_extra_ref, weight_ref, proj_ref, pool_ref, pooled_ref,
    branch_ref, grad_proj_ref, depth_ref, dpooled_ref, dpool, column, *, cells,
):
    highest = lax.Precision.HIGHEST
    _, chan, lanes = branch_ref.shape
    part = grad_proj_ref.shape[1]
    fan = 4 * part
    scale = 1.0 / math.sqrt(cells)
    me, upper = id_ref[0], id_ref[1]
    step = pl.program_id(0)
    size = chan // 2 + part
    top = lax.broadcasted_iota(jnp.int32, (8, lanes), 0) == 0

    def outer(column_of, row_of):
        return lax.dot_general(
            column_of,
            jnp.where(top, row_of, 0.0),
            (((0,), (0,)), ((), ())),
            precision=highest,
            preferred_element_type=f32,
        )

    @pl.when(step == 0)
    def _():
        extra = own_extra_ref[...] + got_extra_ref[4 * size :, :].astype(f32)
        for number in range(chan // fan):
            for tap in range(27):
                row = 32 * number + tap
                depth_ref[tap // 9, tap % 9 : tap % 9 + 1, fan * number : fan * (number + 1)] = (
                    extra[row : row + 1] * scale
                )
        back_sum = jnp.broadcast_to(extra[27:28], (8, fan))
        pool = jnp.broadcast_to(pool_ref[...], (8, fan))
        sig = jax.nn.sigmoid(pool)
        full = slope(pool, sig) * lax.dot_general(
            back_sum,
            proj_ref[...].astype(f32),
            (((1,), (1,)), ((), ())),
            precision=highest,
            preferred_element_type=f32,
        )
        dpooled = lax.dot_general(
            full,
            weight_ref[0].astype(f32),
            (((1,), (1,)), ((), ())),
            precision=highest,
            preferred_element_type=f32,
        )
        dpooled_ref[...] = dpooled[0:1] * (1.0 / cells)
        pool_branch = (pool * sig).astype(bf16).astype(f32)
        for number in range(fan // lanes):
            dpool[0, number] = full[:, lanes * number : lanes * (number + 1)]
            dpool[1, number] = back_sum[:, lanes * number : lanes * (number + 1)]
        for origin in range(4):
            column[origin] = pool_branch[:, part * origin : part * (origin + 1)]

    for number in range(4):
        first = size * number
        rows = slice(chan // 2 * (number % 2), chan // 2 * (number % 2 + 1))
        for ref, half in ((own_ref, upper), (got_ref, 1 - upper)):
            branch_ref[2 * half + number // 2, rows, :] = (
                ref[first : first + chan // 2, :].astype(f32) * scale
            )
        both = own_ref[first + chan // 2 : first + size, :].astype(f32)
        both = both + got_ref[first + chan // 2 : first + size, :].astype(f32)
        grad_proj_ref[number] = both * scale
    branch_ref[4] = outer(jnp.broadcast_to(pooled_ref[...], (8, chan)), dpool[0, step]) * scale
    grad_proj_ref[4] = outer(column[me], dpool[1, step]) * scale


def last_stage(ids, own, got, extra, weight, proj, pool_pre, pooled, cells):
    _, chan, fan = weight.shape
    part = fan // 4
    return pl.pallas_call(
        lambda *refs: last_body(*refs, cells=cells),
        grid=(fan // 128,),
        in_specs=[
            smem(),
            by_lanes(own.shape[0]),
            by_lanes(got.shape[0]),
            whole(*extra.shape),
            whole(*got.shape),
            pl.BlockSpec((1, chan, fan), lambda i: (4, 0, 0)),
            whole(*proj.shape),
            whole(*pool_pre.shape),
            whole(*pooled.shape),
        ],
        out_specs=[by_lanes(5, chan), by_lanes(5, part), whole(3, 9, chan), whole(1, chan)],
        out_shape=[
            shaped(f32, 5, chan, fan),
            shaped(f32, 5, part, fan),
            shaped(f32, 3, 9, chan),
            shaped(f32, 1, chan),
        ],
        scratch_shapes=[
            pltpu.VMEM((2, fan // 128, 8, 128), f32),
            pltpu.VMEM((4, 8, part), f32),
        ],
        compiler_params=params(18),
        cost_estimate=cost(8 * chan * fan, 5_000_000),
        name="last_stage",
    )(ids, own, got, extra, got, weight, proj, pool_pre, pooled)


def shift(value, axis, ahead, closed=True):
    count = lax.axis_size(axis)
    pairs = [
        (i, (i + ahead) % count) for i in range(count) if closed or 0 <= i + ahead < count
    ]
    return lax.ppermute(value, axis, pairs)


def place_in_grid():
    return lax.axis_index("lon") * lax.axis_size("lat") + lax.axis_index("lat")


def swap(value, mask):
    count = lax.axis_size("lon") * lax.axis_size("lat")
    return lax.ppermute(value, GRID, [(i, i ^ mask) for i in range(count)])


def has(mask):
    return (place_in_grid() & mask) != 0


def number_in(bits):
    return sum(has(bit).astype(jnp.int32) << at for at, bit in enumerate(bits))


def mask_of(bits, code):
    return sum(bit for at, bit in enumerate(bits) if (code >> at) & 1)


def grid_sum(value):
    mask = 1
    while mask < lax.axis_size("lon") * lax.axis_size("lat"):
        value = value + swap(value, mask)
        mask *= 2
    return value


core_bit, y_bits = 1, (4, 2)


def z_bits():
    bits, mask = [], 8
    while mask < lax.axis_size("lon") * lax.axis_size("lat"):
        bits.append(mask)
        mask *= 2
    return bits


def per_device(features, depth_kernel, branch_weight, proj_weight, cotangent):
    rows, cols, chan = features.shape
    fan = branch_weight.shape[2]
    part = proj_weight.shape[1]
    cell_count = rows * cols * lax.axis_size("lat") * lax.axis_size("lon")
    me = lax.axis_index("ch")
    flag = lambda mask: has(mask).astype(jnp.int32)
    ids = jnp.stack(
        [me.astype(jnp.int32), flag(core_bit), number_in(y_bits), flag(z_bits()[0])]
    )
    tie = lax.optimization_barrier

    to_right, to_left, colsum = edges(features)
    to_right, to_left, tile = tie((to_right, to_left, features))
    left = shift(to_right, "lon", 1)
    right = shift(to_left, "lon", -1)
    top = shift(tile[rows - margin :], "lat", 1, False)
    bottom = shift(tile[:margin], "lat", -1, False)

    proj_others = [shift(proj_weight, "ch", d) for d in (1, 2, 3)]
    pooled = colsum.reshape(chan // 128, 128)
    bits = z_bits()
    for mask in [core_bit, *bits[:2], y_bits[0]]:
        pooled = pooled + swap(pooled, mask)
    up, down, pooled = corners(left, right, pooled, (top, bottom))
    up = shift(up, "lat", 1, False)
    down = shift(down, "lat", -1, False)
    for mask in [*bits[2:], y_bits[1]]:
        pooled = pooled + swap(pooled, mask)
    pooled = pooled.reshape(1, chan) / cell_count

    halos = (features, left, right, top, bottom, up, down)
    inputs, own, *ahead, own_cot, own_pool = conv_forward(
        ids, halos, depth_kernel, branch_weight, pooled, cotangent
    )
    ahead, proj_others = tie((ahead, proj_others))
    others = [shift(value, "ch", d) for d, value in enumerate(ahead, 1)]
    proj_last, dpre, *sent, gp_own, own_mixed, own_sum, pool_pre = project(
        ids, own, others, own_cot, own_pool, [proj_weight, *proj_others]
    )
    others = [shift(value, "ch", d) for d, value in enumerate(sent, 1)]
    keep, give, dpre_full, gp = weight_grads(ids, dpre, gp_own, others, inputs)
    mixed, back_sum = unpack_mixed(ids, own_mixed, own_sum, others)

    got = swap(give.reshape(2 * chan, fan), core_bit)
    big, *send, token = core_stage(ids, keep.reshape(2 * chan, fan), got, gp)
    taken = [swap(value, mask_of(y_bits, code)) for code, value in enumerate(send, 1)]
    grads, center, mid_left, mid_right, *strips, token = scatter_grads(
        dpre_full, branch_weight, depth_kernel, rows, cols, token
    )
    big, give = y_stage(ids, big, taken, token)
    strips, give = tie((strips, give))
    from_below = [shift(value, "lat", -1, False) for value in strips[:2]]
    from_above = [shift(value, "lat", 1, False) for value in strips[2:]]
    extra = tap_sums(grads, halos, back_sum)
    center, to_left, to_right = home(center, mid_left, mid_right, from_above, from_below)
    for number, mask in enumerate(bits):
        got = swap(give, mask).astype(f32)
        big = big + got
        if number + 1 < len(bits):
            upper = has(bits[number + 1])
            half = big.shape[0] // 2
            give = jnp.where(upper, big[:half], big[half:]).astype(bf16)
            big = jnp.where(upper, big[half:], big[:half])
        if number == 1:
            give, to_left, to_right = tie((give, to_left, to_right))

    from_left = shift(to_right, "lon", 1)
    from_right = shift(to_left, "lon", -1)
    big, from_left, from_right = tie((big, from_left, from_right))

    sent = jnp.concatenate([big, extra]).astype(bf16)
    for number, mask in enumerate(bits[::-1]):
        got = swap(sent, mask)
        size = got.shape[0] - extra.shape[0]
        extra = extra + got[size:].astype(f32)
        big = sent[:size]
        big = jnp.where(
            has(mask),
            jnp.concatenate([got[:size], big]),
            jnp.concatenate([big, got[:size]]),
        )
        sent = jnp.concatenate([big, extra.astype(bf16)])
    taken = [swap(sent, mask_of(y_bits, code)) for code in (1, 2, 3)]
    half, extra = y_gather(ids, big, extra, taken)
    got = swap(half, core_bit)
    grad_branch, grad_proj, grad_depth, dpooled = last_stage(
        ids, half, got, extra, branch_weight, proj_last, pool_pre, pooled, cell_count
    )
    grad_features = finish(center, from_left, from_right, dpooled)
    return (mixed.reshape(rows, cols, part), grad_features, grad_branch, grad_proj, grad_depth)


def solution(mesh):
    return jax.shard_map(
        per_device,
        mesh=mesh,
        in_specs=(
            P("lat", "lon", "ch"),
            P(None, None, "ch"),
            P(None, "ch", None),
            P(None, "ch", None),
            P("lat", "lon", "ch"),
        ),
        out_specs=(
            P("lat", "lon", "ch"),
            P("lat", "lon", "ch"),
            P(None, "ch", None),
            P(None, "ch", None),
            P(None, None, "ch"),
        ),
        check_vma=False,
    )
```

```python
import math

import jax
import jax.numpy as jnp
from jax import lax
from jax.experimental import pallas as pl
from jax.experimental.pallas import tpu as pltpu
from jax.sharding import PartitionSpec as P

dilations = (6, 12, 18)
margin = 18
lead = 24
f32, bf16 = jnp.float32, jnp.bfloat16
GRID = ("lon", "lat")


MIB = 1024 * 1024


def params(size):
    return pltpu.CompilerParams(vmem_limit_bytes=size * MIB)


def smem():
    return pl.BlockSpec(memory_space=pltpu.SMEM)


def vmem():
    return pl.BlockSpec(memory_space=pltpu.VMEM)


def anywhere():
    return pl.BlockSpec(memory_space=pl.ANY)


def stay(value):
    return pltpu.with_memory_space_constraint(value, pltpu.HBM)


def remote():
    return pl.BlockSpec(memory_space=pltpu.HBM)


def by_lanes(*shape, lanes=128):
    return pl.BlockSpec(shape + (lanes,), lambda i: (0,) * len(shape) + (i,))


def whole(*shape):
    return pl.BlockSpec(shape, lambda i: (0,) * len(shape))


def shaped(dtype, *shape):
    return jax.ShapeDtypeStruct(shape, dtype)


def far(dtype, *shape):
    return pltpu.HBM(shape, dtype)


def cost(flops, moved, hard=0):
    return pl.CostEstimate(flops=flops, bytes_accessed=moved, transcendentals=hard)


def window_of(spacing, step_lon):
    base = lead + step_lon * spacing
    return base // 8, base % 8


def roll_rows(value, shift, count):
    if shift:
        value = pltpu.roll(value, value.shape[0] - shift, 0)
    return value[:count]


def pick(value, scalar):
    return pl.multiple_of(value, scalar)


def split_lanes(line):
    return [line[:, 128 * n : 128 * (n + 1)] for n in range(line.shape[1] // 128)]


def edges_body(tile_ref, right_ref, left_ref, sum_ref, packed):
    rows, cols, chan = tile_ref.shape

    def row_step(row, carry):
        line = tile_ref[row].astype(f32)
        for number, block in enumerate(split_lanes(line)):
            place = slice(margin * number, margin * (number + 1))
            packed[0, row, place, :] = block[:margin]
            packed[1, row, place, :] = roll_rows(block, cols - margin, margin)
        return carry + line

    total = lax.fori_loop(0, rows, row_step, jnp.zeros((cols, chan), f32))
    left_ref[...] = packed[0].astype(bf16)
    right_ref[...] = packed[1].astype(bf16)

    @pl.when(pl.program_id(0) == 0)
    def _():
        sum_ref[...] = jnp.zeros_like(sum_ref)

    sum_ref[...] += jnp.sum(total, axis=0, keepdims=True)


def edges(tile):
    rows, cols, chan = tile.shape
    wide = margin * chan // 128
    block = rows // 3
    by_rows = lambda *shape: pl.BlockSpec((block,) + shape, lambda i: (i, 0, 0))
    return pl.pallas_call(
        edges_body,
        grid=(3,),
        in_specs=[by_rows(cols, chan)],
        out_specs=[by_rows(wide, 128), by_rows(wide, 128), whole(1, chan)],
        out_shape=[
            shaped(bf16, rows, wide, 128),
            shaped(bf16, rows, wide, 128),
            shaped(f32, 1, chan),
        ],
        scratch_shapes=[pltpu.VMEM((2, block, wide, 128), f32)],
        compiler_params=params(8),
        cost_estimate=cost(rows * cols * chan, 2_000_000),
        name="edges",
    )(stay(tile))


def corners_body(id_ref, left_ref, right_ref, sum_ref, *refs):
    chip_ref, cross_ref, out_ref = refs[-3:]
    rows = left_ref.shape[0]
    upper = id_ref[1]
    for number, ref in enumerate((left_ref, right_ref)):
        place = slice(margin * number, margin * (number + 1))
        chip_ref[place] = ref[pl.ds((rows - margin) * (1 - upper), margin)]
        cross_ref[place] = ref[pl.ds((rows - margin) * upper, margin)]
    out_ref[...] = sum_ref[...]


def corners(ids, left, right, running, before):
    _, wide, lanes = left.shape
    return pl.pallas_call(
        corners_body,
        in_specs=[smem()] + [vmem()] * 3 + [anywhere()] * len(before),
        out_specs=[vmem()] * 3,
        out_shape=[shaped(bf16, 2 * margin, wide, lanes)] * 2 + [shaped(f32, *running.shape)],
        compiler_params=params(8),
        cost_estimate=cost(1000, 3_000_000),
        name="corners",
    )(ids, left, right, running, *before)


def fill_extended(ext, halos, blocks, upper):
    tile, left, right, chip, cross, chip_corner, cross_corner = halos
    rows, cols, _ = tile.shape
    off, after = lead - margin, lead + cols

    def put(at, row, middle, before, behind, skip=0):
        before, behind = before[row].astype(f32), behind[row + skip].astype(f32)
        for number, block in blocks:
            place = slice(margin * number, margin * (number + 1))
            line = ext(block, at)
            line[lead:after, :] = middle[row, :, 128 * block : 128 * (block + 1)].astype(f32)
            line[off:lead, :] = before[place]
            line[after : after + margin, :] = behind[place]

    def tile_row(row, carry):
        put(margin + row, row, tile, left, right)
        return carry

    chip_first = (margin + rows) * (1 - upper)
    cross_first = (margin + rows) * upper

    def strip_row(row, carry):
        put(chip_first + row, row, chip, chip_corner, chip_corner, margin)
        put(cross_first + row, row, cross, cross_corner, cross_corner, margin)
        return carry

    lax.fori_loop(0, rows, tile_row, 0)
    lax.fori_loop(0, margin, strip_row, 0)


def halo_specs(halos, lanes):
    return [
        by_lanes(*halo.shape[:2], lanes=lanes) if number in (0, 3, 4) else whole(*halo.shape)
        for number, halo in enumerate(halos)
    ]


def fill_taps(taps, kernel_ref):
    for member in range(3):
        for tap in range(9):
            taps[9 * member + tap] = jnp.broadcast_to(
                kernel_ref[member, tap : tap + 1, :], taps.shape[1:]
            )


def pack(row_ref, value, vector):
    size, part = value.shape
    row_ref[...] = jnp.zeros_like(row_ref)
    for number in range(size // 16):
        row_ref[:, part * number : part * (number + 1)] = value[16 * number : 16 * (number + 1)]
    row_ref[0:1, 640 : 640 + vector.shape[1]] = vector
    return row_ref[...].astype(bf16)


def unpack(message, put, part, size, fan):
    for number in range(size // 16):
        put(number, message[:, part * number : part * (number + 1)])
    return message[0:1, 640 : 640 + fan]


def conv_body(
    id_ref, tile_ref, left_ref, right_ref, top_ref, bottom_ref, up_ref, down_ref, kernel_ref,
    weight_ref, pooled_ref, cot_ref,
    inputs_ref, own_ref, one_ref, two_ref, three_ref, own_cot_ref, own_pool_ref,
    ext, cells, taps, total, pool, rows_ref,
):
    step = pl.program_id(0)
    halos = (tile_ref, left_ref, right_ref, top_ref, bottom_ref, up_ref, down_ref)
    rows, cols, _ = tile_ref.shape
    blocks, lanes = 2, 128
    fan = weight_ref.shape[2]

    @pl.when(step == 0)
    def _():
        total[...] = jnp.zeros_like(total)
        pool[...] = jnp.zeros_like(pool)

    fill_taps(taps, kernel_ref)

    for number in range(2):

        @pl.when(step == number)
        def _(number=number):
            fill_extended(
                lambda block, row: ext.at[block, row],
                halos,
                [(blocks * number + block, block) for block in range(blocks)],
                id_ref[1],
            )

    for block in range(blocks):
        across = slice(lanes * block, lanes * (block + 1))

        def conv_rows(pair, carry, block=block, across=across):
            at = (2 * pair, 2 * pair + 1)
            places = [pl.ds(pl.multiple_of(row * cols, 8), cols) for row in at]
            for row, place in zip(at, places):
                cells[0, place, across] = ext[block, margin + row, lead : lead + cols, :]
            for member, spacing in enumerate(dilations):
                summed = [None, None]
                for step_lon in (-1, 0, 1):
                    group, shift = window_of(spacing, step_lon)
                    count = cols // 8 + (shift != 0)
                    part = [None, None]
                    for step_lat in (-1, 0, 1):
                        tap = taps[9 * member + 3 * (step_lat + 1) + step_lon + 1, :, across]
                        for n in (0, 1):
                            window = ext[
                                block,
                                at[n] + margin + step_lat * spacing,
                                8 * group : 8 * (group + count),
                                :,
                            ].reshape(count, 8, lanes)
                            term = window * tap
                            part[n] = term if part[n] is None else part[n] + term
                    for n in (0, 1):
                        piece = roll_rows(part[n].reshape(8 * count, lanes), shift, cols)
                        summed[n] = piece if summed[n] is None else summed[n] + piece
                for n in (0, 1):
                    cells[member + 1, places[n], across] = summed[n]
            return carry

        lax.fori_loop(0, rows // 2, conv_rows, 0)
    for member in range(4):
        block = cells[member].astype(bf16)
        inputs_ref[member] = block
        total[:, fan * member : fan * (member + 1)] += jnp.dot(
            block, weight_ref[member], preferred_element_type=f32
        )
    pool[...] += jnp.dot(
        jnp.broadcast_to(pooled_ref[...], (8, blocks * lanes)),
        weight_ref[4].astype(f32),
        precision=lax.Precision.HIGHEST,
        preferred_element_type=f32,
    )

    @pl.when(step == pl.num_programs(0) - 1)
    def _():
        size = own_ref.shape[0]
        me = id_ref[0]
        band = rows // 4
        part = cot_ref.shape[2]

        def chunk(ahead):
            return total[pl.ds(pl.multiple_of(lax.rem(me + ahead, 4) * size, 16), size), :]

        def cot_chunk(ahead):
            picked = cot_ref[pl.ds(lax.rem(me + ahead, 4) * band, band)]
            return picked.astype(f32).reshape(size, part)

        own_ref[...] = chunk(0)
        own_cot_ref[...] = cot_chunk(0)
        own_pool_ref[...] = pool[0:1, :]
        for ahead, ref in enumerate((one_ref, two_ref, three_ref), 1):
            ref[:size, :] = chunk(ahead).astype(bf16)
            ref[size:, :] = pack(rows_ref, cot_chunk(ahead), pool[0:1, :])


def conv_forward(ids, halos, kernel, weight, pooled, cotangent):
    rows, cols, chan = halos[0].shape
    tall, wide = rows + 2 * margin, cols + 2 * lead
    fan = weight.shape[2]
    lanes = 256
    size = rows * cols // 4
    cells = rows * cols
    part = cotangent.shape[2]
    return pl.pallas_call(
        conv_body,
        grid=(chan // lanes,),
        in_specs=[smem()]
        + halo_specs(halos, lanes)
        + [
            by_lanes(3, 9, lanes=lanes),
            pl.BlockSpec((5, lanes, fan), lambda i: (0, i, 0)),
            by_lanes(1, lanes=lanes),
            whole(*cotangent.shape),
        ],
        out_specs=[by_lanes(4, cells, lanes=lanes), whole(size, 4 * fan)]
        + [whole(size + 16, 4 * fan)] * 3
        + [whole(size, part), whole(1, fan)],
        out_shape=[
            far(bf16, 4, cells, chan),
            far(f32, size, 4 * fan),
        ]
        + [shaped(bf16, size + 16, 4 * fan)] * 3
        + [shaped(f32, size, part), shaped(f32, 1, fan)],
        scratch_shapes=[
            pltpu.VMEM((lanes // 128, tall, wide, 128), f32),
            pltpu.VMEM((4, cells, lanes), f32),
            pltpu.VMEM((27, 8, lanes), f32),
            pltpu.VMEM((cells, 4 * fan), f32),
            pltpu.VMEM((8, fan), f32),
            pltpu.VMEM((16, 4 * fan), f32),
        ],
        compiler_params=params(58),
        cost_estimate=cost(2 * cells * chan * (4 * fan + 27), 20_000_000),
        name="conv_forward",
    )(ids, stay(halos[0]), *halos[1:], kernel, weight, pooled, cotangent)


def slope(value, sig):
    return sig * (1.0 + value * (1.0 - sig))


def proj_body(
    id_ref, own_ref, one_ref, two_ref, three_ref, own_cot_ref, own_pool_ref,
    weight_own, weight_one, weight_two, weight_three, _, last_ref, dpre_ref, send_one_ref, send_two_ref, send_three_ref,
    grad_own_ref, own_mixed_ref, own_sum_ref, pool_ref,
    pre, grads, weights, pieces, cot, rows_ref,
):
    size, part = own_cot_ref.shape
    fan = 4 * part
    me = id_ref[0]
    pre[...] = own_ref[...]
    pool = own_pool_ref[...]
    pieces[me] = own_cot_ref[...]
    for behind, ref in enumerate((one_ref, two_ref, three_ref), 1):
        pre[...] += ref[:size, :].astype(f32)
        origin = lax.rem(me + 4 - behind, 4)

        def put(number, value, origin=origin):
            pieces[origin, 16 * number : 16 * (number + 1), :] = value

        pool = pool + unpack(ref[size:, :].astype(f32), put, part, size, fan)
    for origin in range(4):
        cot[:, part * origin : part * (origin + 1)] = pieces[origin]
    for behind, ref in enumerate((weight_own, weight_one, weight_two, weight_three)):
        first = pl.multiple_of(lax.rem(me + 4 - behind, 4) * part, 16)
        weights[:, pl.ds(first, part), :] = ref[...]
    last_ref[...] = weights[4]

    pool_ref[...] = pool
    pool = jnp.broadcast_to(pool, (8, fan))
    pool_branch = (pool * jax.nn.sigmoid(pool)).astype(bf16)
    proj = jnp.dot(pool_branch, weights[4], preferred_element_type=f32)[0:1, :]
    for member in range(4):
        value = pre[:, fan * member : fan * (member + 1)]
        branch = (value * jax.nn.sigmoid(value)).astype(bf16)
        proj = proj + jnp.dot(branch, weights[member], preferred_element_type=f32)
    sig = jax.nn.sigmoid(proj)
    mixed = (proj * sig).astype(bf16).astype(f32)
    back = (cot[...] * slope(proj, sig)).astype(bf16)
    back_sum = jnp.sum(back.astype(f32), axis=0, keepdims=True)
    own_sum_ref[...] = back_sum
    for target in range(4):
        pieces[target] = mixed[:, part * target : part * (target + 1)]
    own_mixed_ref[...] = pieces[me]
    for member in range(4):
        lanes = slice(fan * member, fan * (member + 1))
        value = pre[:, lanes]
        sig = jax.nn.sigmoid(value)
        branch = (value * sig).astype(bf16)
        grads[member] = lax.dot_general(
            branch, back, (((0,), (0,)), ((), ())), preferred_element_type=f32
        )
        dbranch = lax.dot_general(
            back, weights[member], (((1,), (1,)), ((), ())), preferred_element_type=f32
        )
        dpre = (dbranch * slope(value, sig)).astype(bf16)
        for ref in (dpre_ref, send_one_ref, send_two_ref, send_three_ref):
            ref[:size, lanes] = dpre
        grad_own_ref[member] = grads[member, pl.ds(pl.multiple_of(me * part, 16), part), :]
        for ahead, ref in enumerate((send_one_ref, send_two_ref, send_three_ref), 1):
            first = pl.multiple_of(lax.rem(me + ahead, 4) * part, 16)
            ref[size + 16 :, lanes] = grads[member, pl.ds(first, part), :].astype(bf16)
    for ahead, ref in enumerate((send_one_ref, send_two_ref, send_three_ref), 1):
        ref[size : size + 16, :] = pack(rows_ref, pieces[lax.rem(me + ahead, 4)], back_sum)


def project(ids, own, others, own_cot, own_pool, weights, before):
    size, wide = own.shape
    fan = wide // 4
    part = fan // 4
    return pl.pallas_call(
        proj_body,
        in_specs=[smem()] + [vmem()] * 10 + [anywhere()],
        out_specs=[vmem()] * 9,
        out_shape=[shaped(bf16, fan, fan), shaped(bf16, size, wide)]
        + [shaped(bf16, size + 16 + part, wide)] * 3
        + [shaped(f32, 4, part, fan)]
        + [shaped(f32, size, part), shaped(f32, 1, fan), shaped(f32, 1, fan)],
        scratch_shapes=[
            pltpu.VMEM((size, wide), f32),
            pltpu.VMEM((4, fan, fan), f32),
            pltpu.VMEM((5, fan, fan), bf16),
            pltpu.VMEM((4, size, part), f32),
            pltpu.VMEM((size, fan), f32),
            pltpu.VMEM((16, wide), f32),
        ],
        compiler_params=params(16),
        cost_estimate=cost(6 * size * wide * fan, 4_000_000, 2 * size * wide),
        name="project",
    )(ids, stay(own), *others, own_cot, own_pool, *weights, before)


def weight_body(
    id_ref, own_ref, gp_ref, own_sum_ref, one_ref, two_ref, three_ref, inputs_ref,
    keep_ref, give_ref, full_ref, total_ref, sum_ref,
):
    size = own_ref.shape[0]
    fan = keep_ref.shape[2]
    me, upper = id_ref[0], id_ref[1]
    others = (one_ref, two_ref, three_ref)
    full_ref[pl.ds(pl.multiple_of(me * size, 16), size), :] = own_ref[...]
    for behind, ref in enumerate(others, 1):
        first = pl.multiple_of(lax.rem(me + 4 - behind, 4) * size, 16)
        full_ref[pl.ds(first, size), :] = ref[:size, :]

    def grad(member):
        lanes = pl.ds(pl.multiple_of(member * fan, 256), fan)
        return lax.dot_general(
            inputs_ref[member],
            full_ref[:, lanes],
            (((0,), (0,)), ((), ())),
            preferred_element_type=f32,
        )

    for number in range(2):
        give_ref[number] = grad(2 * (1 - upper) + number).astype(bf16)
        keep_ref[number] = grad(2 * upper + number)
    for member in range(4):
        value = gp_ref[member]
        for ref in others:
            value = value + ref[size + 16 :, fan * member : fan * (member + 1)].astype(f32)
        total_ref[member] = value
    total = own_sum_ref[...]
    for ref in others:
        total = total + ref[size : size + 16, 640 : 640 + fan].astype(f32)[0:1]
    sum_ref[...] = total


def weight_grads(ids, own, gp_own, own_sum, others, inputs):
    size, wide = own.shape
    fan = wide // 4
    part = fan // 4
    _, cells, chan = inputs.shape
    return pl.pallas_call(
        weight_body,
        in_specs=[smem()] + [vmem()] * 7,
        out_specs=[vmem()] * 5,
        out_shape=[
            shaped(f32, 2, chan, fan),
            shaped(bf16, 2, chan, fan),
            shaped(bf16, cells, wide),
            shaped(f32, 4, part, fan),
            shaped(f32, 1, fan),
        ],
        compiler_params=params(20),
        cost_estimate=cost(2 * cells * chan * wide, 6_000_000),
        name="weight_grads",
    )(ids, own, gp_own, own_sum, *others, stay(inputs))


def unpack_body(id_ref, own_mixed_ref, one_ref, two_ref, three_ref, mixed_ref, pieces):
    size, part = own_mixed_ref.shape
    me = id_ref[0]
    pieces[me] = own_mixed_ref[...]
    for behind, ref in enumerate((one_ref, two_ref, three_ref), 1):
        origin = lax.rem(me + 4 - behind, 4)

        def put(number, value, origin=origin):
            pieces[origin, 16 * number : 16 * (number + 1), :] = value

        unpack(ref[...].astype(f32), put, part, size, 4 * part)
    mixed_ref[...] = pieces[...].astype(bf16)


def unpack_mixed(ids, own_mixed, others):
    size, part = own_mixed.shape
    rows = pl.BlockSpec((16, others[0].shape[1]), lambda i: (size // 16, 0))
    return pl.pallas_call(
        unpack_body,
        grid=(1,),
        in_specs=[smem(), whole(size, part)] + [rows] * 3,
        out_specs=whole(4, size, part),
        out_shape=shaped(bf16, 4, size, part),
        scratch_shapes=[pltpu.VMEM((4, size, part), f32)],
        compiler_params=params(8),
        cost_estimate=cost(100_000, 500_000),
        name="unpack_mixed",
    )(ids, own_mixed, *[stay(value) for value in others])


placed = {}
for _member in range(3):
    for _step in (-1, 0, 1):
        _key = (_member, window_of(dilations[_member], _step)[1])
        placed.setdefault(_key, len(placed))


def shift_rows(shifted, source, rows, cols, lanes):
    def row_step(row, carry):
        place = pl.ds(pl.multiple_of(row * cols, 8), cols)
        for member in range(3):
            value = source(member, place)
            wide = jnp.concatenate([value, jnp.zeros((8, lanes), f32)], axis=0)
            for (owner, shift), number in placed.items():
                if owner != member:
                    continue
                shifted[number, row] = pltpu.roll(wide, shift, 0) if shift else wide
        return carry

    lax.fori_loop(0, rows, row_step, 0)


def scatter_body(
    id_ref, dpre_ref, weight_ref, kernel_ref, _,
    grad_ref, center_ref, left_ref, right_ref, chip_ref, cross_corner, cross_center, token_ref,
    taps, first, grads, shifted, strips,
):
    rows, cols, across_all = center_ref.shape
    lanes = 128
    fan = weight_ref.shape[2]
    wide = cols + 2 * margin
    groups = (cols + 2 * lead) // 8
    off = lead - margin
    fill_taps(taps, kernel_ref)
    token_ref[...] = jnp.zeros_like(token_ref)
    for member in range(4):
        piece = lax.dot_general(
            dpre_ref[:, fan * member : fan * (member + 1)],
            weight_ref[member],
            (((1,), (1,)), ((), ())),
            preferred_element_type=f32,
        )
        if member == 0:
            first[...] = piece
        else:
            piece = piece.astype(bf16)
            grad_ref[member - 1] = piece
            grads[member - 1] = piece.astype(f32)

    for block in range(across_all // lanes):
        across = slice(lanes * block, lanes * (block + 1))
        shift_rows(
            shifted,
            lambda member, place, across=across: grads[member, place, across],
            rows,
            cols,
            lanes,
        )
        for begin in range(0, rows + 2 * margin, 6):
            active = [
                (member, step_lat)
                for member, spacing in enumerate(dilations)
                for step_lat in (-1, 0, 1)
                if margin + step_lat * spacing <= begin < margin + rows + step_lat * spacing
            ]
            inside = margin <= begin < margin + rows

            def ext_rows(at, begin=begin, active=active, inside=inside, across=across):
                sums = [[None] * groups, [None] * groups]
                for n in (0, 1):
                    if inside:
                        value = first[pl.ds(pl.multiple_of((at[n] - margin) * cols, 8), cols), across]
                        for number in range(cols // 8):
                            sums[n][lead // 8 + number] = value[8 * number : 8 * (number + 1)]
                for member, step_lat in active:
                    spacing = dilations[member]
                    for step_lon in (-1, 0, 1):
                        group, shift = window_of(spacing, step_lon)
                        count = cols // 8 + (shift != 0)
                        weight = taps[9 * member + 3 * (step_lat + 1) + step_lon + 1, :, across]
                        for n in (0, 1):
                            grad = shifted[
                                placed[member, shift],
                                at[n] - margin - step_lat * spacing,
                                : 8 * count,
                                :,
                            ]
                            for number in range(count):
                                term = grad[8 * number : 8 * (number + 1)] * weight
                                old = sums[n][group + number]
                                sums[n][group + number] = term if old is None else old + term
                for n in (0, 1):
                    parts = [jnp.zeros((8, lanes), f32) if s is None else s for s in sums[n]]
                    center = jnp.concatenate(parts[lead // 8 : (lead + cols) // 8], axis=0)
                    left = roll_rows(jnp.concatenate(parts[: lead // 8], axis=0), off, margin)
                    right = jnp.concatenate(parts[(lead + cols) // 8 :], axis=0)[:margin]
                    if inside:
                        row = at[n] - margin
                        center_ref[row, :, across] = center.astype(bf16)
                        left_ref[row, :, across] = left.astype(bf16)
                        right_ref[row, :, across] = right.astype(bf16)
                    else:
                        side = int(begin >= margin)
                        row = at[n] - side * (margin + rows)
                        strips[side, row, :cols, across] = center
                        strips[side, row, cols : cols + margin, across] = left
                        strips[side, row, cols + margin : wide, across] = right

            if inside:

                def step_rows(step, carry, begin=begin, ext_rows=ext_rows):
                    ext_rows((begin + 2 * step, begin + 2 * step + 1))
                    return carry

                lax.fori_loop(0, 3, step_rows, 0)
            else:
                for step in range(3):
                    ext_rows((begin + 2 * step, begin + 2 * step + 1))

    for upper in (0, 1):

        @pl.when(id_ref[1] == upper)
        def _(upper=upper):
            for row in range(margin):
                chip_ref[row] = strips[1 - upper, row, :wide, :].astype(bf16)
                cross_corner[row] = strips[upper, row, cols:wide, :].astype(bf16)
                cross_center[row] = strips[upper, row, :cols, :].astype(bf16)


def scatter_grads(ids, dpre, weight, kernel, rows, cols, before):
    cells, wide_fan = dpre.shape
    fan = wide_fan // 4
    chan = weight.shape[1]
    wide = cols + 2 * margin
    lanes = 256
    return pl.pallas_call(
        scatter_body,
        grid=(chan // lanes,),
        in_specs=[
            smem(),
            whole(cells, wide_fan),
            pl.BlockSpec((4, lanes, fan), lambda i: (0, i, 0)),
            by_lanes(3, 9, lanes=lanes),
            anywhere(),
        ],
        out_specs=[
            by_lanes(3, cells, lanes=lanes),
            by_lanes(rows, cols, lanes=lanes),
            by_lanes(rows, margin, lanes=lanes),
            by_lanes(rows, margin, lanes=lanes),
        ]
        + [by_lanes(margin, wide, lanes=lanes)]
        + [by_lanes(margin, 2 * margin, lanes=lanes), by_lanes(margin, cols, lanes=lanes)]
        + [whole(8, 128)],
        out_shape=[
            far(bf16, 3, cells, chan),
            far(bf16, rows, cols, chan),
            far(bf16, rows, margin, chan),
            far(bf16, rows, margin, chan),
        ]
        + [shaped(bf16, margin, wide, chan)]
        + [shaped(bf16, margin, 2 * margin, chan), shaped(bf16, margin, cols, chan)]
        + [shaped(f32, 8, 128)],
        scratch_shapes=[
            pltpu.VMEM((27, 8, lanes), f32),
            pltpu.VMEM((cells, lanes), f32),
            pltpu.VMEM((3, cells, lanes), f32),
            pltpu.VMEM((len(placed), rows, cols + 8, 128), f32),
            pltpu.VMEM((2, margin, cols + 2 * lead - 8, lanes), f32),
        ],
        compiler_params=params(24),
        cost_estimate=cost(2 * cells * chan * (wide_fan + 27), 15_000_000),
        name="scatter_grads",
    )(ids, dpre, weight, kernel, before)


def extend_body(
    id_ref, tile_ref, left_ref, right_ref, top_ref, bottom_ref, up_ref, down_ref, _, ext_ref, token_ref, ext
):
    halos = (tile_ref, left_ref, right_ref, top_ref, bottom_ref, up_ref, down_ref)
    ext[...] = jnp.zeros_like(ext)
    token_ref[...] = jnp.zeros_like(token_ref)
    blocks = ext.shape[0]
    fill_extended(
        lambda block, row: ext.at[block, row],
        halos,
        [(block, block) for block in range(blocks)],
        id_ref[1],
    )

    def copy_rows(row, carry):
        for block in range(blocks):
            ext_ref[row, :, 128 * block : 128 * (block + 1)] = ext[block, row].astype(bf16)
        return carry

    lax.fori_loop(0, ext.shape[1], copy_rows, 0)


def extend(ids, halos, before):
    rows, cols, chan = halos[0].shape
    tall, wide = rows + 2 * margin, cols + 2 * lead + 8
    return pl.pallas_call(
        extend_body,
        in_specs=[smem()] + [vmem()] * 7 + [anywhere()],
        out_specs=[vmem()] * 2,
        out_shape=[far(bf16, tall, wide, chan), shaped(f32, 8, 128)],
        scratch_shapes=[pltpu.VMEM((chan // 128, tall, wide, 128), f32)],
        compiler_params=params(36),
        cost_estimate=cost(1_000_000, 10_000_000),
        name="extend",
    )(ids, *[stay(halo) for halo in halos], before)


def taps_body(grad_ref, ext_ref, sum_ref, tap_ref, ext, grads, shifted):
    step = pl.program_id(0)
    tall, wide, lanes = ext_ref.shape
    rows, cols = tall - 2 * margin, wide - 2 * lead - 8
    per = sum_ref.shape[1] // lanes
    first = 32 * (step // per)
    place = pl.ds(pl.multiple_of(lanes * lax.rem(step, per), 128), lanes)

    def widen_row(row, carry):
        ext[row] = ext_ref[row].astype(f32)
        return carry

    lax.fori_loop(0, tall, widen_row, 0, unroll=4)
    grads[...] = grad_ref[...].astype(f32)
    shift_rows(shifted, lambda member, place: grads[member, place, :], rows, cols, lanes)

    def tap_row(row, carry):
        sums = list(carry)
        for member, spacing in enumerate(dilations):
            for step_lon in (-1, 0, 1):
                group, shift = window_of(spacing, step_lon)
                count = cols // 8 + (shift != 0)
                grad = shifted[placed[member, shift], row, : 8 * count, :].reshape(count, 8, lanes)
                for step_lat in (-1, 0, 1):
                    window = ext[
                        row + margin + step_lat * spacing, 8 * group : 8 * (group + count), :
                    ].reshape(count, 8, lanes)
                    tap = 9 * member + 3 * (step_lat + 1) + step_lon + 1
                    sums[tap] = sums[tap] + jnp.sum(grad * window, axis=0)
        return tuple(sums)

    sums = lax.fori_loop(0, rows, tap_row, (jnp.zeros((8, lanes), f32),) * 27)
    rows_of = [jnp.sum(value, axis=0, keepdims=True) for value in sums]
    rows_of.append(sum_ref[:, place])
    rows_of += [jnp.zeros((1, lanes), f32)] * 4
    tap_ref[pl.ds(pl.multiple_of(first, 32), 32), place] = jnp.concatenate(rows_of, axis=0)


def tap_sums(grads, extended, back_sum):
    tall, wide, chan = extended.shape
    _, cells, _ = grads.shape
    rows, cols = tall - 2 * margin, wide - 2 * lead - 8
    lanes = 128
    shape = (32 * chan // back_sum.shape[1], back_sum.shape[1])
    return pl.pallas_call(
        taps_body,
        grid=(chan // lanes,),
        in_specs=[by_lanes(3, cells), by_lanes(tall, wide), whole(*back_sum.shape)],
        out_specs=whole(*shape),
        out_shape=shaped(f32, *shape),
        scratch_shapes=[
            pltpu.VMEM((tall, wide, lanes), f32),
            pltpu.VMEM((3, cells, lanes), f32),
            pltpu.VMEM((len(placed), rows, cols + 8, lanes), f32),
        ],
        compiler_params=params(20),
        cost_estimate=cost(2 * cells * chan * 27, 15_000_000),
        name="tap_sums",
    )(stay(grads), stay(extended), back_sum)


def home_body(
    id_ref, left_ref, right_ref, chip_ref, corner_ref, left_out, right_out, packed, line
):
    rows, _, _ = left_ref.shape
    wide = chip_ref.shape[1]
    cols = wide - 2 * margin
    shifted = rows - margin

    def one_row(row, refs):
        left, right = left_ref[row].astype(f32), right_ref[row].astype(f32)
        for ref, first, number in refs:
            line[number, cols - ref.shape[1] + 2 * margin :, :] = ref[row - first].astype(f32)
            left = left + line[number, cols : cols + margin, :]
            right = right + line[number, cols + margin :, :]
        for number, (one, two) in enumerate(zip(split_lanes(left), split_lanes(right))):
            place = slice(margin * number, margin * (number + 1))
            packed[0, row, place, :] = one
            packed[1, row, place, :] = two

    for upper in (0, 1):
        pieces = [(chip_ref, shifted * (1 - upper), 0), (corner_ref, shifted * upper, 1)]
        cuts = sorted({0, rows} | {at for _, first, _ in pieces for at in (first, first + margin)})

        @pl.when(id_ref[1] == upper)
        def _(pieces=pieces, cuts=cuts):
            for first, last in zip(cuts, cuts[1:]):
                refs = [piece for piece in pieces if piece[1] <= first < piece[1] + margin]

                def step(number, carry, first=first, refs=refs):
                    one_row(first + number, refs)
                    return carry

                lax.fori_loop(0, last - first, step, 0)

    left_out[...] = packed[0].astype(bf16)
    right_out[...] = packed[1].astype(bf16)


def home(ids, left, right, chip, corner):
    rows, _, chan = left.shape
    wide = margin * chan // 128
    return pl.pallas_call(
        home_body,
        in_specs=[smem()] + [vmem()] * 4,
        out_specs=[vmem()] * 2,
        out_shape=[shaped(bf16, rows, wide, 128)] * 2,
        scratch_shapes=[
            pltpu.VMEM((2, rows, wide, 128), f32),
            pltpu.VMEM((2, chip.shape[1], chan), f32),
        ],
        compiler_params=params(16),
        cost_estimate=cost(rows * margin * chan, 5_000_000),
        name="home",
    )(ids, stay(left), stay(right), chip, corner)


def middle_body(id_ref, center_ref, chip_ref, cross_ref, out_ref):
    rows, cols, _ = center_ref.shape
    shifted = rows - margin
    upper = id_ref[1]

    def copy_row(row, carry):
        out_ref[row] = center_ref[row].astype(f32)
        return carry

    def chip_row(row, carry):
        out_ref[shifted * (1 - upper) + row] += chip_ref[row].astype(f32)[:cols]
        return carry

    def cross_row(row, carry):
        out_ref[shifted * upper + row] += cross_ref[row].astype(f32)
        return carry

    lax.fori_loop(0, rows, copy_row, 0)
    lax.fori_loop(0, margin, chip_row, 0)
    lax.fori_loop(0, margin, cross_row, 0)


def middle(ids, center, chip, cross):
    rows, cols, chan = center.shape
    return pl.pallas_call(
        middle_body,
        grid=(chan // 128,),
        in_specs=[
            smem(),
            by_lanes(rows, cols),
            by_lanes(*chip.shape[:2]),
            by_lanes(*cross.shape[:2]),
        ],
        out_specs=by_lanes(rows, cols),
        out_shape=shaped(f32, rows, cols, chan),
        compiler_params=params(12),
        cost_estimate=cost(rows * cols * chan, 4_000_000),
        name="middle",
    )(ids, stay(center), stay(chip), stay(cross))


def finish_body(center_ref, left_ref, right_ref, pooled_ref, out_ref, pads):
    rows, cols, chan = center_ref.shape
    base = pooled_ref[...]

    @pl.when(pl.program_id(0) == 0)
    def _():
        pads[...] = jnp.zeros_like(pads)

    def row_step(row, carry):
        left, right = left_ref[row].astype(f32), right_ref[row].astype(f32)
        for number in range(chan // 128):
            place = slice(margin * number, margin * (number + 1))
            across = slice(128 * number, 128 * (number + 1))
            pads[0, row, :margin, across] = left[place]
            pads[1, row, cols - margin :, across] = right[place]
        return carry

    lax.fori_loop(0, rows, row_step, 0)

    def add_row(row, carry):
        out_ref[row] = (center_ref[row] + pads[0, row] + pads[1, row] + base).astype(bf16)
        return carry

    lax.fori_loop(0, rows, add_row, 0)


def finish(center, left, right, pooled):
    rows, cols, chan = center.shape
    wide = margin * chan // 128
    block = rows // 3
    by_rows = lambda *shape: pl.BlockSpec((block,) + shape, lambda i: (i, 0, 0))
    return pl.pallas_call(
        finish_body,
        grid=(3,),
        in_specs=[by_rows(cols, chan), by_rows(wide, 128), by_rows(wide, 128), whole(1, chan)],
        out_specs=by_rows(cols, chan),
        out_shape=shaped(bf16, rows, cols, chan),
        scratch_shapes=[pltpu.VMEM((2, block, cols, chan), f32)],
        compiler_params=params(10),
        cost_estimate=cost(rows * cols * chan, 4_000_000),
        name="finish",
    )(center, left, right, pooled)


def core_body(id_ref, keep_ref, got_ref, gp_ref, own_ref, one_ref, two_ref, three_ref, token_ref):
    token_ref[...] = jnp.zeros_like(token_ref)
    fan = keep_ref.shape[1]
    rows = own_ref.shape[0] - gp_ref.shape[1]
    here = id_ref[2]
    for code, ref in enumerate((own_ref, one_ref, two_ref, three_ref)):
        target = here ^ code
        place = pl.ds(pl.multiple_of(target * rows, 16), rows)
        ref[:rows, :] = (keep_ref[place, :] + got_ref[place, :].astype(f32)).astype(ref.dtype)
        ref[rows:, :] = gp_ref[target].astype(ref.dtype)


def core_stage(ids, keep, got, gp):
    rows, fan = keep.shape
    part = gp.shape[1]
    size = rows // 4 + part
    return pl.pallas_call(
        core_body,
        in_specs=[smem()] + [vmem()] * 3,
        out_specs=[vmem()] * 5,
        out_shape=[shaped(f32, size, fan)] + [shaped(bf16, size, fan)] * 3 + [shaped(f32, 8, 128)],
        compiler_params=params(12),
        cost_estimate=cost(rows * fan, 3_000_000),
        name="core_stage",
    )(ids, keep, got, gp)


def y_body(id_ref, own_ref, one_ref, two_ref, three_ref, _, keep_ref, give_ref, total):
    half, _ = keep_ref.shape
    upper = id_ref[3]
    total[...] = (
        own_ref[...] + one_ref[...].astype(f32) + two_ref[...].astype(f32) + three_ref[...].astype(f32)
    )
    keep_ref[...] = total[pl.ds(pl.multiple_of(upper * half, 16), half), :]
    give_ref[...] = total[pl.ds(pl.multiple_of((1 - upper) * half, 16), half), :].astype(bf16)


def y_stage(ids, own, others, before):
    size, fan = own.shape
    return pl.pallas_call(
        y_body,
        in_specs=[smem()] + [vmem()] * 4 + [anywhere()],
        out_specs=[vmem()] * 2,
        out_shape=[shaped(f32, size // 2, fan), shaped(bf16, size // 2, fan)],
        scratch_shapes=[pltpu.VMEM((size, fan), f32)],
        compiler_params=params(8),
        cost_estimate=cost(size * fan, 1_000_000),
        name="y_stage",
    )(ids, own, *others, before)


def gather_body(id_ref, own_ref, extra_ref, one_ref, two_ref, three_ref, out_ref, sum_ref):
    size = own_ref.shape[0]
    here = id_ref[2]
    total = extra_ref[...]
    out_ref[pl.ds(pl.multiple_of(here * size, 16), size), :] = own_ref[...]
    for code, ref in enumerate((one_ref, two_ref, three_ref), 1):
        place = pl.ds(pl.multiple_of((here ^ code) * size, 16), size)
        out_ref[place, :] = ref[:size, :]
        total = total + ref[size:, :].astype(f32)
    out_ref[4 * size :, :] = total.astype(bf16)
    sum_ref[...] = total


def y_gather(ids, own, extra, others):
    size, fan = own.shape
    count = extra.shape[0]
    return pl.pallas_call(
        gather_body,
        in_specs=[smem()] + [vmem()] * 5,
        out_specs=[vmem()] * 2,
        out_shape=[shaped(bf16, 4 * size + count, fan), shaped(f32, count, fan)],
        compiler_params=params(8),
        cost_estimate=cost(size * fan, 2_000_000),
        name="y_gather",
    )(ids, own, extra, *others)


def last_body(
    id_ref, own_ref, got_ref, own_extra_ref, got_extra_ref, weight_ref, proj_ref, pool_ref, pooled_ref,
    branch_ref, grad_proj_ref, depth_ref, dpooled_ref, dpool, column, *, cells,
):
    highest = lax.Precision.HIGHEST
    _, chan, lanes = branch_ref.shape
    part = grad_proj_ref.shape[1]
    fan = 4 * part
    scale = 1.0 / math.sqrt(cells)
    me, upper = id_ref[0], id_ref[1]
    step = pl.program_id(0)
    size = chan // 2 + part
    top = lax.broadcasted_iota(jnp.int32, (8, lanes), 0) == 0

    def outer(column_of, row_of):
        return lax.dot_general(
            column_of,
            jnp.where(top, row_of, 0.0),
            (((0,), (0,)), ((), ())),
            precision=highest,
            preferred_element_type=f32,
        )

    @pl.when(step == 0)
    def _():
        extra = own_extra_ref[...] + got_extra_ref[4 * size :, :].astype(f32)
        for number in range(chan // fan):
            for tap in range(27):
                row = 32 * number + tap
                depth_ref[tap // 9, tap % 9 : tap % 9 + 1, fan * number : fan * (number + 1)] = (
                    extra[row : row + 1] * scale
                )
        back_sum = jnp.broadcast_to(extra[27:28], (8, fan))
        pool = jnp.broadcast_to(pool_ref[...], (8, fan))
        sig = jax.nn.sigmoid(pool)
        full = slope(pool, sig) * lax.dot_general(
            back_sum,
            proj_ref[...].astype(f32),
            (((1,), (1,)), ((), ())),
            precision=highest,
            preferred_element_type=f32,
        )
        dpooled = lax.dot_general(
            full,
            weight_ref[0].astype(f32),
            (((1,), (1,)), ((), ())),
            precision=highest,
            preferred_element_type=f32,
        )
        dpooled_ref[...] = dpooled[0:1] * (1.0 / cells)
        pool_branch = (pool * sig).astype(bf16).astype(f32)
        for number in range(fan // lanes):
            dpool[0, number] = full[:, lanes * number : lanes * (number + 1)]
            dpool[1, number] = back_sum[:, lanes * number : lanes * (number + 1)]
        for origin in range(4):
            column[origin] = pool_branch[:, part * origin : part * (origin + 1)]

    for number in range(4):
        first = size * number
        rows = slice(chan // 2 * (number % 2), chan // 2 * (number % 2 + 1))
        for ref, half in ((own_ref, upper), (got_ref, 1 - upper)):
            branch_ref[2 * half + number // 2, rows, :] = (
                ref[first : first + chan // 2, :].astype(f32) * scale
            )
        both = own_ref[first + chan // 2 : first + size, :].astype(f32)
        both = both + got_ref[first + chan // 2 : first + size, :].astype(f32)
        grad_proj_ref[number] = both * scale
    branch_ref[4] = outer(jnp.broadcast_to(pooled_ref[...], (8, chan)), dpool[0, step]) * scale
    grad_proj_ref[4] = outer(column[me], dpool[1, step]) * scale


def last_stage(ids, own, got, extra, weight, proj, pool_pre, pooled, cells):
    _, chan, fan = weight.shape
    part = fan // 4
    return pl.pallas_call(
        lambda *refs: last_body(*refs, cells=cells),
        grid=(fan // 128,),
        in_specs=[
            smem(),
            by_lanes(own.shape[0]),
            by_lanes(got.shape[0]),
            whole(*extra.shape),
            whole(*got.shape),
            pl.BlockSpec((1, chan, fan), lambda i: (4, 0, 0)),
            whole(*proj.shape),
            whole(*pool_pre.shape),
            whole(*pooled.shape),
        ],
        out_specs=[by_lanes(5, chan), by_lanes(5, part), whole(3, 9, chan), whole(1, chan)],
        out_shape=[
            shaped(f32, 5, chan, fan),
            shaped(f32, 5, part, fan),
            shaped(f32, 3, 9, chan),
            shaped(f32, 1, chan),
        ],
        scratch_shapes=[
            pltpu.VMEM((2, fan // 128, 8, 128), f32),
            pltpu.VMEM((4, 8, part), f32),
        ],
        compiler_params=params(18),
        cost_estimate=cost(8 * chan * fan, 5_000_000),
        name="last_stage",
    )(ids, own, got, extra, got, weight, proj, pool_pre, pooled)


def shift(value, axis, ahead, closed=True):
    count = lax.axis_size(axis)
    pairs = [
        (i, (i + ahead) % count) for i in range(count) if closed or 0 <= i + ahead < count
    ]
    return lax.ppermute(value, axis, pairs)


def to_partner(value):
    count = lax.axis_size("lat")
    return lax.ppermute(value, "lat", [(i, i ^ 1) for i in range(count)])


def to_other_chip(value):
    count = lax.axis_size("lat")
    pairs = [(i, i + 1) for i in range(1, count - 1, 2)]
    return lax.ppermute(value, "lat", pairs + [(j, i) for i, j in pairs])


def place_in_grid():
    return lax.axis_index("lon") * lax.axis_size("lat") + lax.axis_index("lat")


def swap(value, mask):
    count = lax.axis_size("lon") * lax.axis_size("lat")
    return lax.ppermute(value, GRID, [(i, i ^ mask) for i in range(count)])


def has(mask):
    return (place_in_grid() & mask) != 0


def number_in(bits):
    return sum(has(bit).astype(jnp.int32) << at for at, bit in enumerate(bits))


def mask_of(bits, code):
    return sum(bit for at, bit in enumerate(bits) if (code >> at) & 1)


def grid_sum(value):
    mask = 1
    while mask < lax.axis_size("lon") * lax.axis_size("lat"):
        value = value + swap(value, mask)
        mask *= 2
    return value


core_bit, y_bits = 1, (4, 2)


def z_bits():
    bits, mask = [], 8
    while mask < lax.axis_size("lon") * lax.axis_size("lat"):
        bits.append(mask)
        mask *= 2
    return bits


def per_device(features, depth_kernel, branch_weight, proj_weight, cotangent):
    rows, cols, chan = features.shape
    fan = branch_weight.shape[2]
    part = proj_weight.shape[1]
    cell_count = rows * cols * lax.axis_size("lat") * lax.axis_size("lon")
    me = lax.axis_index("ch")
    flag = lambda mask: has(mask).astype(jnp.int32)
    ids = jnp.stack(
        [me.astype(jnp.int32), flag(core_bit), number_in(y_bits), flag(z_bits()[0])]
    )
    tie = lax.optimization_barrier

    to_right, to_left, colsum = edges(features)
    left = shift(to_right, "lon", 1)
    right = shift(to_left, "lon", -1)

    proj_others = [shift(proj_weight, "ch", d) for d in (1, 2, 3)]
    pooled = colsum.reshape(chan // 128, 128)
    bits = z_bits()
    pooled = pooled + swap(pooled, core_bit)
    pooled, tile = tie((pooled, features))
    rest = rows - margin
    first = jnp.where(has(core_bit), rest, 0)
    cross = to_other_chip(lax.dynamic_slice_in_dim(tile, first, margin))
    chip = to_partner(lax.dynamic_slice_in_dim(tile, rest - first, margin))
    for mask in [bits[0], bits[2], y_bits[0]]:
        pooled = pooled + swap(pooled, mask)
    chip_corner, cross_corner, pooled = corners(ids, left, right, pooled, (chip, cross))
    cross_corner = to_other_chip(cross_corner)
    chip_corner = to_partner(chip_corner)
    for mask in [bits[1], y_bits[1]]:
        pooled = pooled + swap(pooled, mask)
    pooled = pooled.reshape(1, chan) / cell_count

    halos = (features, left, right, chip, cross, chip_corner, cross_corner)
    inputs, own, *ahead, own_cot, own_pool = conv_forward(
        ids, halos, depth_kernel, branch_weight, pooled, cotangent
    )
    ahead, proj_others = tie((ahead, proj_others))
    extended, token = extend(ids, halos, own_pool)
    others = [shift(value, "ch", d) for d, value in enumerate(ahead, 1)]
    proj_last, dpre, *sent, gp_own, own_mixed, own_sum, pool_pre = project(
        ids, own, others, own_cot, own_pool, [proj_weight, *proj_others], token
    )
    others = [shift(value, "ch", d) for d, value in enumerate(sent, 1)]
    keep, give, dpre_full, gp, back_sum = weight_grads(ids, dpre, gp_own, own_sum, others, inputs)
    mixed = unpack_mixed(ids, own_mixed, others)

    got = swap(give.reshape(2 * chan, fan), core_bit)
    big, *send, token = core_stage(ids, keep.reshape(2 * chan, fan), got, gp)
    taken = [swap(value, mask_of(y_bits, code)) for code, value in enumerate(send, 1)]
    grads, center, mid_left, mid_right, *strips, token = scatter_grads(
        ids, dpre_full, branch_weight, depth_kernel, rows, cols, token
    )
    big, give = y_stage(ids, big, taken, token)
    strips, give = tie((strips, give))
    strips = [to_partner(strips[0])] + [to_other_chip(value) for value in strips[1:]]
    extra = tap_sums(grads, extended, back_sum)
    to_left, to_right = home(ids, mid_left, mid_right, *strips[:2])
    center = middle(ids, center, strips[0], strips[2])
    for number, mask in enumerate(bits):
        got = swap(give, mask).astype(f32)
        big = big + got
        if number + 1 < len(bits):
            upper = has(bits[number + 1])
            half = big.shape[0] // 2
            give = jnp.where(upper, big[:half], big[half:]).astype(bf16)
            big = jnp.where(upper, big[half:], big[:half])
        if number == 1:
            give, to_left, to_right = tie((give, to_left, to_right))

    from_left = shift(to_right, "lon", 1)
    from_right = shift(to_left, "lon", -1)
    big, from_left, from_right, center, mixed = tie((big, from_left, from_right, center, mixed))

    sent = jnp.concatenate([big, extra]).astype(bf16)
    for number, mask in enumerate(bits[::-1]):
        got = swap(sent, mask)
        size = got.shape[0] - extra.shape[0]
        extra = extra + got[size:].astype(f32)
        big = sent[:size]
        big = jnp.where(
            has(mask),
            jnp.concatenate([got[:size], big]),
            jnp.concatenate([big, got[:size]]),
        )
        sent = jnp.concatenate([big, extra.astype(bf16)])
    taken = [swap(sent, mask_of(y_bits, code)) for code in (1, 2, 3)]
    half, extra = y_gather(ids, big, extra, taken)
    got = swap(half, core_bit)
    grad_branch, grad_proj, grad_depth, dpooled = last_stage(
        ids, half, got, extra, branch_weight, proj_last, pool_pre, pooled, cell_count
    )
    grad_features = finish(center, from_left, from_right, dpooled)
    return (mixed.reshape(rows, cols, part), grad_features, grad_branch, grad_proj, grad_depth)


def solution(mesh):
    return jax.shard_map(
        per_device,
        mesh=mesh,
        in_specs=(
            P("lat", "lon", "ch"),
            P(None, None, "ch"),
            P(None, "ch", None),
            P(None, "ch", None),
            P("lat", "lon", "ch"),
        ),
        out_specs=(
            P("lat", "lon", "ch"),
            P("lat", "lon", "ch"),
            P(None, "ch", None),
            P(None, "ch", None),
            P(None, None, "ch"),
        ),
        check_vma=False,
    )
```

```python
import math

import jax
import jax.numpy as jnp
from jax import lax
from jax.experimental import pallas as pl
from jax.experimental.pallas import tpu as pltpu
from jax.sharding import PartitionSpec as P

dilations = (6, 12, 18)
margin = 18
lead = 24
f32, bf16 = jnp.float32, jnp.bfloat16
GRID = ("lon", "lat")


MIB = 1024 * 1024


def params(size):
    return pltpu.CompilerParams(vmem_limit_bytes=size * MIB)


def smem():
    return pl.BlockSpec(memory_space=pltpu.SMEM)


def vmem():
    return pl.BlockSpec(memory_space=pltpu.VMEM)


def anywhere():
    return pl.BlockSpec(memory_space=pl.ANY)


def stay(value):
    return pltpu.with_memory_space_constraint(value, pltpu.HBM)


def remote():
    return pl.BlockSpec(memory_space=pltpu.HBM)


def by_lanes(*shape, lanes=128):
    return pl.BlockSpec(shape + (lanes,), lambda i: (0,) * len(shape) + (i,))


def whole(*shape):
    return pl.BlockSpec(shape, lambda i: (0,) * len(shape))


def shaped(dtype, *shape):
    return jax.ShapeDtypeStruct(shape, dtype)


def far(dtype, *shape):
    return pltpu.HBM(shape, dtype)


def cost(flops, moved, hard=0):
    return pl.CostEstimate(flops=flops, bytes_accessed=moved, transcendentals=hard)


def window_of(spacing, step_lon):
    base = lead + step_lon * spacing
    return base // 8, base % 8


def roll_rows(value, shift, count):
    if shift:
        value = pltpu.roll(value, value.shape[0] - shift, 0)
    return value[:count]


def pick(value, scalar):
    return pl.multiple_of(value, scalar)


def split_lanes(line):
    return [line[:, 128 * n : 128 * (n + 1)] for n in range(line.shape[1] // 128)]


main = margin // 8 * 8
rest = margin - main


def put_packed(packed, number, main_value, rest_value, blocks):
    packed[main * number : main * (number + 1), :] = main_value
    first = main * blocks + rest * number
    packed[first : first + rest, :] = rest_value


def packed_main(line, number):
    return line[main * number : main * (number + 1)]


def packed_rest(line, number, blocks):
    first = main * blocks + rest * number
    return line[first : first + rest]


def edges_body(tile_ref, right_ref, left_ref, sum_ref, packed):
    rows, cols, chan = tile_ref.shape

    def row_step(row, carry):
        line = tile_ref[row].astype(f32)
        blocks = split_lanes(line)
        for number, block in enumerate(blocks):
            put_packed(packed.at[0, row], number, block[:main], block[main:margin], len(blocks))
            put_packed(
                packed.at[1, row],
                number,
                block[cols - main :],
                roll_rows(block, cols - margin, rest),
                len(blocks),
            )
        return carry + line

    total = lax.fori_loop(0, rows, row_step, jnp.zeros((cols, chan), f32), unroll=2)
    left_ref[...] = packed[0].astype(bf16)
    right_ref[...] = packed[1].astype(bf16)

    @pl.when(pl.program_id(0) == 0)
    def _():
        sum_ref[...] = jnp.zeros_like(sum_ref)

    sum_ref[...] += jnp.sum(total, axis=0, keepdims=True)


def edges(tile):
    rows, cols, chan = tile.shape
    wide = margin * chan // 128
    block = rows // 3
    by_rows = lambda *shape: pl.BlockSpec((block,) + shape, lambda i: (i, 0, 0))
    return pl.pallas_call(
        edges_body,
        grid=(3,),
        in_specs=[by_rows(cols, chan)],
        out_specs=[by_rows(wide, 128), by_rows(wide, 128), whole(1, chan)],
        out_shape=[
            shaped(bf16, rows, wide, 128),
            shaped(bf16, rows, wide, 128),
            shaped(f32, 1, chan),
        ],
        scratch_shapes=[pltpu.VMEM((2, block, wide, 128), f32)],
        compiler_params=params(8),
        cost_estimate=cost(rows * cols * chan, 2_000_000),
        name="edges",
    )(stay(tile))


def corners_body(id_ref, left_ref, right_ref, sum_ref, *refs):
    chip_ref, cross_ref, out_ref = refs[-3:]
    rows = left_ref.shape[0]
    upper = id_ref[1]
    for number, ref in enumerate((left_ref, right_ref)):
        place = slice(margin * number, margin * (number + 1))
        chip_ref[place] = ref[pl.ds((rows - margin) * (1 - upper), margin)]
        cross_ref[place] = ref[pl.ds((rows - margin) * upper, margin)]
    out_ref[...] = sum_ref[...]


def corners(ids, left, right, running, before):
    _, wide, lanes = left.shape
    return pl.pallas_call(
        corners_body,
        in_specs=[smem()] + [vmem()] * 3 + [anywhere()] * len(before),
        out_specs=[vmem()] * 3,
        out_shape=[shaped(bf16, 2 * margin, wide, lanes)] * 2 + [shaped(f32, *running.shape)],
        compiler_params=params(8),
        cost_estimate=cost(1000, 3_000_000),
        name="corners",
    )(ids, left, right, running, *before)


def fill_extended(ext, halos, blocks, upper):
    tile, left, right, chip, cross, chip_corner, cross_corner = halos
    rows, cols, _ = tile.shape
    off, after = lead - margin, lead + cols

    def put(at, row, middle, before, behind, skip=0):
        before, behind = before[row].astype(f32), behind[row + skip].astype(f32)
        count = before.shape[0] // margin
        for number, block in blocks:
            line = ext(block, at)
            line[lead:after, :] = middle[row, :, 128 * block : 128 * (block + 1)].astype(f32)
            line[lead - main : lead, :] = packed_main(before, number)
            line[off : off + rest, :] = packed_rest(before, number, count)
            line[after : after + main, :] = packed_main(behind, number)
            line[after + main : after + margin, :] = packed_rest(behind, number, count)

    def tile_row(row, carry):
        put(margin + row, row, tile, left, right)
        return carry

    chip_first = (margin + rows) * (1 - upper)
    cross_first = (margin + rows) * upper

    def strip_row(row, carry):
        put(chip_first + row, row, chip, chip_corner, chip_corner, margin)
        put(cross_first + row, row, cross, cross_corner, cross_corner, margin)
        return carry

    lax.fori_loop(0, rows, tile_row, 0, unroll=2)
    lax.fori_loop(0, margin, strip_row, 0, unroll=2)


def halo_specs(halos, lanes):
    return [
        by_lanes(*halo.shape[:2], lanes=lanes) if number in (0, 3, 4) else whole(*halo.shape)
        for number, halo in enumerate(halos)
    ]


def fill_taps(taps, kernel_ref):
    for member in range(3):
        for tap in range(9):
            taps[9 * member + tap] = jnp.broadcast_to(
                kernel_ref[member, tap : tap + 1, :], taps.shape[1:]
            )


def pack(row_ref, value, vector):
    size, part = value.shape
    row_ref[...] = jnp.zeros_like(row_ref)
    for number in range(size // 16):
        row_ref[:, part * number : part * (number + 1)] = value[16 * number : 16 * (number + 1)]
    row_ref[0:1, 640 : 640 + vector.shape[1]] = vector
    return row_ref[...].astype(bf16)


def unpack(message, put, part, size, fan):
    for number in range(size // 16):
        put(number, message[:, part * number : part * (number + 1)])
    return message[0:1, 640 : 640 + fan]


def conv_body(
    id_ref, tile_ref, left_ref, right_ref, top_ref, bottom_ref, up_ref, down_ref, kernel_ref,
    weight_ref, pooled_ref, cot_ref,
    inputs_ref, own_ref, one_ref, two_ref, three_ref, own_cot_ref, own_pool_ref,
    ext, cells, taps, total, pool, rows_ref,
):
    step = pl.program_id(0)
    halos = (tile_ref, left_ref, right_ref, top_ref, bottom_ref, up_ref, down_ref)
    rows, cols, _ = tile_ref.shape
    blocks, lanes = 2, 128
    fan = weight_ref.shape[2]

    @pl.when(step == 0)
    def _():
        total[...] = jnp.zeros_like(total)
        pool[...] = jnp.zeros_like(pool)

    fill_taps(taps, kernel_ref)

    for number in range(2):

        @pl.when(step == number)
        def _(number=number):
            fill_extended(
                lambda block, row: ext.at[block, row],
                halos,
                [(blocks * number + block, block) for block in range(blocks)],
                id_ref[1],
            )

    for block in range(blocks):
        across = slice(lanes * block, lanes * (block + 1))

        def conv_rows(pair, carry, block=block, across=across):
            at = (2 * pair, 2 * pair + 1)
            places = [pl.ds(pl.multiple_of(row * cols, 8), cols) for row in at]
            for row, place in zip(at, places):
                cells[0, place, across] = ext[block, margin + row, lead : lead + cols, :]
            for member, spacing in enumerate(dilations):
                summed = [None, None]
                for step_lon in (-1, 0, 1):
                    group, shift = window_of(spacing, step_lon)
                    count = cols // 8 + (shift != 0)
                    part = [None, None]
                    for step_lat in (-1, 0, 1):
                        tap = taps[9 * member + 3 * (step_lat + 1) + step_lon + 1, :, across]
                        for n in (0, 1):
                            window = ext[
                                block,
                                at[n] + margin + step_lat * spacing,
                                8 * group : 8 * (group + count),
                                :,
                            ].reshape(count, 8, lanes)
                            term = window * tap
                            part[n] = term if part[n] is None else part[n] + term
                    for n in (0, 1):
                        piece = roll_rows(part[n].reshape(8 * count, lanes), shift, cols)
                        summed[n] = piece if summed[n] is None else summed[n] + piece
                for n in (0, 1):
                    cells[member + 1, places[n], across] = summed[n]
            return carry

        lax.fori_loop(0, rows // 2, conv_rows, 0, unroll=2)
    for member in range(4):
        block = cells[member].astype(bf16)
        inputs_ref[member] = block
        total[:, fan * member : fan * (member + 1)] += jnp.dot(
            block, weight_ref[member], preferred_element_type=f32
        )
    pool[...] += jnp.dot(
        jnp.broadcast_to(pooled_ref[...], (8, blocks * lanes)),
        weight_ref[4].astype(f32),
        precision=lax.Precision.HIGHEST,
        preferred_element_type=f32,
    )

    @pl.when(step == pl.num_programs(0) - 1)
    def _():
        size = own_ref.shape[0]
        me = id_ref[0]
        band = rows // 4
        part = cot_ref.shape[2]

        def chunk(ahead):
            return total[pl.ds(pl.multiple_of(lax.rem(me + ahead, 4) * size, 16), size), :]

        def cot_chunk(ahead):
            picked = cot_ref[pl.ds(lax.rem(me + ahead, 4) * band, band)]
            return picked.astype(f32).reshape(size, part)

        own_ref[...] = chunk(0)
        own_cot_ref[...] = cot_chunk(0)
        own_pool_ref[...] = pool[0:1, :]
        for ahead, ref in enumerate((one_ref, two_ref, three_ref), 1):
            ref[:size, :] = chunk(ahead).astype(bf16)
            ref[size:, :] = pack(rows_ref, cot_chunk(ahead), pool[0:1, :])


def conv_forward(ids, halos, kernel, weight, pooled, cotangent):
    rows, cols, chan = halos[0].shape
    tall, wide = rows + 2 * margin, cols + 2 * lead
    fan = weight.shape[2]
    lanes = 256
    size = rows * cols // 4
    cells = rows * cols
    part = cotangent.shape[2]
    return pl.pallas_call(
        conv_body,
        grid=(chan // lanes,),
        in_specs=[smem()]
        + halo_specs(halos, lanes)
        + [
            by_lanes(3, 9, lanes=lanes),
            pl.BlockSpec((5, lanes, fan), lambda i: (0, i, 0)),
            by_lanes(1, lanes=lanes),
            whole(*cotangent.shape),
        ],
        out_specs=[by_lanes(4, cells, lanes=lanes), whole(size, 4 * fan)]
        + [whole(size + 16, 4 * fan)] * 3
        + [whole(size, part), whole(1, fan)],
        out_shape=[
            far(bf16, 4, cells, chan),
            far(f32, size, 4 * fan),
        ]
        + [shaped(bf16, size + 16, 4 * fan)] * 3
        + [shaped(f32, size, part), shaped(f32, 1, fan)],
        scratch_shapes=[
            pltpu.VMEM((lanes // 128, tall, wide, 128), f32),
            pltpu.VMEM((4, cells, lanes), f32),
            pltpu.VMEM((27, 8, lanes), f32),
            pltpu.VMEM((cells, 4 * fan), f32),
            pltpu.VMEM((8, fan), f32),
            pltpu.VMEM((16, 4 * fan), f32),
        ],
        compiler_params=params(58),
        cost_estimate=cost(2 * cells * chan * (4 * fan + 27), 20_000_000),
        name="conv_forward",
    )(ids, stay(halos[0]), *halos[1:], kernel, weight, pooled, cotangent)


def slope(value, sig):
    return sig * (1.0 + value * (1.0 - sig))


def proj_body(
    id_ref, own_ref, one_ref, two_ref, three_ref, own_cot_ref, own_pool_ref,
    weight_own, weight_one, weight_two, weight_three, _, last_ref, dpre_ref, send_one_ref, send_two_ref, send_three_ref,
    grad_own_ref, own_mixed_ref, own_sum_ref, pool_ref,
    pre, grads, weights, pieces, cot, rows_ref,
):
    size, part = own_cot_ref.shape
    fan = 4 * part
    me = id_ref[0]
    pre[...] = own_ref[...]
    pool = own_pool_ref[...]
    pieces[me] = own_cot_ref[...]
    for behind, ref in enumerate((one_ref, two_ref, three_ref), 1):
        pre[...] += ref[:size, :].astype(f32)
        origin = lax.rem(me + 4 - behind, 4)

        def put(number, value, origin=origin):
            pieces[origin, 16 * number : 16 * (number + 1), :] = value

        pool = pool + unpack(ref[size:, :].astype(f32), put, part, size, fan)
    for origin in range(4):
        cot[:, part * origin : part * (origin + 1)] = pieces[origin]
    for behind, ref in enumerate((weight_own, weight_one, weight_two, weight_three)):
        first = pl.multiple_of(lax.rem(me + 4 - behind, 4) * part, 16)
        weights[:, pl.ds(first, part), :] = ref[...]
    last_ref[...] = weights[4]

    pool_ref[...] = pool
    pool = jnp.broadcast_to(pool, (8, fan))
    pool_branch = (pool * jax.nn.sigmoid(pool)).astype(bf16)
    proj = jnp.dot(pool_branch, weights[4], preferred_element_type=f32)[0:1, :]
    for member in range(4):
        value = pre[:, fan * member : fan * (member + 1)]
        branch = (value * jax.nn.sigmoid(value)).astype(bf16)
        proj = proj + jnp.dot(branch, weights[member], preferred_element_type=f32)
    sig = jax.nn.sigmoid(proj)
    mixed = (proj * sig).astype(bf16).astype(f32)
    back = (cot[...] * slope(proj, sig)).astype(bf16)
    back_sum = jnp.sum(back.astype(f32), axis=0, keepdims=True)
    own_sum_ref[...] = back_sum
    for target in range(4):
        pieces[target] = mixed[:, part * target : part * (target + 1)]
    own_mixed_ref[...] = pieces[me]
    for member in range(4):
        lanes = slice(fan * member, fan * (member + 1))
        value = pre[:, lanes]
        sig = jax.nn.sigmoid(value)
        branch = (value * sig).astype(bf16)
        grads[member] = lax.dot_general(
            branch, back, (((0,), (0,)), ((), ())), preferred_element_type=f32
        )
        dbranch = lax.dot_general(
            back, weights[member], (((1,), (1,)), ((), ())), preferred_element_type=f32
        )
        dpre = (dbranch * slope(value, sig)).astype(bf16)
        for ref in (dpre_ref, send_one_ref, send_two_ref, send_three_ref):
            ref[:size, lanes] = dpre
        grad_own_ref[member] = grads[member, pl.ds(pl.multiple_of(me * part, 16), part), :]
        for ahead, ref in enumerate((send_one_ref, send_two_ref, send_three_ref), 1):
            first = pl.multiple_of(lax.rem(me + ahead, 4) * part, 16)
            ref[size + 16 :, lanes] = grads[member, pl.ds(first, part), :].astype(bf16)
    for ahead, ref in enumerate((send_one_ref, send_two_ref, send_three_ref), 1):
        ref[size : size + 16, :] = pack(rows_ref, pieces[lax.rem(me + ahead, 4)], back_sum)


def project(ids, own, others, own_cot, own_pool, weights, before):
    size, wide = own.shape
    fan = wide // 4
    part = fan // 4
    return pl.pallas_call(
        proj_body,
        in_specs=[smem()] + [vmem()] * 10 + [anywhere()],
        out_specs=[vmem()] * 9,
        out_shape=[shaped(bf16, fan, fan), shaped(bf16, size, wide)]
        + [shaped(bf16, size + 16 + part, wide)] * 3
        + [shaped(f32, 4, part, fan)]
        + [shaped(f32, size, part), shaped(f32, 1, fan), shaped(f32, 1, fan)],
        scratch_shapes=[
            pltpu.VMEM((size, wide), f32),
            pltpu.VMEM((4, fan, fan), f32),
            pltpu.VMEM((5, fan, fan), bf16),
            pltpu.VMEM((4, size, part), f32),
            pltpu.VMEM((size, fan), f32),
            pltpu.VMEM((16, wide), f32),
        ],
        compiler_params=params(16),
        cost_estimate=cost(6 * size * wide * fan, 4_000_000, 2 * size * wide),
        name="project",
    )(ids, stay(own), *others, own_cot, own_pool, *weights, before)


def weight_body(
    id_ref, own_ref, gp_ref, own_sum_ref, one_ref, two_ref, three_ref, inputs_ref,
    keep_ref, give_ref, full_ref, total_ref, sum_ref,
):
    size = own_ref.shape[0]
    fan = keep_ref.shape[2]
    me, upper = id_ref[0], id_ref[1]
    others = (one_ref, two_ref, three_ref)
    full_ref[pl.ds(pl.multiple_of(me * size, 16), size), :] = own_ref[...]
    for behind, ref in enumerate(others, 1):
        first = pl.multiple_of(lax.rem(me + 4 - behind, 4) * size, 16)
        full_ref[pl.ds(first, size), :] = ref[:size, :]

    def grad(member):
        lanes = pl.ds(pl.multiple_of(member * fan, 256), fan)
        return lax.dot_general(
            inputs_ref[member],
            full_ref[:, lanes],
            (((0,), (0,)), ((), ())),
            preferred_element_type=f32,
        )

    for number in range(2):
        give_ref[number] = grad(2 * (1 - upper) + number).astype(bf16)
        keep_ref[number] = grad(2 * upper + number)
    for member in range(4):
        value = gp_ref[member]
        for ref in others:
            value = value + ref[size + 16 :, fan * member : fan * (member + 1)].astype(f32)
        total_ref[member] = value
    total = own_sum_ref[...]
    for ref in others:
        total = total + ref[size : size + 16, 640 : 640 + fan].astype(f32)[0:1]
    sum_ref[...] = total


def weight_grads(ids, own, gp_own, own_sum, others, inputs):
    size, wide = own.shape
    fan = wide // 4
    part = fan // 4
    _, cells, chan = inputs.shape
    return pl.pallas_call(
        weight_body,
        in_specs=[smem()] + [vmem()] * 7,
        out_specs=[vmem()] * 5,
        out_shape=[
            shaped(f32, 2, chan, fan),
            shaped(bf16, 2, chan, fan),
            shaped(bf16, cells, wide),
            shaped(f32, 4, part, fan),
            shaped(f32, 1, fan),
        ],
        compiler_params=params(20),
        cost_estimate=cost(2 * cells * chan * wide, 6_000_000),
        name="weight_grads",
    )(ids, own, gp_own, own_sum, *others, stay(inputs))


def unpack_body(id_ref, own_mixed_ref, one_ref, two_ref, three_ref, mixed_ref, pieces):
    size, part = own_mixed_ref.shape
    me = id_ref[0]
    pieces[me] = own_mixed_ref[...]
    for behind, ref in enumerate((one_ref, two_ref, three_ref), 1):
        origin = lax.rem(me + 4 - behind, 4)

        def put(number, value, origin=origin):
            pieces[origin, 16 * number : 16 * (number + 1), :] = value

        unpack(ref[...].astype(f32), put, part, size, 4 * part)
    mixed_ref[...] = pieces[...].astype(bf16)


def unpack_mixed(ids, own_mixed, others):
    size, part = own_mixed.shape
    rows = pl.BlockSpec((16, others[0].shape[1]), lambda i: (size // 16, 0))
    return pl.pallas_call(
        unpack_body,
        grid=(1,),
        in_specs=[smem(), whole(size, part)] + [rows] * 3,
        out_specs=whole(4, size, part),
        out_shape=shaped(bf16, 4, size, part),
        scratch_shapes=[pltpu.VMEM((4, size, part), f32)],
        compiler_params=params(8),
        cost_estimate=cost(100_000, 500_000),
        name="unpack_mixed",
    )(ids, own_mixed, *[stay(value) for value in others])


placed = {}
for _member in range(3):
    for _step in (-1, 0, 1):
        _key = (_member, window_of(dilations[_member], _step)[1])
        placed.setdefault(_key, len(placed))


def shift_rows(shifted, source, rows, cols, lanes):
    def row_step(row, carry):
        place = pl.ds(pl.multiple_of(row * cols, 8), cols)
        for member in range(3):
            value = source(member, place)
            wide = jnp.concatenate([value, jnp.zeros((8, lanes), f32)], axis=0)
            for (owner, shift), number in placed.items():
                if owner != member:
                    continue
                shifted[number, row] = pltpu.roll(wide, shift, 0) if shift else wide
        return carry

    lax.fori_loop(0, rows, row_step, 0, unroll=4)


def scatter_body(
    id_ref, dpre_ref, weight_ref, kernel_ref, _,
    grad_ref, center_ref, left_ref, right_ref, chip_ref, cross_corner, cross_center, token_ref,
    taps, first, grads, shifted, strips,
):
    rows, cols, across_all = center_ref.shape
    lanes = 128
    fan = weight_ref.shape[2]
    wide = cols + 2 * margin
    groups = (cols + 2 * lead) // 8
    off = lead - margin
    fill_taps(taps, kernel_ref)
    token_ref[...] = jnp.zeros_like(token_ref)
    for member in range(4):
        piece = lax.dot_general(
            dpre_ref[:, fan * member : fan * (member + 1)],
            weight_ref[member],
            (((1,), (1,)), ((), ())),
            preferred_element_type=f32,
        )
        if member == 0:
            first[...] = piece
        else:
            piece = piece.astype(bf16)
            grad_ref[member - 1] = piece
            grads[member - 1] = piece.astype(f32)

    for block in range(across_all // lanes):
        across = slice(lanes * block, lanes * (block + 1))
        shift_rows(
            shifted,
            lambda member, place, across=across: grads[member, place, across],
            rows,
            cols,
            lanes,
        )
        for begin in range(0, rows + 2 * margin, 6):
            active = [
                (member, step_lat)
                for member, spacing in enumerate(dilations)
                for step_lat in (-1, 0, 1)
                if margin + step_lat * spacing <= begin < margin + rows + step_lat * spacing
            ]
            inside = margin <= begin < margin + rows

            def ext_rows(at, begin=begin, active=active, inside=inside, across=across):
                sums = [[None] * groups, [None] * groups]
                for n in (0, 1):
                    if inside:
                        value = first[pl.ds(pl.multiple_of((at[n] - margin) * cols, 8), cols), across]
                        for number in range(cols // 8):
                            sums[n][lead // 8 + number] = value[8 * number : 8 * (number + 1)]
                for member, step_lat in active:
                    spacing = dilations[member]
                    for step_lon in (-1, 0, 1):
                        group, shift = window_of(spacing, step_lon)
                        count = cols // 8 + (shift != 0)
                        weight = taps[9 * member + 3 * (step_lat + 1) + step_lon + 1, :, across]
                        for n in (0, 1):
                            grad = shifted[
                                placed[member, shift],
                                at[n] - margin - step_lat * spacing,
                                : 8 * count,
                                :,
                            ]
                            for number in range(count):
                                term = grad[8 * number : 8 * (number + 1)] * weight
                                old = sums[n][group + number]
                                sums[n][group + number] = term if old is None else old + term
                for n in (0, 1):
                    parts = [jnp.zeros((8, lanes), f32) if s is None else s for s in sums[n]]
                    center = jnp.concatenate(parts[lead // 8 : (lead + cols) // 8], axis=0)
                    left = jnp.concatenate(
                        parts[(lead - main) // 8 : lead // 8] + [roll_rows(parts[off // 8], off % 8, 8)],
                        axis=0,
                    )[:margin]
                    right = jnp.concatenate(parts[(lead + cols) // 8 :], axis=0)[:margin]
                    if inside:
                        row = at[n] - margin
                        center_ref[row, :, across] = center.astype(bf16)
                        left_ref[row, :, across] = left.astype(bf16)
                        right_ref[row, :, across] = right.astype(bf16)
                    else:
                        side = int(begin >= margin)
                        row = at[n] - side * (margin + rows)
                        strips[side, row, :cols, across] = center
                        strips[side, row, cols : cols + margin, across] = left
                        strips[side, row, cols + margin : wide, across] = right

            if inside:

                def step_rows(step, carry, begin=begin, ext_rows=ext_rows):
                    ext_rows((begin + 2 * step, begin + 2 * step + 1))
                    return carry

                lax.fori_loop(0, 3, step_rows, 0, unroll=3)
            else:
                for step in range(3):
                    ext_rows((begin + 2 * step, begin + 2 * step + 1))

    for upper in (0, 1):

        @pl.when(id_ref[1] == upper)
        def _(upper=upper):
            for row in range(margin):
                chip_ref[row] = strips[1 - upper, row, :wide, :].astype(bf16)
                cross_corner[row] = strips[upper, row, cols:wide, :].astype(bf16)
                cross_center[row] = strips[upper, row, :cols, :].astype(bf16)


def scatter_grads(ids, dpre, weight, kernel, rows, cols, before):
    cells, wide_fan = dpre.shape
    fan = wide_fan // 4
    chan = weight.shape[1]
    wide = cols + 2 * margin
    lanes = 256
    return pl.pallas_call(
        scatter_body,
        grid=(chan // lanes,),
        in_specs=[
            smem(),
            whole(cells, wide_fan),
            pl.BlockSpec((4, lanes, fan), lambda i: (0, i, 0)),
            by_lanes(3, 9, lanes=lanes),
            anywhere(),
        ],
        out_specs=[
            by_lanes(3, cells, lanes=lanes),
            by_lanes(rows, cols, lanes=lanes),
            by_lanes(rows, margin, lanes=lanes),
            by_lanes(rows, margin, lanes=lanes),
        ]
        + [by_lanes(margin, wide, lanes=lanes)]
        + [by_lanes(margin, 2 * margin, lanes=lanes), by_lanes(margin, cols, lanes=lanes)]
        + [whole(8, 128)],
        out_shape=[
            far(bf16, 3, cells, chan),
            far(bf16, rows, cols, chan),
            far(bf16, rows, margin, chan),
            far(bf16, rows, margin, chan),
        ]
        + [shaped(bf16, margin, wide, chan)]
        + [shaped(bf16, margin, 2 * margin, chan), shaped(bf16, margin, cols, chan)]
        + [shaped(f32, 8, 128)],
        scratch_shapes=[
            pltpu.VMEM((27, 8, lanes), f32),
            pltpu.VMEM((cells, lanes), f32),
            pltpu.VMEM((3, cells, lanes), f32),
            pltpu.VMEM((len(placed), rows, cols + 8, 128), f32),
            pltpu.VMEM((2, margin, cols + 2 * lead - 8, lanes), f32),
        ],
        compiler_params=params(24),
        cost_estimate=cost(2 * cells * chan * (wide_fan + 27), 15_000_000),
        name="scatter_grads",
    )(ids, dpre, weight, kernel, before)


def extend_body(
    id_ref, tile_ref, left_ref, right_ref, top_ref, bottom_ref, up_ref, down_ref, _, ext_ref, token_ref, ext
):
    halos = (tile_ref, left_ref, right_ref, top_ref, bottom_ref, up_ref, down_ref)
    ext[...] = jnp.zeros_like(ext)
    token_ref[...] = jnp.zeros_like(token_ref)
    blocks = ext.shape[0]
    fill_extended(
        lambda block, row: ext.at[block, row],
        halos,
        [(block, block) for block in range(blocks)],
        id_ref[1],
    )

    def copy_rows(row, carry):
        for block in range(blocks):
            ext_ref[row, :, 128 * block : 128 * (block + 1)] = ext[block, row].astype(bf16)
        return carry

    lax.fori_loop(0, ext.shape[1], copy_rows, 0, unroll=4)


def extend(ids, halos, before):
    rows, cols, chan = halos[0].shape
    tall, wide = rows + 2 * margin, cols + 2 * lead + 8
    return pl.pallas_call(
        extend_body,
        in_specs=[smem()] + [vmem()] * 7 + [anywhere()],
        out_specs=[vmem()] * 2,
        out_shape=[far(bf16, tall, wide, chan), shaped(f32, 8, 128)],
        scratch_shapes=[pltpu.VMEM((chan // 128, tall, wide, 128), f32)],
        compiler_params=params(36),
        cost_estimate=cost(1_000_000, 10_000_000),
        name="extend",
    )(ids, *[stay(halo) for halo in halos], before)


def taps_body(grad_ref, ext_ref, sum_ref, tap_ref, ext, grads, shifted):
    step = pl.program_id(0)
    tall, wide, lanes = ext_ref.shape
    rows, cols = tall - 2 * margin, wide - 2 * lead - 8
    per = sum_ref.shape[1] // lanes
    first = 32 * (step // per)
    place = pl.ds(pl.multiple_of(lanes * lax.rem(step, per), 128), lanes)

    def widen_row(row, carry):
        ext[row] = ext_ref[row].astype(f32)
        return carry

    lax.fori_loop(0, tall, widen_row, 0, unroll=4)
    grads[...] = grad_ref[...].astype(f32)
    shift_rows(shifted, lambda member, place: grads[member, place, :], rows, cols, lanes)

    def tap_row(row, carry):
        sums = list(carry)
        for member, spacing in enumerate(dilations):
            for step_lon in (-1, 0, 1):
                group, shift = window_of(spacing, step_lon)
                count = cols // 8 + (shift != 0)
                grad = shifted[placed[member, shift], row, : 8 * count, :].reshape(count, 8, lanes)
                for step_lat in (-1, 0, 1):
                    window = ext[
                        row + margin + step_lat * spacing, 8 * group : 8 * (group + count), :
                    ].reshape(count, 8, lanes)
                    tap = 9 * member + 3 * (step_lat + 1) + step_lon + 1
                    sums[tap] = sums[tap] + jnp.sum(grad * window, axis=0)
        return tuple(sums)

    sums = lax.fori_loop(0, rows, tap_row, (jnp.zeros((8, lanes), f32),) * 27, unroll=2)
    rows_of = [jnp.sum(value, axis=0, keepdims=True) for value in sums]
    rows_of.append(sum_ref[:, place])
    rows_of += [jnp.zeros((1, lanes), f32)] * 4
    tap_ref[pl.ds(pl.multiple_of(first, 32), 32), place] = jnp.concatenate(rows_of, axis=0)


def tap_sums(grads, extended, back_sum):
    tall, wide, chan = extended.shape
    _, cells, _ = grads.shape
    rows, cols = tall - 2 * margin, wide - 2 * lead - 8
    lanes = 128
    shape = (32 * chan // back_sum.shape[1], back_sum.shape[1])
    return pl.pallas_call(
        taps_body,
        grid=(chan // lanes,),
        in_specs=[by_lanes(3, cells), by_lanes(tall, wide), whole(*back_sum.shape)],
        out_specs=whole(*shape),
        out_shape=shaped(f32, *shape),
        scratch_shapes=[
            pltpu.VMEM((tall, wide, lanes), f32),
            pltpu.VMEM((3, cells, lanes), f32),
            pltpu.VMEM((len(placed), rows, cols + 8, lanes), f32),
        ],
        compiler_params=params(20),
        cost_estimate=cost(2 * cells * chan * 27, 15_000_000),
        name="tap_sums",
    )(stay(grads), stay(extended), back_sum)


def home_body(
    id_ref, left_ref, right_ref, chip_ref, corner_ref, left_out, right_out, packed, line
):
    rows, _, _ = left_ref.shape
    wide = chip_ref.shape[1]
    cols = wide - 2 * margin
    shifted = rows - margin

    def one_row(row, refs):
        left, right = left_ref[row].astype(f32), right_ref[row].astype(f32)
        for ref, first, number in refs:
            line[number, cols - ref.shape[1] + 2 * margin :, :] = ref[row - first].astype(f32)
            left = left + line[number, cols : cols + margin, :]
            right = right + line[number, cols + margin :, :]
        pairs = list(zip(split_lanes(left), split_lanes(right)))
        for number, pair in enumerate(pairs):
            for side, value in enumerate(pair):
                put_packed(packed.at[side, row], number, value[:main], value[main:], len(pairs))

    for upper in (0, 1):
        pieces = [(chip_ref, shifted * (1 - upper), 0), (corner_ref, shifted * upper, 1)]
        cuts = sorted({0, rows} | {at for _, first, _ in pieces for at in (first, first + margin)})

        @pl.when(id_ref[1] == upper)
        def _(pieces=pieces, cuts=cuts):
            for first, last in zip(cuts, cuts[1:]):
                refs = [piece for piece in pieces if piece[1] <= first < piece[1] + margin]

                def step(number, carry, first=first, refs=refs):
                    one_row(first + number, refs)
                    return carry

                lax.fori_loop(0, last - first, step, 0, unroll=3)

    left_out[...] = packed[0].astype(bf16)
    right_out[...] = packed[1].astype(bf16)


def home(ids, left, right, chip, corner):
    rows, _, chan = left.shape
    wide = margin * chan // 128
    return pl.pallas_call(
        home_body,
        in_specs=[smem()] + [vmem()] * 4,
        out_specs=[vmem()] * 2,
        out_shape=[shaped(bf16, rows, wide, 128)] * 2,
        scratch_shapes=[
            pltpu.VMEM((2, rows, wide, 128), f32),
            pltpu.VMEM((2, chip.shape[1], chan), f32),
        ],
        compiler_params=params(16),
        cost_estimate=cost(rows * margin * chan, 5_000_000),
        name="home",
    )(ids, stay(left), stay(right), chip, corner)


def middle_body(id_ref, center_ref, chip_ref, cross_ref, out_ref):
    rows, cols, _ = center_ref.shape
    shifted = rows - margin
    out_ref[...] = center_ref[...].astype(f32)
    for upper in (0, 1):
        chip_first, cross_first = shifted * (1 - upper), shifted * upper

        @pl.when(id_ref[1] == upper)
        def _(chip_first=chip_first, cross_first=cross_first):
            for row in range(margin):
                out_ref[chip_first + row] += chip_ref[row].astype(f32)[:cols]
            for row in range(margin):
                out_ref[cross_first + row] += cross_ref[row].astype(f32)


def middle(ids, center, chip, cross):
    rows, cols, chan = center.shape
    return pl.pallas_call(
        middle_body,
        grid=(chan // 128,),
        in_specs=[
            smem(),
            by_lanes(rows, cols),
            by_lanes(*chip.shape[:2]),
            by_lanes(*cross.shape[:2]),
        ],
        out_specs=by_lanes(rows, cols),
        out_shape=shaped(f32, rows, cols, chan),
        compiler_params=params(12),
        cost_estimate=cost(rows * cols * chan, 4_000_000),
        name="middle",
    )(ids, stay(center), stay(chip), stay(cross))


def finish_body(center_ref, left_ref, right_ref, pooled_ref, out_ref, pads):
    rows, cols, chan = center_ref.shape
    base = pooled_ref[...]

    @pl.when(pl.program_id(0) == 0)
    def _():
        pads[...] = jnp.zeros_like(pads)

    def row_step(row, carry):
        left, right = left_ref[row].astype(f32), right_ref[row].astype(f32)
        count = chan // 128
        for number in range(count):
            across = slice(128 * number, 128 * (number + 1))
            pads[0, row, :main, across] = packed_main(left, number)
            pads[0, row, main:margin, across] = packed_rest(left, number, count)
            pads[1, row, cols - main :, across] = packed_main(right, number)
            pads[1, row, cols - margin : cols - main, across] = packed_rest(right, number, count)
        return carry

    lax.fori_loop(0, rows, row_step, 0, unroll=4)

    def add_row(row, carry):
        out_ref[row] = (center_ref[row] + pads[0, row] + pads[1, row] + base).astype(bf16)
        return carry

    lax.fori_loop(0, rows, add_row, 0, unroll=4)


def finish(center, left, right, pooled):
    rows, cols, chan = center.shape
    wide = margin * chan // 128
    block = rows // 3
    by_rows = lambda *shape: pl.BlockSpec((block,) + shape, lambda i: (i, 0, 0))
    return pl.pallas_call(
        finish_body,
        grid=(3,),
        in_specs=[by_rows(cols, chan), by_rows(wide, 128), by_rows(wide, 128), whole(1, chan)],
        out_specs=by_rows(cols, chan),
        out_shape=shaped(bf16, rows, cols, chan),
        scratch_shapes=[pltpu.VMEM((2, block, cols, chan), f32)],
        compiler_params=params(10),
        cost_estimate=cost(rows * cols * chan, 4_000_000),
        name="finish",
    )(center, left, right, pooled)


def core_body(id_ref, keep_ref, got_ref, gp_ref, own_ref, one_ref, two_ref, three_ref, token_ref):
    token_ref[...] = jnp.zeros_like(token_ref)
    fan = keep_ref.shape[1]
    rows = own_ref.shape[0] - gp_ref.shape[1]
    here = id_ref[2]
    for code, ref in enumerate((own_ref, one_ref, two_ref, three_ref)):
        target = here ^ code
        place = pl.ds(pl.multiple_of(target * rows, 16), rows)
        ref[:rows, :] = (keep_ref[place, :] + got_ref[place, :].astype(f32)).astype(ref.dtype)
        ref[rows:, :] = gp_ref[target].astype(ref.dtype)


def core_stage(ids, keep, got, gp):
    rows, fan = keep.shape
    part = gp.shape[1]
    size = rows // 4 + part
    return pl.pallas_call(
        core_body,
        in_specs=[smem()] + [vmem()] * 3,
        out_specs=[vmem()] * 5,
        out_shape=[shaped(f32, size, fan)] + [shaped(bf16, size, fan)] * 3 + [shaped(f32, 8, 128)],
        compiler_params=params(12),
        cost_estimate=cost(rows * fan, 3_000_000),
        name="core_stage",
    )(ids, keep, got, gp)


def y_body(id_ref, own_ref, one_ref, two_ref, three_ref, _, keep_ref, give_ref, total):
    half, _ = keep_ref.shape
    upper = id_ref[3]
    total[...] = (
        own_ref[...] + one_ref[...].astype(f32) + two_ref[...].astype(f32) + three_ref[...].astype(f32)
    )
    keep_ref[...] = total[pl.ds(pl.multiple_of(upper * half, 16), half), :]
    give_ref[...] = total[pl.ds(pl.multiple_of((1 - upper) * half, 16), half), :].astype(bf16)


def y_stage(ids, own, others, before):
    size, fan = own.shape
    return pl.pallas_call(
        y_body,
        in_specs=[smem()] + [vmem()] * 4 + [anywhere()],
        out_specs=[vmem()] * 2,
        out_shape=[shaped(f32, size // 2, fan), shaped(bf16, size // 2, fan)],
        scratch_shapes=[pltpu.VMEM((size, fan), f32)],
        compiler_params=params(8),
        cost_estimate=cost(size * fan, 1_000_000),
        name="y_stage",
    )(ids, own, *others, before)


def gather_body(id_ref, own_ref, extra_ref, one_ref, two_ref, three_ref, out_ref, sum_ref):
    size = own_ref.shape[0]
    here = id_ref[2]
    total = extra_ref[...]
    out_ref[pl.ds(pl.multiple_of(here * size, 16), size), :] = own_ref[...]
    for code, ref in enumerate((one_ref, two_ref, three_ref), 1):
        place = pl.ds(pl.multiple_of((here ^ code) * size, 16), size)
        out_ref[place, :] = ref[:size, :]
        total = total + ref[size:, :].astype(f32)
    out_ref[4 * size :, :] = total.astype(bf16)
    sum_ref[...] = total


def y_gather(ids, own, extra, others):
    size, fan = own.shape
    count = extra.shape[0]
    return pl.pallas_call(
        gather_body,
        in_specs=[smem()] + [vmem()] * 5,
        out_specs=[vmem()] * 2,
        out_shape=[shaped(bf16, 4 * size + count, fan), shaped(f32, count, fan)],
        compiler_params=params(8),
        cost_estimate=cost(size * fan, 2_000_000),
        name="y_gather",
    )(ids, own, extra, *others)


def last_body(
    id_ref, own_ref, got_ref, own_extra_ref, got_extra_ref, weight_ref, proj_ref, pool_ref, pooled_ref,
    branch_ref, grad_proj_ref, depth_ref, dpooled_ref, dpool, column, *, cells,
):
    highest = lax.Precision.HIGHEST
    _, chan, lanes = branch_ref.shape
    part = grad_proj_ref.shape[1]
    fan = 4 * part
    scale = 1.0 / math.sqrt(cells)
    me, upper = id_ref[0], id_ref[1]
    step = pl.program_id(0)
    size = chan // 2 + part
    top = lax.broadcasted_iota(jnp.int32, (8, lanes), 0) == 0

    def outer(column_of, row_of):
        return lax.dot_general(
            column_of,
            jnp.where(top, row_of, 0.0),
            (((0,), (0,)), ((), ())),
            precision=highest,
            preferred_element_type=f32,
        )

    @pl.when(step == 0)
    def _():
        extra = own_extra_ref[...] + got_extra_ref[4 * size :, :].astype(f32)
        for number in range(chan // fan):
            for tap in range(27):
                row = 32 * number + tap
                depth_ref[tap // 9, tap % 9 : tap % 9 + 1, fan * number : fan * (number + 1)] = (
                    extra[row : row + 1] * scale
                )
        back_sum = jnp.broadcast_to(extra[27:28], (8, fan))
        pool = jnp.broadcast_to(pool_ref[...], (8, fan))
        sig = jax.nn.sigmoid(pool)
        full = slope(pool, sig) * lax.dot_general(
            back_sum,
            proj_ref[...].astype(f32),
            (((1,), (1,)), ((), ())),
            precision=highest,
            preferred_element_type=f32,
        )
        dpooled = lax.dot_general(
            full,
            weight_ref[0].astype(f32),
            (((1,), (1,)), ((), ())),
            precision=highest,
            preferred_element_type=f32,
        )
        dpooled_ref[...] = dpooled[0:1] * (1.0 / cells)
        pool_branch = (pool * sig).astype(bf16).astype(f32)
        for number in range(fan // lanes):
            dpool[0, number] = full[:, lanes * number : lanes * (number + 1)]
            dpool[1, number] = back_sum[:, lanes * number : lanes * (number + 1)]
        for origin in range(4):
            column[origin] = pool_branch[:, part * origin : part * (origin + 1)]

    for number in range(4):
        first = size * number
        rows = slice(chan // 2 * (number % 2), chan // 2 * (number % 2 + 1))
        for ref, half in ((own_ref, upper), (got_ref, 1 - upper)):
            branch_ref[2 * half + number // 2, rows, :] = (
                ref[first : first + chan // 2, :].astype(f32) * scale
            )
        both = own_ref[first + chan // 2 : first + size, :].astype(f32)
        both = both + got_ref[first + chan // 2 : first + size, :].astype(f32)
        grad_proj_ref[number] = both * scale
    branch_ref[4] = outer(jnp.broadcast_to(pooled_ref[...], (8, chan)), dpool[0, step]) * scale
    grad_proj_ref[4] = outer(column[me], dpool[1, step]) * scale


def last_stage(ids, own, got, extra, weight, proj, pool_pre, pooled, cells):
    _, chan, fan = weight.shape
    part = fan // 4
    return pl.pallas_call(
        lambda *refs: last_body(*refs, cells=cells),
        grid=(fan // 128,),
        in_specs=[
            smem(),
            by_lanes(own.shape[0]),
            by_lanes(got.shape[0]),
            whole(*extra.shape),
            whole(*got.shape),
            pl.BlockSpec((1, chan, fan), lambda i: (4, 0, 0)),
            whole(*proj.shape),
            whole(*pool_pre.shape),
            whole(*pooled.shape),
        ],
        out_specs=[by_lanes(5, chan), by_lanes(5, part), whole(3, 9, chan), whole(1, chan)],
        out_shape=[
            shaped(f32, 5, chan, fan),
            shaped(f32, 5, part, fan),
            shaped(f32, 3, 9, chan),
            shaped(f32, 1, chan),
        ],
        scratch_shapes=[
            pltpu.VMEM((2, fan // 128, 8, 128), f32),
            pltpu.VMEM((4, 8, part), f32),
        ],
        compiler_params=params(18),
        cost_estimate=cost(8 * chan * fan, 5_000_000),
        name="last_stage",
    )(ids, own, got, extra, got, weight, proj, pool_pre, pooled)


def shift(value, axis, ahead, closed=True):
    count = lax.axis_size(axis)
    pairs = [
        (i, (i + ahead) % count) for i in range(count) if closed or 0 <= i + ahead < count
    ]
    return lax.ppermute(value, axis, pairs)


def to_partner(value):
    count = lax.axis_size("lat")
    return lax.ppermute(value, "lat", [(i, i ^ 1) for i in range(count)])


def to_other_chip(value):
    count = lax.axis_size("lat")
    pairs = [(i, i + 1) for i in range(1, count - 1, 2)]
    return lax.ppermute(value, "lat", pairs + [(j, i) for i, j in pairs])


def place_in_grid():
    return lax.axis_index("lon") * lax.axis_size("lat") + lax.axis_index("lat")


def swap(value, mask):
    count = lax.axis_size("lon") * lax.axis_size("lat")
    return lax.ppermute(value, GRID, [(i, i ^ mask) for i in range(count)])


def has(mask):
    return (place_in_grid() & mask) != 0


def number_in(bits):
    return sum(has(bit).astype(jnp.int32) << at for at, bit in enumerate(bits))


def mask_of(bits, code):
    return sum(bit for at, bit in enumerate(bits) if (code >> at) & 1)


def grid_sum(value):
    mask = 1
    while mask < lax.axis_size("lon") * lax.axis_size("lat"):
        value = value + swap(value, mask)
        mask *= 2
    return value


core_bit, y_bits = 1, (4, 2)


def z_bits():
    bits, mask = [], 8
    while mask < lax.axis_size("lon") * lax.axis_size("lat"):
        bits.append(mask)
        mask *= 2
    return bits


def per_device(features, depth_kernel, branch_weight, proj_weight, cotangent):
    rows, cols, chan = features.shape
    fan = branch_weight.shape[2]
    part = proj_weight.shape[1]
    cell_count = rows * cols * lax.axis_size("lat") * lax.axis_size("lon")
    me = lax.axis_index("ch")
    flag = lambda mask: has(mask).astype(jnp.int32)
    ids = jnp.stack(
        [me.astype(jnp.int32), flag(core_bit), number_in(y_bits), flag(z_bits()[0])]
    )
    tie = lax.optimization_barrier

    to_right, to_left, colsum = edges(features)
    left = shift(to_right, "lon", 1)
    right = shift(to_left, "lon", -1)

    proj_others = [shift(proj_weight, "ch", d) for d in (1, 2, 3)]
    pooled = colsum.reshape(chan // 128, 128)
    bits = z_bits()
    pooled = pooled + swap(pooled, core_bit)
    pooled, tile = tie((pooled, features))
    rest = rows - margin
    first = jnp.where(has(core_bit), rest, 0)
    cross = to_other_chip(lax.dynamic_slice_in_dim(tile, first, margin))
    chip = to_partner(lax.dynamic_slice_in_dim(tile, rest - first, margin))
    for mask in [bits[0], bits[2], y_bits[0]]:
        pooled = pooled + swap(pooled, mask)
    chip_corner, cross_corner, pooled = corners(ids, left, right, pooled, (chip, cross))
    cross_corner = to_other_chip(cross_corner)
    chip_corner = to_partner(chip_corner)
    for mask in [bits[1], y_bits[1]]:
        pooled = pooled + swap(pooled, mask)
    pooled = pooled.reshape(1, chan) / cell_count

    halos = (features, left, right, chip, cross, chip_corner, cross_corner)
    inputs, own, *ahead, own_cot, own_pool = conv_forward(
        ids, halos, depth_kernel, branch_weight, pooled, cotangent
    )
    ahead, proj_others = tie((ahead, proj_others))
    extended, token = extend(ids, halos, own_pool)
    others = [shift(value, "ch", d) for d, value in enumerate(ahead, 1)]
    proj_last, dpre, *sent, gp_own, own_mixed, own_sum, pool_pre = project(
        ids, own, others, own_cot, own_pool, [proj_weight, *proj_others], token
    )
    others = [shift(value, "ch", d) for d, value in enumerate(sent, 1)]
    keep, give, dpre_full, gp, back_sum = weight_grads(ids, dpre, gp_own, own_sum, others, inputs)
    mixed = unpack_mixed(ids, own_mixed, others)

    got = swap(give.reshape(2 * chan, fan), core_bit)
    big, *send, token = core_stage(ids, keep.reshape(2 * chan, fan), got, gp)
    taken = [swap(value, mask_of(y_bits, code)) for code, value in enumerate(send, 1)]
    grads, center, mid_left, mid_right, *strips, token = scatter_grads(
        ids, dpre_full, branch_weight, depth_kernel, rows, cols, token
    )
    big, give = y_stage(ids, big, taken, token)
    strips, give = tie((strips, give))
    strips = [to_partner(strips[0])] + [to_other_chip(value) for value in strips[1:]]
    extra = tap_sums(grads, extended, back_sum)
    to_left, to_right = home(ids, mid_left, mid_right, *strips[:2])
    center = middle(ids, center, strips[0], strips[2])
    for number, mask in enumerate(bits):
        got = swap(give, mask).astype(f32)
        big = big + got
        if number + 1 < len(bits):
            upper = has(bits[number + 1])
            half = big.shape[0] // 2
            give = jnp.where(upper, big[:half], big[half:]).astype(bf16)
            big = jnp.where(upper, big[half:], big[:half])
        if number == 1:
            give, to_left, to_right = tie((give, to_left, to_right))

    from_left = shift(to_right, "lon", 1)
    from_right = shift(to_left, "lon", -1)
    big, from_left, from_right, center, mixed = tie((big, from_left, from_right, center, mixed))

    sent = jnp.concatenate([big, extra]).astype(bf16)
    for number, mask in enumerate(bits[::-1]):
        got = swap(sent, mask)
        size = got.shape[0] - extra.shape[0]
        extra = extra + got[size:].astype(f32)
        big = sent[:size]
        big = jnp.where(
            has(mask),
            jnp.concatenate([got[:size], big]),
            jnp.concatenate([big, got[:size]]),
        )
        sent = jnp.concatenate([big, extra.astype(bf16)])
    taken = [swap(sent, mask_of(y_bits, code)) for code in (1, 2, 3)]
    half, extra = y_gather(ids, big, extra, taken)
    got = swap(half, core_bit)
    grad_branch, grad_proj, grad_depth, dpooled = last_stage(
        ids, half, got, extra, branch_weight, proj_last, pool_pre, pooled, cell_count
    )
    grad_features = finish(center, from_left, from_right, dpooled)
    return (mixed.reshape(rows, cols, part), grad_features, grad_branch, grad_proj, grad_depth)


def solution(mesh):
    return jax.shard_map(
        per_device,
        mesh=mesh,
        in_specs=(
            P("lat", "lon", "ch"),
            P(None, None, "ch"),
            P(None, "ch", None),
            P(None, "ch", None),
            P("lat", "lon", "ch"),
        ),
        out_specs=(
            P("lat", "lon", "ch"),
            P("lat", "lon", "ch"),
            P(None, "ch", None),
            P(None, "ch", None),
            P(None, None, "ch"),
        ),
        check_vma=False,
    )
```

```python
import math

import jax
import jax.numpy as jnp
from jax import lax
from jax.experimental import pallas as pl
from jax.experimental.pallas import tpu as pltpu
from jax.sharding import PartitionSpec as P

dilations = (6, 12, 18)
margin = 18
lead = 24
f32, bf16 = jnp.float32, jnp.bfloat16
GRID = ("lon", "lat")


MIB = 1024 * 1024


def params(size):
    return pltpu.CompilerParams(vmem_limit_bytes=size * MIB)


def smem():
    return pl.BlockSpec(memory_space=pltpu.SMEM)


def vmem():
    return pl.BlockSpec(memory_space=pltpu.VMEM)


def anywhere():
    return pl.BlockSpec(memory_space=pl.ANY)


def stay(value):
    return pltpu.with_memory_space_constraint(value, pltpu.HBM)


def remote():
    return pl.BlockSpec(memory_space=pltpu.HBM)


def by_lanes(*shape, lanes=128):
    return pl.BlockSpec(shape + (lanes,), lambda i: (0,) * len(shape) + (i,))


def whole(*shape):
    return pl.BlockSpec(shape, lambda i: (0,) * len(shape))


def shaped(dtype, *shape):
    return jax.ShapeDtypeStruct(shape, dtype)


def far(dtype, *shape):
    return pltpu.HBM(shape, dtype)


def cost(flops, moved, hard=0):
    return pl.CostEstimate(flops=flops, bytes_accessed=moved, transcendentals=hard)


def window_of(spacing, step_lon):
    base = lead + step_lon * spacing
    return base // 8, base % 8


def roll_rows(value, shift, count):
    if shift:
        value = pltpu.roll(value, value.shape[0] - shift, 0)
    return value[:count]


def pick(value, scalar):
    return pl.multiple_of(value, scalar)


def split_lanes(line):
    return [line[:, 128 * n : 128 * (n + 1)] for n in range(line.shape[1] // 128)]


main = margin // 8 * 8
rest = margin - main


def put_packed(packed, number, main_value, rest_value, blocks):
    packed[main * number : main * (number + 1), :] = main_value
    first = main * blocks + rest * number
    packed[first : first + rest, :] = rest_value


def packed_main(line, number):
    return line[main * number : main * (number + 1)]


def packed_rest(line, number, blocks):
    first = main * blocks + rest * number
    return line[first : first + rest]


def edges_body(tile_ref, right_ref, left_ref, sum_ref, packed):
    rows, cols, chan = tile_ref.shape

    def row_step(row, carry):
        line = tile_ref[row].astype(f32)
        blocks = split_lanes(line)
        for number, block in enumerate(blocks):
            put_packed(packed.at[0, row], number, block[:main], block[main:margin], len(blocks))
            put_packed(
                packed.at[1, row],
                number,
                block[cols - main :],
                roll_rows(block, cols - margin, rest),
                len(blocks),
            )
        return carry + line

    total = lax.fori_loop(0, rows, row_step, jnp.zeros((cols, chan), f32), unroll=2)
    left_ref[...] = packed[0].astype(bf16)
    right_ref[...] = packed[1].astype(bf16)

    @pl.when(pl.program_id(0) == 0)
    def _():
        sum_ref[...] = jnp.zeros_like(sum_ref)

    sum_ref[...] += jnp.sum(total, axis=0, keepdims=True)


def edges(tile):
    rows, cols, chan = tile.shape
    wide = margin * chan // 128
    block = rows // 3
    by_rows = lambda *shape: pl.BlockSpec((block,) + shape, lambda i: (i, 0, 0))
    return pl.pallas_call(
        edges_body,
        grid=(3,),
        in_specs=[by_rows(cols, chan)],
        out_specs=[by_rows(wide, 128), by_rows(wide, 128), whole(1, chan)],
        out_shape=[
            shaped(bf16, rows, wide, 128),
            shaped(bf16, rows, wide, 128),
            shaped(f32, 1, chan),
        ],
        scratch_shapes=[pltpu.VMEM((2, block, wide, 128), f32)],
        compiler_params=params(8),
        cost_estimate=cost(rows * cols * chan, 2_000_000),
        name="edges",
    )(stay(tile))


def corners_body(id_ref, left_ref, right_ref, sum_ref, *refs):
    chip_ref, cross_ref, out_ref = refs[-3:]
    rows = left_ref.shape[0]
    upper = id_ref[1]
    for number, ref in enumerate((left_ref, right_ref)):
        place = slice(margin * number, margin * (number + 1))
        chip_ref[place] = ref[pl.ds((rows - margin) * (1 - upper), margin)]
        cross_ref[place] = ref[pl.ds((rows - margin) * upper, margin)]
    out_ref[...] = sum_ref[...]


def corners(ids, left, right, running, before):
    _, wide, lanes = left.shape
    return pl.pallas_call(
        corners_body,
        in_specs=[smem()] + [vmem()] * 3 + [anywhere()] * len(before),
        out_specs=[vmem()] * 3,
        out_shape=[shaped(bf16, 2 * margin, wide, lanes)] * 2 + [shaped(f32, *running.shape)],
        compiler_params=params(8),
        cost_estimate=cost(1000, 3_000_000),
        name="corners",
    )(ids, left, right, running, *before)


def fill_extended(ext, halos, blocks, upper):
    tile, left, right, chip, cross, chip_corner, cross_corner = halos
    rows, cols, _ = tile.shape
    off, after = lead - margin, lead + cols

    def put(at, row, middle, before, behind, skip=0):
        before, behind = before[row].astype(f32), behind[row + skip].astype(f32)
        count = before.shape[0] // margin
        for number, block in blocks:
            line = ext(block, at)
            line[lead:after, :] = middle[row, :, 128 * block : 128 * (block + 1)].astype(f32)
            line[lead - main : lead, :] = packed_main(before, number)
            line[off : off + rest, :] = packed_rest(before, number, count)
            line[after : after + main, :] = packed_main(behind, number)
            line[after + main : after + margin, :] = packed_rest(behind, number, count)

    def tile_row(row, carry):
        put(margin + row, row, tile, left, right)
        return carry

    chip_first = (margin + rows) * (1 - upper)
    cross_first = (margin + rows) * upper

    def strip_row(row, carry):
        put(chip_first + row, row, chip, chip_corner, chip_corner, margin)
        put(cross_first + row, row, cross, cross_corner, cross_corner, margin)
        return carry

    lax.fori_loop(0, rows, tile_row, 0, unroll=2)
    lax.fori_loop(0, margin, strip_row, 0, unroll=2)


def halo_specs(halos, lanes):
    return [
        by_lanes(*halo.shape[:2], lanes=lanes) if number in (0, 3, 4) else vmem()
        for number, halo in enumerate(halos)
    ]


def fill_taps(taps, kernel_ref):
    for member in range(3):
        for tap in range(9):
            taps[9 * member + tap] = jnp.broadcast_to(
                kernel_ref[member, tap : tap + 1, :], taps.shape[1:]
            )


def pack(row_ref, value, vector):
    size, part = value.shape
    row_ref[...] = jnp.zeros_like(row_ref)
    for number in range(size // 16):
        row_ref[:, part * number : part * (number + 1)] = value[16 * number : 16 * (number + 1)]
    row_ref[0:1, 640 : 640 + vector.shape[1]] = vector
    return row_ref[...].astype(bf16)


def unpack(message, put, part, size, fan):
    for number in range(size // 16):
        put(number, message[:, part * number : part * (number + 1)])
    return message[0:1, 640 : 640 + fan]


def conv_body(
    id_ref, tile_ref, left_ref, right_ref, top_ref, bottom_ref, up_ref, down_ref, kernel_ref,
    weight_ref, pooled_ref, cot_ref,
    inputs_ref, own_ref, one_ref, two_ref, three_ref, own_cot_ref, own_pool_ref,
    ext, cells, taps, total, pool, rows_ref,
):
    step = pl.program_id(0)
    halos = (tile_ref, left_ref, right_ref, top_ref, bottom_ref, up_ref, down_ref)
    rows, cols, _ = tile_ref.shape
    blocks, lanes = 2, 128
    fan = weight_ref.shape[2]

    @pl.when(step == 0)
    def _():
        total[...] = jnp.zeros_like(total)
        pool[...] = jnp.zeros_like(pool)

    fill_taps(taps, kernel_ref)

    for number in range(2):

        @pl.when(step == number)
        def _(number=number):
            fill_extended(
                lambda block, row: ext.at[block, row],
                halos,
                [(blocks * number + block, block) for block in range(blocks)],
                id_ref[1],
            )

    for block in range(blocks):
        across = slice(lanes * block, lanes * (block + 1))

        def conv_rows(pair, carry, block=block, across=across):
            at = (2 * pair, 2 * pair + 1)
            places = [pl.ds(pl.multiple_of(row * cols, 8), cols) for row in at]
            for row, place in zip(at, places):
                cells[0, place, across] = ext[block, margin + row, lead : lead + cols, :]
            for member, spacing in enumerate(dilations):
                summed = [None, None]
                for step_lon in (-1, 0, 1):
                    group, shift = window_of(spacing, step_lon)
                    count = cols // 8 + (shift != 0)
                    part = [None, None]
                    for step_lat in (-1, 0, 1):
                        tap = taps[9 * member + 3 * (step_lat + 1) + step_lon + 1, :, across]
                        for n in (0, 1):
                            window = ext[
                                block,
                                at[n] + margin + step_lat * spacing,
                                8 * group : 8 * (group + count),
                                :,
                            ].reshape(count, 8, lanes)
                            term = window * tap
                            part[n] = term if part[n] is None else part[n] + term
                    for n in (0, 1):
                        piece = roll_rows(part[n].reshape(8 * count, lanes), shift, cols)
                        summed[n] = piece if summed[n] is None else summed[n] + piece
                for n in (0, 1):
                    cells[member + 1, places[n], across] = summed[n]
            return carry

        lax.fori_loop(0, rows // 2, conv_rows, 0, unroll=2)
    for member in range(4):
        block = cells[member].astype(bf16)
        inputs_ref[member] = block
        total[:, fan * member : fan * (member + 1)] += jnp.dot(
            block, weight_ref[member], preferred_element_type=f32
        )
    pool[...] += jnp.dot(
        jnp.broadcast_to(pooled_ref[...], (8, blocks * lanes)),
        weight_ref[4].astype(f32),
        precision=lax.Precision.HIGHEST,
        preferred_element_type=f32,
    )

    @pl.when(step == pl.num_programs(0) - 1)
    def _():
        size = own_ref.shape[0]
        me = id_ref[0]
        band = rows // 4
        part = cot_ref.shape[2]

        def chunk(ahead):
            return total[pl.ds(pl.multiple_of(lax.rem(me + ahead, 4) * size, 16), size), :]

        def cot_chunk(ahead):
            picked = cot_ref[pl.ds(lax.rem(me + ahead, 4) * band, band)]
            return picked.astype(f32).reshape(size, part)

        own_ref[...] = chunk(0)
        own_cot_ref[...] = cot_chunk(0)
        own_pool_ref[...] = pool[0:1, :]
        for ahead, ref in enumerate((one_ref, two_ref, three_ref), 1):
            ref[:size, :] = chunk(ahead).astype(bf16)
            ref[size:, :] = pack(rows_ref, cot_chunk(ahead), pool[0:1, :])


def conv_forward(ids, halos, kernel, weight, pooled, cotangent):
    rows, cols, chan = halos[0].shape
    tall, wide = rows + 2 * margin, cols + 2 * lead
    fan = weight.shape[2]
    lanes = 256
    size = rows * cols // 4
    cells = rows * cols
    part = cotangent.shape[2]
    return pl.pallas_call(
        conv_body,
        grid=(chan // lanes,),
        in_specs=[smem()]
        + halo_specs(halos, lanes)
        + [
            by_lanes(3, 9, lanes=lanes),
            pl.BlockSpec((5, lanes, fan), lambda i: (0, i, 0)),
            by_lanes(1, lanes=lanes),
            whole(*cotangent.shape),
        ],
        out_specs=[by_lanes(4, cells, lanes=lanes), whole(size, 4 * fan)]
        + [whole(size + 16, 4 * fan)] * 3
        + [whole(size, part), whole(1, fan)],
        out_shape=[
            far(bf16, 4, cells, chan),
            far(f32, size, 4 * fan),
        ]
        + [shaped(bf16, size + 16, 4 * fan)] * 3
        + [shaped(f32, size, part), shaped(f32, 1, fan)],
        scratch_shapes=[
            pltpu.VMEM((lanes // 128, tall, wide, 128), f32),
            pltpu.VMEM((4, cells, lanes), f32),
            pltpu.VMEM((27, 8, lanes), f32),
            pltpu.VMEM((cells, 4 * fan), f32),
            pltpu.VMEM((8, fan), f32),
            pltpu.VMEM((16, 4 * fan), f32),
        ],
        compiler_params=params(40),
        cost_estimate=cost(2 * cells * chan * (4 * fan + 27), 20_000_000),
        name="conv_forward",
    )(ids, stay(halos[0]), *halos[1:], kernel, weight, pooled, cotangent)


def slope(value, sig):
    return sig * (1.0 + value * (1.0 - sig))


def proj_body(
    id_ref, own_ref, one_ref, two_ref, three_ref, own_cot_ref, own_pool_ref,
    weight_own, weight_one, weight_two, weight_three, _, last_ref, dpre_ref, send_one_ref, send_two_ref, send_three_ref,
    grad_own_ref, own_mixed_ref, own_sum_ref, pool_ref,
    pre, grads, weights, pieces, cot, rows_ref,
):
    size, part = own_cot_ref.shape
    fan = 4 * part
    me = id_ref[0]
    pre[...] = own_ref[...]
    pool = own_pool_ref[...]
    pieces[me] = own_cot_ref[...]
    for behind, ref in enumerate((one_ref, two_ref, three_ref), 1):
        pre[...] += ref[:size, :].astype(f32)
        origin = lax.rem(me + 4 - behind, 4)

        def put(number, value, origin=origin):
            pieces[origin, 16 * number : 16 * (number + 1), :] = value

        pool = pool + unpack(ref[size:, :].astype(f32), put, part, size, fan)
    for origin in range(4):
        cot[:, part * origin : part * (origin + 1)] = pieces[origin]
    for behind, ref in enumerate((weight_own, weight_one, weight_two, weight_three)):
        first = pl.multiple_of(lax.rem(me + 4 - behind, 4) * part, 16)
        weights[:, pl.ds(first, part), :] = ref[...]
    last_ref[...] = weights[4]

    pool_ref[...] = pool
    pool = jnp.broadcast_to(pool, (8, fan))
    pool_branch = (pool * jax.nn.sigmoid(pool)).astype(bf16)
    proj = jnp.dot(pool_branch, weights[4], preferred_element_type=f32)[0:1, :]
    for member in range(4):
        value = pre[:, fan * member : fan * (member + 1)]
        branch = (value * jax.nn.sigmoid(value)).astype(bf16)
        proj = proj + jnp.dot(branch, weights[member], preferred_element_type=f32)
    sig = jax.nn.sigmoid(proj)
    mixed = (proj * sig).astype(bf16).astype(f32)
    back = (cot[...] * slope(proj, sig)).astype(bf16)
    back_sum = jnp.sum(back.astype(f32), axis=0, keepdims=True)
    own_sum_ref[...] = back_sum
    for target in range(4):
        pieces[target] = mixed[:, part * target : part * (target + 1)]
    own_mixed_ref[...] = pieces[me]
    for member in range(4):
        lanes = slice(fan * member, fan * (member + 1))
        value = pre[:, lanes]
        sig = jax.nn.sigmoid(value)
        branch = (value * sig).astype(bf16)
        grads[member] = lax.dot_general(
            branch, back, (((0,), (0,)), ((), ())), preferred_element_type=f32
        )
        dbranch = lax.dot_general(
            back, weights[member], (((1,), (1,)), ((), ())), preferred_element_type=f32
        )
        dpre = (dbranch * slope(value, sig)).astype(bf16)
        for ref in (dpre_ref, send_one_ref, send_two_ref, send_three_ref):
            ref[:size, lanes] = dpre
        grad_own_ref[member] = grads[member, pl.ds(pl.multiple_of(me * part, 16), part), :]
        for ahead, ref in enumerate((send_one_ref, send_two_ref, send_three_ref), 1):
            first = pl.multiple_of(lax.rem(me + ahead, 4) * part, 16)
            ref[size + 16 :, lanes] = grads[member, pl.ds(first, part), :].astype(bf16)
    for ahead, ref in enumerate((send_one_ref, send_two_ref, send_three_ref), 1):
        ref[size : size + 16, :] = pack(rows_ref, pieces[lax.rem(me + ahead, 4)], back_sum)


def project(ids, own, others, own_cot, own_pool, weights, before):
    size, wide = own.shape
    fan = wide // 4
    part = fan // 4
    return pl.pallas_call(
        proj_body,
        in_specs=[smem()] + [vmem()] * 10 + [anywhere()],
        out_specs=[vmem()] * 9,
        out_shape=[shaped(bf16, fan, fan), shaped(bf16, size, wide)]
        + [shaped(bf16, size + 16 + part, wide)] * 3
        + [shaped(f32, 4, part, fan)]
        + [shaped(f32, size, part), shaped(f32, 1, fan), shaped(f32, 1, fan)],
        scratch_shapes=[
            pltpu.VMEM((size, wide), f32),
            pltpu.VMEM((4, fan, fan), f32),
            pltpu.VMEM((5, fan, fan), bf16),
            pltpu.VMEM((4, size, part), f32),
            pltpu.VMEM((size, fan), f32),
            pltpu.VMEM((16, wide), f32),
        ],
        compiler_params=params(16),
        cost_estimate=cost(6 * size * wide * fan, 4_000_000, 2 * size * wide),
        name="project",
    )(ids, stay(own), *others, own_cot, own_pool, *weights, before)


def weight_body(
    id_ref, own_ref, gp_ref, own_sum_ref, one_ref, two_ref, three_ref, inputs_ref,
    keep_ref, give_ref, full_ref, total_ref, sum_ref,
):
    size = own_ref.shape[0]
    fan = keep_ref.shape[2]
    me, upper = id_ref[0], id_ref[1]
    others = (one_ref, two_ref, three_ref)
    full_ref[pl.ds(pl.multiple_of(me * size, 16), size), :] = own_ref[...]
    for behind, ref in enumerate(others, 1):
        first = pl.multiple_of(lax.rem(me + 4 - behind, 4) * size, 16)
        full_ref[pl.ds(first, size), :] = ref[:size, :]

    def grad(member):
        lanes = pl.ds(pl.multiple_of(member * fan, 256), fan)
        return lax.dot_general(
            inputs_ref[member],
            full_ref[:, lanes],
            (((0,), (0,)), ((), ())),
            preferred_element_type=f32,
        )

    for number in range(2):
        give_ref[number] = grad(2 * (1 - upper) + number).astype(bf16)
        keep_ref[number] = grad(2 * upper + number)
    for member in range(4):
        value = gp_ref[member]
        for ref in others:
            value = value + ref[size + 16 :, fan * member : fan * (member + 1)].astype(f32)
        total_ref[member] = value
    total = own_sum_ref[...]
    for ref in others:
        total = total + ref[size : size + 16, 640 : 640 + fan].astype(f32)[0:1]
    sum_ref[...] = total


def weight_grads(ids, own, gp_own, own_sum, others, inputs):
    size, wide = own.shape
    fan = wide // 4
    part = fan // 4
    _, cells, chan = inputs.shape
    return pl.pallas_call(
        weight_body,
        in_specs=[smem()] + [vmem()] * 7,
        out_specs=[vmem()] * 5,
        out_shape=[
            shaped(f32, 2, chan, fan),
            shaped(bf16, 2, chan, fan),
            shaped(bf16, cells, wide),
            shaped(f32, 4, part, fan),
            shaped(f32, 1, fan),
        ],
        compiler_params=params(20),
        cost_estimate=cost(2 * cells * chan * wide, 6_000_000),
        name="weight_grads",
    )(ids, own, gp_own, own_sum, *others, stay(inputs))


def unpack_body(id_ref, own_mixed_ref, one_ref, two_ref, three_ref, mixed_ref, pieces):
    size, part = own_mixed_ref.shape
    me = id_ref[0]
    pieces[me] = own_mixed_ref[...]
    for behind, ref in enumerate((one_ref, two_ref, three_ref), 1):
        origin = lax.rem(me + 4 - behind, 4)

        def put(number, value, origin=origin):
            pieces[origin, 16 * number : 16 * (number + 1), :] = value

        unpack(ref[...].astype(f32), put, part, size, 4 * part)
    mixed_ref[...] = pieces[...].astype(bf16)


def unpack_mixed(ids, own_mixed, others):
    size, part = own_mixed.shape
    rows = pl.BlockSpec((16, others[0].shape[1]), lambda i: (size // 16, 0))
    return pl.pallas_call(
        unpack_body,
        grid=(1,),
        in_specs=[smem(), whole(size, part)] + [rows] * 3,
        out_specs=whole(4, size, part),
        out_shape=shaped(bf16, 4, size, part),
        scratch_shapes=[pltpu.VMEM((4, size, part), f32)],
        compiler_params=params(8),
        cost_estimate=cost(100_000, 500_000),
        name="unpack_mixed",
    )(ids, own_mixed, *[stay(value) for value in others])


placed = {}
for _member in range(3):
    for _step in (-1, 0, 1):
        _key = (_member, window_of(dilations[_member], _step)[1])
        placed.setdefault(_key, len(placed))


def shift_rows(shifted, source, rows, cols, lanes):
    def row_step(row, carry):
        place = pl.ds(pl.multiple_of(row * cols, 8), cols)
        for member in range(3):
            value = source(member, place)
            wide = jnp.concatenate([value, jnp.zeros((8, lanes), f32)], axis=0)
            for (owner, shift), number in placed.items():
                if owner != member:
                    continue
                shifted[number, row] = pltpu.roll(wide, shift, 0) if shift else wide
        return carry

    lax.fori_loop(0, rows, row_step, 0, unroll=4)


def scatter_body(
    id_ref, dpre_ref, weight_ref, kernel_ref, _,
    grad_ref, center_ref, left_ref, right_ref, chip_ref, cross_corner, cross_center, token_ref,
    taps, first, grads, shifted, strips,
):
    rows, cols, across_all = center_ref.shape
    lanes = 128
    fan = weight_ref.shape[2]
    wide = cols + 2 * margin
    groups = (cols + 2 * lead) // 8
    off = lead - margin
    fill_taps(taps, kernel_ref)
    token_ref[...] = jnp.zeros_like(token_ref)
    for member in range(4):
        piece = lax.dot_general(
            dpre_ref[:, fan * member : fan * (member + 1)],
            weight_ref[member],
            (((1,), (1,)), ((), ())),
            preferred_element_type=f32,
        )
        if member == 0:
            first[...] = piece
        else:
            piece = piece.astype(bf16)
            grad_ref[member - 1] = piece
            grads[member - 1] = piece.astype(f32)

    for block in range(across_all // lanes):
        across = slice(lanes * block, lanes * (block + 1))
        shift_rows(
            shifted,
            lambda member, place, across=across: grads[member, place, across],
            rows,
            cols,
            lanes,
        )
        for begin in range(0, rows + 2 * margin, 6):
            active = [
                (member, step_lat)
                for member, spacing in enumerate(dilations)
                for step_lat in (-1, 0, 1)
                if margin + step_lat * spacing <= begin < margin + rows + step_lat * spacing
            ]
            inside = margin <= begin < margin + rows

            def ext_rows(at, begin=begin, active=active, inside=inside, across=across):
                sums = [[None] * groups, [None] * groups]
                for n in (0, 1):
                    if inside:
                        value = first[pl.ds(pl.multiple_of((at[n] - margin) * cols, 8), cols), across]
                        for number in range(cols // 8):
                            sums[n][lead // 8 + number] = value[8 * number : 8 * (number + 1)]
                for member, step_lat in active:
                    spacing = dilations[member]
                    for step_lon in (-1, 0, 1):
                        group, shift = window_of(spacing, step_lon)
                        count = cols // 8 + (shift != 0)
                        weight = taps[9 * member + 3 * (step_lat + 1) + step_lon + 1, :, across]
                        for n in (0, 1):
                            grad = shifted[
                                placed[member, shift],
                                at[n] - margin - step_lat * spacing,
                                : 8 * count,
                                :,
                            ]
                            for number in range(count):
                                term = grad[8 * number : 8 * (number + 1)] * weight
                                old = sums[n][group + number]
                                sums[n][group + number] = term if old is None else old + term
                for n in (0, 1):
                    parts = [jnp.zeros((8, lanes), f32) if s is None else s for s in sums[n]]
                    center = jnp.concatenate(parts[lead // 8 : (lead + cols) // 8], axis=0)
                    left = jnp.concatenate(
                        parts[(lead - main) // 8 : lead // 8] + [roll_rows(parts[off // 8], off % 8, 8)],
                        axis=0,
                    )[:margin]
                    right = jnp.concatenate(parts[(lead + cols) // 8 :], axis=0)[:margin]
                    if inside:
                        row = at[n] - margin
                        center_ref[row, :, across] = center.astype(bf16)
                        left_ref[row, :, across] = left.astype(bf16)
                        right_ref[row, :, across] = right.astype(bf16)
                    else:
                        side = int(begin >= margin)
                        row = at[n] - side * (margin + rows)
                        strips[side, row, :cols, across] = center
                        strips[side, row, cols : cols + margin, across] = left
                        strips[side, row, cols + margin : wide, across] = right

            if inside:

                def step_rows(step, carry, begin=begin, ext_rows=ext_rows):
                    ext_rows((begin + 2 * step, begin + 2 * step + 1))
                    return carry

                lax.fori_loop(0, 3, step_rows, 0, unroll=3)
            else:
                for step in range(3):
                    ext_rows((begin + 2 * step, begin + 2 * step + 1))

    for upper in (0, 1):

        @pl.when(id_ref[1] == upper)
        def _(upper=upper):
            for row in range(margin):
                chip_ref[row] = strips[1 - upper, row, :wide, :].astype(bf16)
                cross_corner[row] = strips[upper, row, cols:wide, :].astype(bf16)
                cross_center[row] = strips[upper, row, :cols, :].astype(bf16)


def scatter_grads(ids, dpre, weight, kernel, rows, cols, before):
    cells, wide_fan = dpre.shape
    fan = wide_fan // 4
    chan = weight.shape[1]
    wide = cols + 2 * margin
    lanes = 256
    return pl.pallas_call(
        scatter_body,
        grid=(chan // lanes,),
        in_specs=[
            smem(),
            whole(cells, wide_fan),
            pl.BlockSpec((4, lanes, fan), lambda i: (0, i, 0)),
            by_lanes(3, 9, lanes=lanes),
            anywhere(),
        ],
        out_specs=[
            by_lanes(3, cells, lanes=lanes),
            by_lanes(rows, cols, lanes=lanes),
            by_lanes(rows, margin, lanes=lanes),
            by_lanes(rows, margin, lanes=lanes),
        ]
        + [by_lanes(margin, wide, lanes=lanes)]
        + [by_lanes(margin, 2 * margin, lanes=lanes), by_lanes(margin, cols, lanes=lanes)]
        + [whole(8, 128)],
        out_shape=[
            far(bf16, 3, cells, chan),
            far(bf16, rows, cols, chan),
            far(bf16, rows, margin, chan),
            far(bf16, rows, margin, chan),
        ]
        + [shaped(bf16, margin, wide, chan)]
        + [shaped(bf16, margin, 2 * margin, chan), shaped(bf16, margin, cols, chan)]
        + [shaped(f32, 8, 128)],
        scratch_shapes=[
            pltpu.VMEM((27, 8, lanes), f32),
            pltpu.VMEM((cells, lanes), f32),
            pltpu.VMEM((3, cells, lanes), f32),
            pltpu.VMEM((len(placed), rows, cols + 8, 128), f32),
            pltpu.VMEM((2, margin, cols + 2 * lead - 8, lanes), f32),
        ],
        compiler_params=params(24),
        cost_estimate=cost(2 * cells * chan * (wide_fan + 27), 15_000_000),
        name="scatter_grads",
    )(ids, dpre, weight, kernel, before)


def extend_body(
    id_ref, tile_ref, left_ref, right_ref, top_ref, bottom_ref, up_ref, down_ref, _, ext_ref, token_ref, ext
):
    halos = (tile_ref, left_ref, right_ref, top_ref, bottom_ref, up_ref, down_ref)
    ext[...] = jnp.zeros_like(ext)
    token_ref[...] = jnp.zeros_like(token_ref)
    blocks = ext.shape[0]
    fill_extended(
        lambda block, row: ext.at[block, row],
        halos,
        [(block, block) for block in range(blocks)],
        id_ref[1],
    )

    def copy_rows(row, carry):
        for block in range(blocks):
            ext_ref[row, :, 128 * block : 128 * (block + 1)] = ext[block, row].astype(bf16)
        return carry

    lax.fori_loop(0, ext.shape[1], copy_rows, 0, unroll=4)


def extend(ids, halos, before):
    rows, cols, chan = halos[0].shape
    tall, wide = rows + 2 * margin, cols + 2 * lead + 8
    return pl.pallas_call(
        extend_body,
        in_specs=[smem()] + [vmem()] * 7 + [anywhere()],
        out_specs=[vmem()] * 2,
        out_shape=[far(bf16, tall, wide, chan), shaped(f32, 8, 128)],
        scratch_shapes=[pltpu.VMEM((chan // 128, tall, wide, 128), f32)],
        compiler_params=params(36),
        cost_estimate=cost(1_000_000, 10_000_000),
        name="extend",
    )(ids, *[stay(halo) for halo in halos], before)


def taps_body(grad_ref, ext_ref, sum_ref, tap_ref, ext, grads, shifted):
    step = pl.program_id(0)
    tall, wide, lanes = ext_ref.shape
    rows, cols = tall - 2 * margin, wide - 2 * lead - 8
    per = sum_ref.shape[1] // lanes
    first = 32 * (step // per)
    place = pl.ds(pl.multiple_of(lanes * lax.rem(step, per), 128), lanes)

    def widen_row(row, carry):
        ext[row] = ext_ref[row].astype(f32)
        return carry

    lax.fori_loop(0, tall, widen_row, 0, unroll=4)
    grads[...] = grad_ref[...].astype(f32)
    shift_rows(shifted, lambda member, place: grads[member, place, :], rows, cols, lanes)

    def tap_row(row, carry):
        sums = list(carry)
        for member, spacing in enumerate(dilations):
            for step_lon in (-1, 0, 1):
                group, shift = window_of(spacing, step_lon)
                count = cols // 8 + (shift != 0)
                grad = shifted[placed[member, shift], row, : 8 * count, :].reshape(count, 8, lanes)
                for step_lat in (-1, 0, 1):
                    window = ext[
                        row + margin + step_lat * spacing, 8 * group : 8 * (group + count), :
                    ].reshape(count, 8, lanes)
                    tap = 9 * member + 3 * (step_lat + 1) + step_lon + 1
                    sums[tap] = sums[tap] + jnp.sum(grad * window, axis=0)
        return tuple(sums)

    sums = lax.fori_loop(0, rows, tap_row, (jnp.zeros((8, lanes), f32),) * 27, unroll=2)
    rows_of = [jnp.sum(value, axis=0, keepdims=True) for value in sums]
    rows_of.append(sum_ref[:, place])
    rows_of += [jnp.zeros((1, lanes), f32)] * 4
    tap_ref[pl.ds(pl.multiple_of(first, 32), 32), place] = jnp.concatenate(rows_of, axis=0)


def tap_sums(grads, extended, back_sum):
    tall, wide, chan = extended.shape
    _, cells, _ = grads.shape
    rows, cols = tall - 2 * margin, wide - 2 * lead - 8
    lanes = 128
    shape = (32 * chan // back_sum.shape[1], back_sum.shape[1])
    return pl.pallas_call(
        taps_body,
        grid=(chan // lanes,),
        in_specs=[by_lanes(3, cells), by_lanes(tall, wide), whole(*back_sum.shape)],
        out_specs=whole(*shape),
        out_shape=shaped(f32, *shape),
        scratch_shapes=[
            pltpu.VMEM((tall, wide, lanes), f32),
            pltpu.VMEM((3, cells, lanes), f32),
            pltpu.VMEM((len(placed), rows, cols + 8, lanes), f32),
        ],
        compiler_params=params(20),
        cost_estimate=cost(2 * cells * chan * 27, 15_000_000),
        name="tap_sums",
    )(stay(grads), stay(extended), back_sum)


def home_body(
    id_ref, left_ref, right_ref, chip_ref, corner_ref, left_out, right_out, packed, line
):
    rows, _, _ = left_ref.shape
    wide = chip_ref.shape[1]
    cols = wide - 2 * margin
    shifted = rows - margin

    def one_row(row, refs):
        left, right = left_ref[row].astype(f32), right_ref[row].astype(f32)
        for ref, first, number in refs:
            line[number, cols - ref.shape[1] + 2 * margin :, :] = ref[row - first].astype(f32)
            left = left + line[number, cols : cols + margin, :]
            right = right + line[number, cols + margin :, :]
        pairs = list(zip(split_lanes(left), split_lanes(right)))
        for number, pair in enumerate(pairs):
            for side, value in enumerate(pair):
                put_packed(packed.at[side, row], number, value[:main], value[main:], len(pairs))

    for upper in (0, 1):
        pieces = [(chip_ref, shifted * (1 - upper), 0), (corner_ref, shifted * upper, 1)]
        cuts = sorted({0, rows} | {at for _, first, _ in pieces for at in (first, first + margin)})

        @pl.when(id_ref[1] == upper)
        def _(pieces=pieces, cuts=cuts):
            for first, last in zip(cuts, cuts[1:]):
                refs = [piece for piece in pieces if piece[1] <= first < piece[1] + margin]

                def step(number, carry, first=first, refs=refs):
                    one_row(first + number, refs)
                    return carry

                lax.fori_loop(0, last - first, step, 0, unroll=3)

    left_out[...] = packed[0].astype(bf16)
    right_out[...] = packed[1].astype(bf16)


def home(ids, left, right, chip, corner):
    rows, _, chan = left.shape
    wide = margin * chan // 128
    return pl.pallas_call(
        home_body,
        in_specs=[smem()] + [vmem()] * 4,
        out_specs=[vmem()] * 2,
        out_shape=[shaped(bf16, rows, wide, 128)] * 2,
        scratch_shapes=[
            pltpu.VMEM((2, rows, wide, 128), f32),
            pltpu.VMEM((2, chip.shape[1], chan), f32),
        ],
        compiler_params=params(16),
        cost_estimate=cost(rows * margin * chan, 5_000_000),
        name="home",
    )(ids, stay(left), stay(right), chip, corner)


def middle_body(id_ref, center_ref, chip_ref, cross_ref, out_ref):
    rows, cols, _ = center_ref.shape
    shifted = rows - margin
    out_ref[...] = center_ref[...].astype(f32)
    for upper in (0, 1):
        chip_first, cross_first = shifted * (1 - upper), shifted * upper

        @pl.when(id_ref[1] == upper)
        def _(chip_first=chip_first, cross_first=cross_first):
            for row in range(margin):
                out_ref[chip_first + row] += chip_ref[row].astype(f32)[:cols]
            for row in range(margin):
                out_ref[cross_first + row] += cross_ref[row].astype(f32)


def middle(ids, center, chip, cross):
    rows, cols, chan = center.shape
    return pl.pallas_call(
        middle_body,
        grid=(chan // 128,),
        in_specs=[
            smem(),
            by_lanes(rows, cols),
            by_lanes(*chip.shape[:2]),
            by_lanes(*cross.shape[:2]),
        ],
        out_specs=by_lanes(rows, cols),
        out_shape=shaped(f32, rows, cols, chan),
        compiler_params=params(12),
        cost_estimate=cost(rows * cols * chan, 4_000_000),
        name="middle",
    )(ids, stay(center), stay(chip), stay(cross))


def finish_body(center_ref, left_ref, right_ref, pooled_ref, out_ref, pads):
    rows, cols, chan = center_ref.shape
    base = pooled_ref[...]

    @pl.when(pl.program_id(0) == 0)
    def _():
        pads[...] = jnp.zeros_like(pads)

    def row_step(row, carry):
        left, right = left_ref[row].astype(f32), right_ref[row].astype(f32)
        count = chan // 128
        for number in range(count):
            across = slice(128 * number, 128 * (number + 1))
            pads[0, row, :main, across] = packed_main(left, number)
            pads[0, row, main:margin, across] = packed_rest(left, number, count)
            pads[1, row, cols - main :, across] = packed_main(right, number)
            pads[1, row, cols - margin : cols - main, across] = packed_rest(right, number, count)
        return carry

    lax.fori_loop(0, rows, row_step, 0, unroll=4)

    def add_row(row, carry):
        out_ref[row] = (center_ref[row] + pads[0, row] + pads[1, row] + base).astype(bf16)
        return carry

    lax.fori_loop(0, rows, add_row, 0, unroll=4)


def finish(center, left, right, pooled):
    rows, cols, chan = center.shape
    wide = margin * chan // 128
    block = rows // 3
    by_rows = lambda *shape: pl.BlockSpec((block,) + shape, lambda i: (i, 0, 0))
    return pl.pallas_call(
        finish_body,
        grid=(3,),
        in_specs=[by_rows(cols, chan), by_rows(wide, 128), by_rows(wide, 128), whole(1, chan)],
        out_specs=by_rows(cols, chan),
        out_shape=shaped(bf16, rows, cols, chan),
        scratch_shapes=[pltpu.VMEM((2, block, cols, chan), f32)],
        compiler_params=params(10),
        cost_estimate=cost(rows * cols * chan, 4_000_000),
        name="finish",
    )(center, left, right, pooled)


def core_body(id_ref, keep_ref, got_ref, gp_ref, own_ref, one_ref, two_ref, three_ref, token_ref):
    token_ref[...] = jnp.zeros_like(token_ref)
    fan = keep_ref.shape[1]
    rows = own_ref.shape[0] - gp_ref.shape[1]
    here = id_ref[2]
    for code, ref in enumerate((own_ref, one_ref, two_ref, three_ref)):
        target = here ^ code
        place = pl.ds(pl.multiple_of(target * rows, 16), rows)
        ref[:rows, :] = (keep_ref[place, :] + got_ref[place, :].astype(f32)).astype(ref.dtype)
        ref[rows:, :] = gp_ref[target].astype(ref.dtype)


def core_stage(ids, keep, got, gp):
    rows, fan = keep.shape
    part = gp.shape[1]
    size = rows // 4 + part
    return pl.pallas_call(
        core_body,
        in_specs=[smem()] + [vmem()] * 3,
        out_specs=[vmem()] * 5,
        out_shape=[shaped(f32, size, fan)] + [shaped(bf16, size, fan)] * 3 + [shaped(f32, 8, 128)],
        compiler_params=params(12),
        cost_estimate=cost(rows * fan, 3_000_000),
        name="core_stage",
    )(ids, keep, got, gp)


def y_body(id_ref, own_ref, one_ref, two_ref, three_ref, _, keep_ref, give_ref, total):
    half, _ = keep_ref.shape
    upper = id_ref[3]
    total[...] = (
        own_ref[...] + one_ref[...].astype(f32) + two_ref[...].astype(f32) + three_ref[...].astype(f32)
    )
    keep_ref[...] = total[pl.ds(pl.multiple_of(upper * half, 16), half), :]
    give_ref[...] = total[pl.ds(pl.multiple_of((1 - upper) * half, 16), half), :].astype(bf16)


def y_stage(ids, own, others, before):
    size, fan = own.shape
    return pl.pallas_call(
        y_body,
        in_specs=[smem()] + [vmem()] * 4 + [anywhere()],
        out_specs=[vmem()] * 2,
        out_shape=[shaped(f32, size // 2, fan), shaped(bf16, size // 2, fan)],
        scratch_shapes=[pltpu.VMEM((size, fan), f32)],
        compiler_params=params(8),
        cost_estimate=cost(size * fan, 1_000_000),
        name="y_stage",
    )(ids, own, *others, before)


def gather_body(id_ref, own_ref, extra_ref, one_ref, two_ref, three_ref, out_ref, sum_ref):
    size = own_ref.shape[0]
    here = id_ref[2]
    total = extra_ref[...]
    out_ref[pl.ds(pl.multiple_of(here * size, 16), size), :] = own_ref[...]
    for code, ref in enumerate((one_ref, two_ref, three_ref), 1):
        place = pl.ds(pl.multiple_of((here ^ code) * size, 16), size)
        out_ref[place, :] = ref[:size, :]
        total = total + ref[size:, :].astype(f32)
    out_ref[4 * size :, :] = total.astype(bf16)
    sum_ref[...] = total


def y_gather(ids, own, extra, others):
    size, fan = own.shape
    count = extra.shape[0]
    return pl.pallas_call(
        gather_body,
        in_specs=[smem()] + [vmem()] * 5,
        out_specs=[vmem()] * 2,
        out_shape=[shaped(bf16, 4 * size + count, fan), shaped(f32, count, fan)],
        compiler_params=params(8),
        cost_estimate=cost(size * fan, 2_000_000),
        name="y_gather",
    )(ids, own, extra, *others)


def last_body(
    id_ref, own_ref, got_ref, own_extra_ref, got_extra_ref, weight_ref, proj_ref, pool_ref, pooled_ref,
    branch_ref, grad_proj_ref, depth_ref, dpooled_ref, dpool, column, *, cells,
):
    highest = lax.Precision.HIGHEST
    _, chan, lanes = branch_ref.shape
    part = grad_proj_ref.shape[1]
    fan = 4 * part
    scale = 1.0 / math.sqrt(cells)
    me, upper = id_ref[0], id_ref[1]
    step = pl.program_id(0)
    size = chan // 2 + part
    top = lax.broadcasted_iota(jnp.int32, (8, lanes), 0) == 0

    def outer(column_of, row_of):
        return lax.dot_general(
            column_of,
            jnp.where(top, row_of, 0.0),
            (((0,), (0,)), ((), ())),
            precision=highest,
            preferred_element_type=f32,
        )

    @pl.when(step == 0)
    def _():
        extra = own_extra_ref[...] + got_extra_ref[4 * size :, :].astype(f32)
        for number in range(chan // fan):
            for tap in range(27):
                row = 32 * number + tap
                depth_ref[tap // 9, tap % 9 : tap % 9 + 1, fan * number : fan * (number + 1)] = (
                    extra[row : row + 1] * scale
                )
        back_sum = jnp.broadcast_to(extra[27:28], (8, fan))
        pool = jnp.broadcast_to(pool_ref[...], (8, fan))
        sig = jax.nn.sigmoid(pool)
        full = slope(pool, sig) * lax.dot_general(
            back_sum,
            proj_ref[...].astype(f32),
            (((1,), (1,)), ((), ())),
            precision=highest,
            preferred_element_type=f32,
        )
        dpooled = lax.dot_general(
            full,
            weight_ref[0].astype(f32),
            (((1,), (1,)), ((), ())),
            precision=highest,
            preferred_element_type=f32,
        )
        dpooled_ref[...] = dpooled[0:1] * (1.0 / cells)
        pool_branch = (pool * sig).astype(bf16).astype(f32)
        for number in range(fan // lanes):
            dpool[0, number] = full[:, lanes * number : lanes * (number + 1)]
            dpool[1, number] = back_sum[:, lanes * number : lanes * (number + 1)]
        for origin in range(4):
            column[origin] = pool_branch[:, part * origin : part * (origin + 1)]

    for number in range(4):
        first = size * number
        rows = slice(chan // 2 * (number % 2), chan // 2 * (number % 2 + 1))
        for ref, half in ((own_ref, upper), (got_ref, 1 - upper)):
            branch_ref[2 * half + number // 2, rows, :] = (
                ref[first : first + chan // 2, :].astype(f32) * scale
            )
        both = own_ref[first + chan // 2 : first + size, :].astype(f32)
        both = both + got_ref[first + chan // 2 : first + size, :].astype(f32)
        grad_proj_ref[number] = both * scale
    branch_ref[4] = outer(jnp.broadcast_to(pooled_ref[...], (8, chan)), dpool[0, step]) * scale
    grad_proj_ref[4] = outer(column[me], dpool[1, step]) * scale


def last_stage(ids, own, got, extra, weight, proj, pool_pre, pooled, cells):
    _, chan, fan = weight.shape
    part = fan // 4
    return pl.pallas_call(
        lambda *refs: last_body(*refs, cells=cells),
        grid=(fan // 128,),
        in_specs=[
            smem(),
            by_lanes(own.shape[0]),
            by_lanes(got.shape[0]),
            whole(*extra.shape),
            whole(*got.shape),
            pl.BlockSpec((1, chan, fan), lambda i: (4, 0, 0)),
            whole(*proj.shape),
            whole(*pool_pre.shape),
            whole(*pooled.shape),
        ],
        out_specs=[by_lanes(5, chan), by_lanes(5, part), whole(3, 9, chan), whole(1, chan)],
        out_shape=[
            shaped(f32, 5, chan, fan),
            shaped(f32, 5, part, fan),
            shaped(f32, 3, 9, chan),
            shaped(f32, 1, chan),
        ],
        scratch_shapes=[
            pltpu.VMEM((2, fan // 128, 8, 128), f32),
            pltpu.VMEM((4, 8, part), f32),
        ],
        compiler_params=params(18),
        cost_estimate=cost(8 * chan * fan, 5_000_000),
        name="last_stage",
    )(ids, own, got, extra, got, weight, proj, pool_pre, pooled)


def shift(value, axis, ahead, closed=True):
    count = lax.axis_size(axis)
    pairs = [
        (i, (i + ahead) % count) for i in range(count) if closed or 0 <= i + ahead < count
    ]
    return lax.ppermute(value, axis, pairs)


def to_partner(value):
    count = lax.axis_size("lat")
    return lax.ppermute(value, "lat", [(i, i ^ 1) for i in range(count)])


def to_other_chip(value):
    count = lax.axis_size("lat")
    pairs = [(i, i + 1) for i in range(1, count - 1, 2)]
    return lax.ppermute(value, "lat", pairs + [(j, i) for i, j in pairs])


def place_in_grid():
    return lax.axis_index("lon") * lax.axis_size("lat") + lax.axis_index("lat")


def swap(value, mask):
    count = lax.axis_size("lon") * lax.axis_size("lat")
    return lax.ppermute(value, GRID, [(i, i ^ mask) for i in range(count)])


def has(mask):
    return (place_in_grid() & mask) != 0


def number_in(bits):
    return sum(has(bit).astype(jnp.int32) << at for at, bit in enumerate(bits))


def mask_of(bits, code):
    return sum(bit for at, bit in enumerate(bits) if (code >> at) & 1)


def grid_sum(value):
    mask = 1
    while mask < lax.axis_size("lon") * lax.axis_size("lat"):
        value = value + swap(value, mask)
        mask *= 2
    return value


core_bit, y_bits = 1, (4, 2)


def z_bits():
    bits, mask = [], 8
    while mask < lax.axis_size("lon") * lax.axis_size("lat"):
        bits.append(mask)
        mask *= 2
    return bits


def per_device(features, depth_kernel, branch_weight, proj_weight, cotangent):
    rows, cols, chan = features.shape
    fan = branch_weight.shape[2]
    part = proj_weight.shape[1]
    cell_count = rows * cols * lax.axis_size("lat") * lax.axis_size("lon")
    me = lax.axis_index("ch")
    flag = lambda mask: has(mask).astype(jnp.int32)
    ids = jnp.stack(
        [me.astype(jnp.int32), flag(core_bit), number_in(y_bits), flag(z_bits()[0])]
    )
    tie = lax.optimization_barrier

    to_right, to_left, colsum = edges(features)
    left = shift(to_right, "lon", 1)
    right = shift(to_left, "lon", -1)

    proj_others = [shift(proj_weight, "ch", d) for d in (1, 2, 3)]
    pooled = colsum.reshape(chan // 128, 128)
    bits = z_bits()
    pooled = pooled + swap(pooled, core_bit)
    pooled, tile = tie((pooled, features))
    rest = rows - margin
    first = jnp.where(has(core_bit), rest, 0)
    cross = to_other_chip(lax.dynamic_slice_in_dim(tile, first, margin))
    chip = to_partner(lax.dynamic_slice_in_dim(tile, rest - first, margin))
    for mask in [bits[0], bits[2], y_bits[0]]:
        pooled = pooled + swap(pooled, mask)
    chip_corner, cross_corner, pooled = corners(ids, left, right, pooled, (chip, cross))
    cross_corner = to_other_chip(cross_corner)
    chip_corner = to_partner(chip_corner)
    for mask in [bits[1], y_bits[1]]:
        pooled = pooled + swap(pooled, mask)
    pooled = pooled.reshape(1, chan) / cell_count

    halos = (features, left, right, chip, cross, chip_corner, cross_corner)
    inputs, own, *ahead, own_cot, own_pool = conv_forward(
        ids, halos, depth_kernel, branch_weight, pooled, cotangent
    )
    ahead, proj_others = tie((ahead, proj_others))
    extended, token = extend(ids, halos, own_pool)
    others = [shift(value, "ch", d) for d, value in enumerate(ahead, 1)]
    proj_last, dpre, *sent, gp_own, own_mixed, own_sum, pool_pre = project(
        ids, own, others, own_cot, own_pool, [proj_weight, *proj_others], token
    )
    others = [shift(value, "ch", d) for d, value in enumerate(sent, 1)]
    keep, give, dpre_full, gp, back_sum = weight_grads(ids, dpre, gp_own, own_sum, others, inputs)
    mixed = unpack_mixed(ids, own_mixed, others)

    got = swap(give.reshape(2 * chan, fan), core_bit)
    big, *send, token = core_stage(ids, keep.reshape(2 * chan, fan), got, gp)
    taken = [swap(value, mask_of(y_bits, code)) for code, value in enumerate(send, 1)]
    grads, center, mid_left, mid_right, *strips, token = scatter_grads(
        ids, dpre_full, branch_weight, depth_kernel, rows, cols, token
    )
    big, give = y_stage(ids, big, taken, token)
    strips, give = tie((strips, give))
    strips = [to_partner(strips[0])] + [to_other_chip(value) for value in strips[1:]]
    extra = tap_sums(grads, extended, back_sum)
    to_left, to_right = home(ids, mid_left, mid_right, *strips[:2])
    center = middle(ids, center, strips[0], strips[2])
    for number, mask in enumerate(bits):
        got = swap(give, mask).astype(f32)
        big = big + got
        if number + 1 < len(bits):
            upper = has(bits[number + 1])
            half = big.shape[0] // 2
            give = jnp.where(upper, big[:half], big[half:]).astype(bf16)
            big = jnp.where(upper, big[half:], big[:half])
        if number == 1:
            give, to_left, to_right = tie((give, to_left, to_right))

    from_left = shift(to_right, "lon", 1)
    from_right = shift(to_left, "lon", -1)
    big, from_left, from_right, center, mixed = tie((big, from_left, from_right, center, mixed))

    sent = jnp.concatenate([big, extra]).astype(bf16)
    for number, mask in enumerate(bits[::-1]):
        got = swap(sent, mask)
        size = got.shape[0] - extra.shape[0]
        extra = extra + got[size:].astype(f32)
        big = sent[:size]
        big = jnp.where(
            has(mask),
            jnp.concatenate([got[:size], big]),
            jnp.concatenate([big, got[:size]]),
        )
        sent = jnp.concatenate([big, extra.astype(bf16)])
    taken = [swap(sent, mask_of(y_bits, code)) for code in (1, 2, 3)]
    half, extra = y_gather(ids, big, extra, taken)
    got = swap(half, core_bit)
    grad_branch, grad_proj, grad_depth, dpooled = last_stage(
        ids, half, got, extra, branch_weight, proj_last, pool_pre, pooled, cell_count
    )
    grad_features = finish(center, from_left, from_right, dpooled)
    return (mixed.reshape(rows, cols, part), grad_features, grad_branch, grad_proj, grad_depth)


def solution(mesh):
    return jax.shard_map(
        per_device,
        mesh=mesh,
        in_specs=(
            P("lat", "lon", "ch"),
            P(None, None, "ch"),
            P(None, "ch", None),
            P(None, "ch", None),
            P("lat", "lon", "ch"),
        ),
        out_specs=(
            P("lat", "lon", "ch"),
            P("lat", "lon", "ch"),
            P(None, "ch", None),
            P(None, "ch", None),
            P(None, None, "ch"),
        ),
        check_vma=False,
    )
```
